32 devices in a mesh: groups: 2 (over y), slab: 4 (over z), sub: 4 (over x, core).
Axes of the slice: x: 2, y: 2, z: 4, core: 2. Of those that a mesh axis runs over, the one named last changes fastest.
Arguments:
- velocity: float32 [3, 64, 128, 512], P(None, ('groups', 'slab'), 'sub'), parts along dimension 1, may hold values from -6 to 6
- template: bfloat16 [64, 128, 512], P(('groups', 'slab'), 'sub'), parts along dimension 0, may hold values from -6 to 6
- moving: bfloat16 [64, 128, 512], P(('groups', 'slab'), 'sub'), parts along dimension 0, may hold values from -6 to 6
- stiffness: float32 [64, 128, 512], P(('groups', 'slab'), 'sub'), parts along dimension 0, may hold values from 0.25 to 4
- fetch_plane: int32 [64, 128, 4], P(('groups', 'slab'), 'sub'), parts along dimension 0, may hold values from 0 to 31, as said below
- tissue: int32 [64, 128, 4], P(('groups', 'slab'), 'sub'), parts along dimension 0, may hold values 0 or 1
Outputs:
- new_velocity: float32 [3, 64, 128, 512], P(None, ('groups', 'slab'), 'sub'), parts along dimension 1
- warped: bfloat16 [64, 128, 512], P(('groups', 'slab'), 'sub'), parts along dimension 0
The draws below stay inside these ranges and needn't reach their ends.
There are 2 independent parts, one for each index of `groups`. The reference program is written for one: setup_inputs(seed, part) draws one part's arguments, and reference() takes and returns one part's arrays. A program takes and returns all parts, laid end to end along the dimension named above; each array names one. Nothing has to cross between parts.
Inputs may be any that keep to these rules, and one draw needn't show every extreme that they name: `fetch_plane`: take the blocks with z in [s*8, (s+1)*8) and y in [q*32, (q+1)*32) for any s and q: at most 512 of them name planes in one range [t*8, (t+1)*8), and in every draw one range t is named by exactly 512 blocks of every such group.
All inputs are finite; a program needn't handle non-finite values. No bound on the sum of `tissue` on one device may be relied on, other than what follows from the above.
Results may differ from the reference program's by a relative error of at most 0.001.
Values may be sent and summed in bfloat16 or wider, within the bound.
No kernel may reach another device: no remote copies, remote signals or barrier semaphores. Data moves between devices by JAX's collectives and lax.ppermute only.
A program may use at most 64 MiB of HBM per device.

```python
import math
import jax
import jax.numpy as jnp

CZ = 8
CY = 32
NX = 512
BLOCK = 128
NBX = 4
NZ = 32
NY = 128


def draw_fetch_plane(key, part):
    key = jax.random.fold_in(key, 7)
    slab_count = NZ // CZ
    sub_count = NY // CY
    devices = slab_count * sub_count
    per_dev = CZ * CY * NBX
    most = 2 * (per_dev // slab_count)
    pool_size = (slab_count - 1) * most
    spare = per_dev - most
    key_hot, key_pool, key_within = jax.random.split(key, 3)
    hottest = jax.random.randint(key_hot, (), 0, slab_count)
    pool = 1 + jnp.arange(pool_size, dtype=jnp.int32) // most

    def one_device(device_key):
        first_key, second_key = jax.random.split(device_key)
        taken = pool[jax.random.permutation(first_key, pool_size)[:spare]]
        offsets = jnp.concatenate([jnp.zeros((most,), jnp.int32), taken])
        return offsets[jax.random.permutation(second_key, per_dev)]
    offsets = jax.vmap(one_device)(jax.random.split(key_pool, devices))
    holder = (hottest + offsets) % slab_count
    within = jax.random.randint(key_within, (devices, per_dev), 0, CZ)
    planes = holder * CZ + within
    layout = planes.reshape(slab_count, sub_count, CZ, CY, NBX)
    return jnp.transpose(layout, (0, 2, 1, 3, 4)).reshape(NZ, NY, NBX).astype(jnp.int32)


def place_ends(drawn, own_key, least, largest):
    spot = [jax.random.randint(jax.random.fold_in(own_key, axis), (), 0, length) for axis, length in enumerate(drawn.shape)]
    main_axis = drawn.shape.index(max(drawn.shape))
    next_to = spot[:main_axis] + [(spot[main_axis] + 1) % drawn.shape[main_axis]] + spot[main_axis + 1:]
    return drawn.at[tuple(spot)].set(least).at[tuple(next_to)].set(largest)


def block_levels(key, shape, shards, low, top_value):
    factor_of, own = 1.0, jax.random.fold_in(key, 6)
    for position, shards_of in shards:
        heights = jnp.exp(jax.random.uniform(jax.random.fold_in(own, position), (shards_of,), jnp.float32, low / len(shards), top_value / len(shards)))
        factor_of = factor_of * jnp.repeat(heights, shape[position] // shards_of).reshape([-1 if axis == position else 1 for axis in range(len(shape))])
    return factor_of


def gaussian(stream_key, dims, width, most, cuts=(), kind=jnp.bfloat16):
    gain = block_levels(stream_key, dims, cuts, -0.22, 0.18) if cuts else 1.0
    entries = jax.random.normal(stream_key, dims, jnp.float32) * width * gain
    return jnp.minimum(jnp.maximum(entries, -most), most).astype(kind)


def setup_inputs(seed: int = 0, part: int = 0) -> dict:
    arg_keys = jax.random.split(jax.random.key(seed), 7)
    part_splits = jax.random.split(jax.random.fold_in(arg_keys[6], part), 7)
    return {
        "velocity": gaussian(part_splits[0], (3, NZ, NY, NX), 1.0, 6.0, ((1, 4), (2, 4)), jnp.float32),
        "template": gaussian(part_splits[1], (NZ, NY, NX), 1.0, 6.0, ((0, 4), (1, 4))),
        "moving": gaussian(part_splits[2], (NZ, NY, NX), 1.0, 6.0, ((0, 4), (1, 4))),
        "stiffness": jnp.clip(jnp.exp(math.log(4.0) - 2.7725887 * jax.random.uniform(part_splits[3], (NZ, NY, NX), jnp.float32) ** block_levels(part_splits[3], (NZ, NY, NX), ((0, 4), (1, 4)), -0.2, 0.2)), 0.25, 4.0),
        "fetch_plane": draw_fetch_plane(jax.random.fold_in(jax.random.fold_in(arg_keys[6], part), 71), part),
        "tissue": place_ends((jax.random.randint(part_splits[5], (NZ, NY, NBX), 0, 5) < 3).astype(jnp.int32), jax.random.fold_in(part_splits[5], 1), 0, 1),
    }


def symbol_sq(length):
    wave_ids = jnp.arange(length, dtype=jnp.int32)
    signed = jnp.where(wave_ids < length // 2, wave_ids, wave_ids - length).astype(jnp.float32)
    wave = (2.0 * jnp.pi / length) * signed
    return wave * wave


def reference(velocity, template, moving, stiffness, fetch_plane, tissue):
    rows_y = jnp.arange(NY, dtype=jnp.int32)[None, :, None]
    cols_x = jnp.arange(NBX, dtype=jnp.int32)[None, None, :]
    lookup = ((fetch_plane * NY + rows_y) * NBX + cols_x).astype(jnp.int32)
    warped = moving.reshape(NZ * NY * NBX, BLOCK)[lookup.reshape(-1)].reshape(NZ, NY, NX)
    image = warped.astype(jnp.float32)
    residual = image - template.astype(jnp.float32)
    tissue_vox = jnp.repeat(tissue.astype(jnp.float32), BLOCK, axis=2)
    weight_field = tissue_vox * stiffness * residual
    grads = [0.5 * (jnp.roll(image, -1, axis_id) - jnp.roll(image, 1, axis_id)) for axis_id in range(3)]
    force = jnp.stack([weight_field * grad for grad in grads])
    factor = 1.0 / (symbol_sq(NZ)[:, None, None] + symbol_sq(NY)[None, :, None] + symbol_sq(NX)[None, None, :] + 1.0 / 256.0)
    spectrum = jnp.fft.fftn(force, axes=(1, 2, 3))
    smoothed = jnp.real(jnp.fft.ifftn(spectrum * factor, axes=(1, 2, 3)))
    new_velocity = 0.5 * (velocity - smoothed)
    return new_velocity, warped
```

```python
import functools

import jax
import jax.numpy as jnp
import numpy as np
from jax import lax
from jax.experimental import pallas as pl
from jax.experimental.pallas import tpu as pltpu
from jax.sharding import PartitionSpec as P

BLOCK = 128


def extended(cells, sides, width):
    for axis, dim in sides:
        count = lax.axis_size(axis)
        head = lax.slice_in_dim(cells, 0, width, axis=dim)
        tail = lax.slice_in_dim(cells, cells.shape[dim] - width, cells.shape[dim], axis=dim)
        cells = jnp.concatenate(
            [
                lax.ppermute(tail, axis, [(i, (i + 1) % count) for i in range(count)]),
                cells,
                lax.ppermute(head, axis, [((i + 1) % count, i) for i in range(count)]),
            ],
            axis=dim,
        )
    return cells


def tables(length):
    wave_ids = jnp.arange(length, dtype=jnp.int32)
    phase = wave_ids[:, None] * wave_ids[None, :] % length
    angle = 2.0 * jnp.pi / length * phase.astype(jnp.float32)
    return (jnp.cos(angle), jnp.sin(angle))


def apply_along(values, matrix, axis_id):
    result = lax.dot_general(
        values,
        matrix,
        (((axis_id,), (0,)), ((), ())),
        precision=lax.Precision.HIGHEST,
        preferred_element_type=jnp.float32,
    )
    return jnp.moveaxis(result, -1, axis_id)


def forward_along(values_pair, axis_id):
    real_part, imag_part = values_pair
    cosine, sine = tables(real_part.shape[axis_id])
    return (
        apply_along(real_part, cosine, axis_id) + apply_along(imag_part, sine, axis_id),
        apply_along(imag_part, cosine, axis_id) - apply_along(real_part, sine, axis_id),
    )


def inverse_along(values_pair, axis_id):
    real_part, imag_part = values_pair
    length = real_part.shape[axis_id]
    cosine, sine = tables(length)
    scale = 1.0 / length
    return (
        (apply_along(real_part, cosine, axis_id) - apply_along(imag_part, sine, axis_id)) * scale,
        (apply_along(imag_part, cosine, axis_id) + apply_along(real_part, sine, axis_id)) * scale,
    )


def symbol_sq(length, first_id, span):
    wave_ids = first_id + jnp.arange(span, dtype=jnp.int32)
    signed = jnp.where(wave_ids < length // 2, wave_ids, wave_ids - length).astype(jnp.float32)
    wave = 2.0 * jnp.pi / length * signed
    return wave * wave


def local_general(velocity, template, moving, stiffness, fetch_plane, tissue):
    planes_dev, rows_dev, x_length = moving.shape
    blocks_x = x_length // BLOCK
    slabs = lax.axis_size("slab")
    subs = lax.axis_size("sub")
    my_slab = lax.axis_index("slab")
    my_sub = lax.axis_index("sub")
    per_dev = planes_dev * rows_dev * blocks_x
    capacity = 2 * per_dev // slabs
    source_plane = fetch_plane.reshape(-1)
    block_ids = jnp.arange(per_dev, dtype=jnp.int32)
    row_of = block_ids // blocks_x % rows_dev
    column_of = block_ids % blocks_x
    moving_rows = moving.reshape(per_dev, BLOCK)
    holder = source_plane // planes_dev
    within = (source_plane % planes_dev * rows_dev + row_of) * blocks_x + column_of
    matches = (holder[:, None] == jnp.arange(slabs, dtype=jnp.int32)[None, :]).astype(jnp.int32)
    earlier = jnp.sum((jnp.cumsum(matches, axis=0) - matches) * matches, axis=1)
    target = holder * capacity + earlier
    wanted = (
        jnp.zeros((slabs * capacity,), jnp.int32).at[target].set(within).reshape(slabs, capacity)
    )
    asked = lax.all_to_all(wanted, "slab", split_axis=0, concat_axis=0, tiled=True)
    fetched = moving_rows[asked.reshape(-1)].reshape(asked.shape + (BLOCK,))
    replies = lax.all_to_all(fetched, "slab", split_axis=0, concat_axis=0, tiled=True)
    warped_rows = replies.reshape(slabs * capacity, BLOCK)[target]
    warped = warped_rows.reshape(planes_dev, rows_dev, x_length)
    padded = extended(warped, (("slab", 0), ("sub", 1)), 1).astype(jnp.float32)
    image = padded[1:-1, 1:-1]
    grad_z = 0.5 * (padded[2:, 1:-1] - padded[:-2, 1:-1])
    grad_y = 0.5 * (padded[1:-1, 2:] - padded[1:-1, :-2])
    grad_x = 0.5 * (jnp.roll(image, -1, 2) - jnp.roll(image, 1, 2))
    residual = image - template.astype(jnp.float32)
    tissue_vox = jnp.repeat(tissue.astype(jnp.float32), BLOCK, axis=2)
    weight_field = tissue_vox * stiffness * residual
    force = jnp.stack([weight_field * grad_z, weight_field * grad_y, weight_field * grad_x])
    cos_x, sin_x = tables(x_length)
    real_part = apply_along(force, cos_x, 3)
    imag_part = -apply_along(force, sin_x, 3)
    moved = (
        lax.all_to_all(real_part, "sub", split_axis=3, concat_axis=2, tiled=True),
        lax.all_to_all(imag_part, "sub", split_axis=3, concat_axis=2, tiled=True),
    )
    moved = forward_along(moved, 2)
    moved = (
        lax.all_to_all(moved[0], "slab", split_axis=2, concat_axis=1, tiled=True),
        lax.all_to_all(moved[1], "slab", split_axis=2, concat_axis=1, tiled=True),
    )
    moved = forward_along(moved, 1)
    total_z = moved[0].shape[1]
    y_span = moved[0].shape[2]
    x_span = moved[0].shape[3]
    factor = 1.0 / (
        symbol_sq(total_z, 0, total_z)[:, None, None]
        + symbol_sq(y_span * slabs, my_slab * y_span, y_span)[None, :, None]
        + symbol_sq(x_span * subs, my_sub * x_span, x_span)[None, None, :]
        + 1.0 / 256.0
    )
    moved = (moved[0] * factor, moved[1] * factor)
    moved = inverse_along(moved, 1)
    moved = (
        lax.all_to_all(moved[0], "slab", split_axis=1, concat_axis=2, tiled=True),
        lax.all_to_all(moved[1], "slab", split_axis=1, concat_axis=2, tiled=True),
    )
    moved = inverse_along(moved, 2)
    real_part, imag_part = (
        lax.all_to_all(moved[0], "sub", split_axis=2, concat_axis=3, tiled=True),
        lax.all_to_all(moved[1], "sub", split_axis=2, concat_axis=3, tiled=True),
    )
    smoothed = (apply_along(real_part, cos_x, 3) - apply_along(imag_part, sin_x, 3)) * (
        1.0 / x_length
    )
    new_velocity = 0.5 * (velocity - smoothed)
    return (new_velocity, warped)


VMEM_BYTES = 50 * 1024 * 1024


def real_basis(length):
    index = np.arange(length)
    half = length // 2
    wave = np.where(index <= half, index, index - half)[:, None]
    angle = 2.0 * np.pi / length * (wave * index[None, :] % length)
    rows = np.where(index[:, None] <= half, np.cos(angle), np.sin(angle)) * np.sqrt(2.0 / length)
    rows[0] /= np.sqrt(2.0)
    rows[half] /= np.sqrt(2.0)
    return rows


def in_two(table):
    high = np.asarray(table, np.float32).astype(jnp.bfloat16)
    low = (np.asarray(table, np.float64) - high.astype(np.float64)).astype(jnp.bfloat16)
    return np.stack([high, low])


def split(values):
    high = values.astype(jnp.bfloat16)
    return high, (values - high.astype(jnp.float32)).astype(jnp.bfloat16)


def times(left, right, dims):
    def one(a, b):
        return lax.dot_general(a, b, (dims, ((), ())), preferred_element_type=jnp.float32)

    return one(left[0], right[0]) + (one(left[0], right[1]) + one(left[1], right[0]))


def wave_sq(index, length):
    wave = jnp.where(index <= length // 2, index, index - length // 2).astype(jnp.float32)
    wave = wave * (2.0 * np.pi / length)
    return wave * wave


def around(value, count):
    return lax.rem(value + 2 * count, count)


def call(kernel, out_shape, arguments, scratch=(), flops=0, nbytes=0):
    smem = pl.BlockSpec(memory_space=pltpu.SMEM)
    vmem = pl.BlockSpec(memory_space=pltpu.VMEM)
    return pl.pallas_call(
        kernel,
        out_shape=out_shape,
        in_specs=[smem] + [vmem] * (len(arguments) - 1),
        out_specs=jax.tree.map(lambda _: vmem, out_shape),
        scratch_shapes=list(scratch),
        compiler_params=pltpu.CompilerParams(vmem_limit_bytes=VMEM_BYTES),
        cost_estimate=pl.CostEstimate(flops=flops, bytes_accessed=nbytes, transcendentals=0),
    )(*arguments)


def send_columns_kernel(slabs, place, moving, fetch, *sends):
    planes, rows, _ = moving.shape
    me = place[0]
    lane = lax.broadcasted_iota(jnp.int32, (rows, BLOCK), 1)
    narrow = lax.broadcasted_iota(jnp.int32, (rows, fetch.shape[2]), 1)
    for step, send in enumerate(sends):
        to = around(me + step, slabs)
        columns = pl.ds(pl.multiple_of(to * BLOCK, BLOCK), BLOCK)
        send[0:planes] = moving[:, :, columns]
        wanted = jnp.zeros((rows, BLOCK), jnp.float32)
        for z in range(planes):
            one = jnp.sum(jnp.where(narrow == to, fetch[z].astype(jnp.float32), 0.0), axis=1, keepdims=True)
            wanted = jnp.where(lane == z, one, wanted)
        send[planes] = wanted.astype(jnp.bfloat16)


def pick_kernel(slabs, place, *refs):
    received, sends, picked = refs[:slabs], refs[slabs:-1], refs[-1]
    planes = received[0].shape[0] - 1
    rows = received[0].shape[1]
    me = place[0]
    total = slabs * planes
    group = 4
    for step in range(slabs):
        first = around(me - step, slabs) * planes
        names = received[step][planes].astype(jnp.float32)
        for start in range(0, planes, group):
            wanted = [
                jnp.broadcast_to(names[:, z : z + 1], (rows, BLOCK)) for z in range(start, start + group)
            ]
            found = [jnp.zeros((rows, BLOCK), jnp.float32) for _ in range(group)]
            for other in range(slabs):
                base = (around(me - other, slabs) * planes).astype(jnp.float32)
                for plane in range(planes):
                    values = received[other][plane].astype(jnp.float32)
                    found = [
                        jnp.where(w == base + float(plane), values, f) for w, f in zip(wanted, found)
                    ]
            for z in range(group):
                picked[first + start + z] = found[z].astype(jnp.bfloat16)
    for step, send in enumerate(sends):
        first = around(me + step, slabs) * planes
        for k in range(planes + 2):
            send[k] = picked[around(first + (k - 1), total)]


def force_kernel(slabs, place, *refs):
    received = refs[:slabs]
    above, below, template, stiffness, tissue, basis, warped, spectra, image, edges = refs[slabs:]
    planes, rows, x_length = template.shape
    me = place[0]
    for step in range(slabs):
        block = pl.ds(pl.multiple_of(around(me - step, slabs) * BLOCK, BLOCK), BLOCK)
        image[:, :, block] = received[step][...].astype(jnp.float32)
        warped[:, :, block] = received[step][1:-1]
        edges[0, :, block] = above[step].astype(jnp.float32)
        edges[1, :, block] = below[step].astype(jnp.float32)
    row = lax.broadcasted_iota(jnp.int32, (rows, x_length), 0)
    forces = [[], [], []]
    for z in range(planes):
        here = image[z + 1]
        marked = tissue[z].astype(jnp.float32)
        marked = jnp.concatenate(
            [jnp.broadcast_to(marked[:, b : b + 1], (rows, BLOCK)) for b in range(x_length // BLOCK)], axis=1
        )
        weight = 0.5 * (marked * stiffness[z] * (here - template[z].astype(jnp.float32)))
        before = jnp.where(row == 0, edges[0, z : z + 1, :], pltpu.roll(here, 1, 0))
        after = jnp.where(row == rows - 1, edges[1, z : z + 1, :], pltpu.roll(here, rows - 1, 0))
        forces[0].append(weight * (image[z + 2] - image[z]))
        forces[1].append(weight * (after - before))
        forces[2].append(weight * (pltpu.roll(here, x_length - 1, 1) - pltpu.roll(here, 1, 1)))
    devices, part = spectra.shape[:2]
    part //= 3
    for a in range(3):
        force = split(jnp.concatenate(forces[a], axis=0))
        spectrum = times((basis[0], basis[1]), force, ((1,), (1,)))
        spectra[:, a * part : (a + 1) * part, :] = spectrum.reshape(devices, part, planes * rows)


def solve_kernel(subs, place, spectra, basis_z, basis_y, out, cells):
    devices, lanes_used, area = spectra.shape
    total_z, total_y, lanes = cells.shape
    slabs = devices // subs
    planes, rows = total_z // slabs, total_y // subs
    pad = jnp.zeros((lanes - lanes_used, area), jnp.float32)
    for d in range(devices):
        block = jnp.concatenate([spectra[d], pad], axis=0).T.reshape(planes, rows, lanes)
        s, q = d // subs, d % subs
        cells[s * planes : (s + 1) * planes, q * rows : (q + 1) * rows, :] = block
    tables_z, tables_y = (basis_z[0], basis_z[1]), (basis_y[0], basis_y[1])
    part = lanes_used // 3
    lane = lax.broadcasted_iota(jnp.int32, (1, lanes), 1)
    x_sq = wave_sq(place[0] * part + lax.rem(lane, part), part * devices)
    y_sq = wave_sq(lax.broadcasted_iota(jnp.int32, (total_y, 1), 0), total_y)
    xy = (x_sq + y_sq) * 256.0 + 1.0
    tile = basis_z.shape[1] // total_z
    for g in range(total_y // tile):
        own = cells[:, g * tile : (g + 1) * tile, :].reshape(total_z * tile, lanes)
        own = times(tables_z, split(own), ((1,), (0,)))
        cells[:, g * tile : (g + 1) * tile, :] = own.reshape(total_z, tile, lanes)
    for z in range(total_z):
        wave = 2.0 * np.pi / total_z * (z if z <= total_z // 2 else z - total_z // 2)
        own = times(tables_y, split(cells[z]), ((1,), (0,)))
        own = own / (xy + 256.0 * wave * wave)
        cells[z] = times(tables_y, split(own), ((0,), (0,)))
    for g in range(total_y // tile):
        own = cells[:, g * tile : (g + 1) * tile, :].reshape(total_z * tile, lanes)
        own = times(tables_z, split(own), ((0,), (0,)))
        cells[:, g * tile : (g + 1) * tile, :] = own.reshape(total_z, tile, lanes)
    for d in range(devices):
        s, q = d // subs, d % subs
        block = cells[s * planes : (s + 1) * planes, q * rows : (q + 1) * rows, :]
        out[d] = block.reshape(area, lanes).T[:lanes_used]


def update_kernel(place, spectra, velocity, basis, out):
    devices, part, area = spectra.shape
    part //= 3
    _, planes, rows, x_length = velocity.shape
    for a in range(3):
        own = spectra[:, a * part : (a + 1) * part, :].reshape(x_length, area).T
        smoothed = times(split(own), (basis[0], basis[1]), ((1,), (0,)))
        out[a] = 0.5 * (velocity[a] - 32.0 * smoothed.reshape(planes, rows, x_length))


def local_blocks(velocity, template, moving, stiffness, fetch_plane, tissue):
    planes, rows, x_length = moving.shape
    slabs, subs = lax.axis_size("slab"), lax.axis_size("sub")
    total_z, total_y = planes * slabs, rows * subs
    devices = slabs * subs
    part = x_length // devices
    area = planes * rows
    my_slab = lax.axis_index("slab")
    my_place = my_slab * subs + lax.axis_index("sub")
    slab_id, place_id = my_slab.reshape(1), my_place.reshape(1)
    bf16, f32 = jnp.bfloat16, jnp.float32

    def shape(dims, kind=f32):
        return jax.ShapeDtypeStruct(dims, kind)

    def scatter(sends):
        return [sends[0]] + [
            lax.ppermute(sends[d], "slab", [(i, (i + d) % slabs) for i in range(slabs)])
            for d in range(1, slabs)
        ]

    sends = call(
        functools.partial(send_columns_kernel, slabs),
        [shape((planes + 1, rows, BLOCK), bf16)] * slabs,
        (slab_id, moving, fetch_plane),
    )
    received = scatter(sends)
    sends = call(
        functools.partial(pick_kernel, slabs),
        [shape((planes + 2, rows, BLOCK), bf16)] * slabs,
        (slab_id, *received),
        [pltpu.VMEM((total_z, rows, BLOCK), bf16)],
    )
    received = scatter(sends)
    last = jnp.stack([r[1:-1, rows - 1] for r in received])
    first = jnp.stack([r[1:-1, 0] for r in received])
    above = lax.ppermute(last, "sub", [(i, (i + 1) % subs) for i in range(subs)])
    below = lax.ppermute(first, "sub", [((i + 1) % subs, i) for i in range(subs)])
    basis_x = in_two(real_basis(x_length))
    tile = 8
    basis_z = in_two(np.kron(real_basis(total_z), np.eye(tile)))
    basis_y = in_two(real_basis(total_y))
    warped, spectra = call(
        functools.partial(force_kernel, slabs),
        [shape((planes, rows, x_length), bf16), shape((devices, 3 * part, area))],
        (slab_id, *received, above, below, template, stiffness, tissue, in_two(8.0 * real_basis(x_length))),
        [pltpu.VMEM((planes + 2, rows, x_length), f32), pltpu.VMEM((2, planes, x_length), f32)],
    )
    spectra = spectra.astype(jnp.float16)
    spectra = lax.all_to_all(spectra, ("slab", "sub"), split_axis=0, concat_axis=0, tiled=True)
    spectra = call(
        functools.partial(solve_kernel, subs),
        shape((devices, 3 * part, area)),
        (place_id, spectra.astype(f32), basis_z, basis_y),
        [pltpu.VMEM((total_z, total_y, 128), f32)],
    )
    spectra = spectra.astype(jnp.float16)
    spectra = lax.all_to_all(spectra, ("slab", "sub"), split_axis=0, concat_axis=0, tiled=True)
    new_velocity = call(
        update_kernel,
        shape(velocity.shape),
        (place_id, spectra.astype(f32), velocity, basis_x),
    )
    return (new_velocity, warped)


def local(velocity, template, moving, stiffness, fetch_plane, tissue):
    planes, rows, x_length = moving.shape
    slabs, subs = lax.axis_size("slab"), lax.axis_size("sub")
    part = x_length // (slabs * subs)
    fits = (
        x_length == slabs * BLOCK
        and planes == 8
        and rows % 16 == 0
        and part % 16 == 0
        and 3 * part <= 128
        and planes * slabs * 8 == 256
        and rows * subs == 128
    )
    run = local_blocks if fits else local_general
    return run(velocity, template, moving, stiffness, fetch_plane, tissue)


def solution(mesh):
    placed = (
        P(None, ("groups", "slab"), "sub", None),
        P(("groups", "slab"), "sub", None),
        P(("groups", "slab"), "sub", None),
        P(("groups", "slab"), "sub", None),
        P(("groups", "slab"), "sub", None),
        P(("groups", "slab"), "sub", None),
    )
    return jax.shard_map(
        local,
        mesh=mesh,
        in_specs=placed,
        out_specs=(P(None, ("groups", "slab"), "sub", None), P(("groups", "slab"), "sub", None)),
        check_vma=False,
    )
```

```python
import functools

import jax
import jax.numpy as jnp
import numpy as np
from jax import lax
from jax.experimental import pallas as pl
from jax.experimental.pallas import tpu as pltpu
from jax.sharding import PartitionSpec as P

BLOCK = 128


def extended(cells, sides, width):
    for axis, dim in sides:
        count = lax.axis_size(axis)
        head = lax.slice_in_dim(cells, 0, width, axis=dim)
        tail = lax.slice_in_dim(cells, cells.shape[dim] - width, cells.shape[dim], axis=dim)
        cells = jnp.concatenate(
            [
                lax.ppermute(tail, axis, [(i, (i + 1) % count) for i in range(count)]),
                cells,
                lax.ppermute(head, axis, [((i + 1) % count, i) for i in range(count)]),
            ],
            axis=dim,
        )
    return cells


def tables(length):
    wave_ids = jnp.arange(length, dtype=jnp.int32)
    phase = wave_ids[:, None] * wave_ids[None, :] % length
    angle = 2.0 * jnp.pi / length * phase.astype(jnp.float32)
    return (jnp.cos(angle), jnp.sin(angle))


def apply_along(values, matrix, axis_id):
    result = lax.dot_general(
        values,
        matrix,
        (((axis_id,), (0,)), ((), ())),
        precision=lax.Precision.HIGHEST,
        preferred_element_type=jnp.float32,
    )
    return jnp.moveaxis(result, -1, axis_id)


def forward_along(values_pair, axis_id):
    real_part, imag_part = values_pair
    cosine, sine = tables(real_part.shape[axis_id])
    return (
        apply_along(real_part, cosine, axis_id) + apply_along(imag_part, sine, axis_id),
        apply_along(imag_part, cosine, axis_id) - apply_along(real_part, sine, axis_id),
    )


def inverse_along(values_pair, axis_id):
    real_part, imag_part = values_pair
    length = real_part.shape[axis_id]
    cosine, sine = tables(length)
    scale = 1.0 / length
    return (
        (apply_along(real_part, cosine, axis_id) - apply_along(imag_part, sine, axis_id)) * scale,
        (apply_along(imag_part, cosine, axis_id) + apply_along(real_part, sine, axis_id)) * scale,
    )


def symbol_sq(length, first_id, span):
    wave_ids = first_id + jnp.arange(span, dtype=jnp.int32)
    signed = jnp.where(wave_ids < length // 2, wave_ids, wave_ids - length).astype(jnp.float32)
    wave = 2.0 * jnp.pi / length * signed
    return wave * wave


def local_general(velocity, template, moving, stiffness, fetch_plane, tissue):
    planes_dev, rows_dev, x_length = moving.shape
    blocks_x = x_length // BLOCK
    slabs = lax.axis_size("slab")
    subs = lax.axis_size("sub")
    my_slab = lax.axis_index("slab")
    my_sub = lax.axis_index("sub")
    per_dev = planes_dev * rows_dev * blocks_x
    capacity = 2 * per_dev // slabs
    source_plane = fetch_plane.reshape(-1)
    block_ids = jnp.arange(per_dev, dtype=jnp.int32)
    row_of = block_ids // blocks_x % rows_dev
    column_of = block_ids % blocks_x
    moving_rows = moving.reshape(per_dev, BLOCK)
    holder = source_plane // planes_dev
    within = (source_plane % planes_dev * rows_dev + row_of) * blocks_x + column_of
    matches = (holder[:, None] == jnp.arange(slabs, dtype=jnp.int32)[None, :]).astype(jnp.int32)
    earlier = jnp.sum((jnp.cumsum(matches, axis=0) - matches) * matches, axis=1)
    target = holder * capacity + earlier
    wanted = (
        jnp.zeros((slabs * capacity,), jnp.int32).at[target].set(within).reshape(slabs, capacity)
    )
    asked = lax.all_to_all(wanted, "slab", split_axis=0, concat_axis=0, tiled=True)
    fetched = moving_rows[asked.reshape(-1)].reshape(asked.shape + (BLOCK,))
    replies = lax.all_to_all(fetched, "slab", split_axis=0, concat_axis=0, tiled=True)
    warped_rows = replies.reshape(slabs * capacity, BLOCK)[target]
    warped = warped_rows.reshape(planes_dev, rows_dev, x_length)
    padded = extended(warped, (("slab", 0), ("sub", 1)), 1).astype(jnp.float32)
    image = padded[1:-1, 1:-1]
    grad_z = 0.5 * (padded[2:, 1:-1] - padded[:-2, 1:-1])
    grad_y = 0.5 * (padded[1:-1, 2:] - padded[1:-1, :-2])
    grad_x = 0.5 * (jnp.roll(image, -1, 2) - jnp.roll(image, 1, 2))
    residual = image - template.astype(jnp.float32)
    tissue_vox = jnp.repeat(tissue.astype(jnp.float32), BLOCK, axis=2)
    weight_field = tissue_vox * stiffness * residual
    force = jnp.stack([weight_field * grad_z, weight_field * grad_y, weight_field * grad_x])
    cos_x, sin_x = tables(x_length)
    real_part = apply_along(force, cos_x, 3)
    imag_part = -apply_along(force, sin_x, 3)
    moved = (
        lax.all_to_all(real_part, "sub", split_axis=3, concat_axis=2, tiled=True),
        lax.all_to_all(imag_part, "sub", split_axis=3, concat_axis=2, tiled=True),
    )
    moved = forward_along(moved, 2)
    moved = (
        lax.all_to_all(moved[0], "slab", split_axis=2, concat_axis=1, tiled=True),
        lax.all_to_all(moved[1], "slab", split_axis=2, concat_axis=1, tiled=True),
    )
    moved = forward_along(moved, 1)
    total_z = moved[0].shape[1]
    y_span = moved[0].shape[2]
    x_span = moved[0].shape[3]
    factor = 1.0 / (
        symbol_sq(total_z, 0, total_z)[:, None, None]
        + symbol_sq(y_span * slabs, my_slab * y_span, y_span)[None, :, None]
        + symbol_sq(x_span * subs, my_sub * x_span, x_span)[None, None, :]
        + 1.0 / 256.0
    )
    moved = (moved[0] * factor, moved[1] * factor)
    moved = inverse_along(moved, 1)
    moved = (
        lax.all_to_all(moved[0], "slab", split_axis=1, concat_axis=2, tiled=True),
        lax.all_to_all(moved[1], "slab", split_axis=1, concat_axis=2, tiled=True),
    )
    moved = inverse_along(moved, 2)
    real_part, imag_part = (
        lax.all_to_all(moved[0], "sub", split_axis=2, concat_axis=3, tiled=True),
        lax.all_to_all(moved[1], "sub", split_axis=2, concat_axis=3, tiled=True),
    )
    smoothed = (apply_along(real_part, cos_x, 3) - apply_along(imag_part, sin_x, 3)) * (
        1.0 / x_length
    )
    new_velocity = 0.5 * (velocity - smoothed)
    return (new_velocity, warped)


VMEM_BYTES = 50 * 1024 * 1024
COEFFICIENT_UNIT = 8191.0


def real_basis(length):
    index = np.arange(length)
    half = length // 2
    wave = np.where(index <= half, index, index - half)[:, None]
    angle = 2.0 * np.pi / length * (wave * index[None, :] % length)
    rows = np.where(index[:, None] <= half, np.cos(angle), np.sin(angle)) * np.sqrt(2.0 / length)
    rows[0] /= np.sqrt(2.0)
    rows[half] /= np.sqrt(2.0)
    return rows


def in_two(table):
    high = np.asarray(table, np.float32).astype(jnp.bfloat16)
    low = (np.asarray(table, np.float64) - high.astype(np.float64)).astype(jnp.bfloat16)
    return np.stack([high, low])


def split(values):
    high = values.astype(jnp.bfloat16)
    return high, (values - high.astype(jnp.float32)).astype(jnp.bfloat16)


def times(left, right, dims):
    def one(a, b):
        return lax.dot_general(a, b, (dims, ((), ())), preferred_element_type=jnp.float32)

    return one(left[0], right[0]) + (one(left[0], right[1]) + one(left[1], right[0]))


def wave_sq(index, length):
    wave = jnp.where(index <= length // 2, index, index - length // 2).astype(jnp.float32)
    wave = wave * (2.0 * np.pi / length)
    return wave * wave


def around(value, count):
    return lax.rem(value + 2 * count, count)


def call(kernel, out_shape, arguments, scratch=(), flops=0, nbytes=0):
    smem = pl.BlockSpec(memory_space=pltpu.SMEM)
    vmem = pl.BlockSpec(memory_space=pltpu.VMEM)
    return pl.pallas_call(
        kernel,
        out_shape=out_shape,
        in_specs=[smem] + [vmem] * (len(arguments) - 1),
        out_specs=jax.tree.map(lambda _: vmem, out_shape),
        scratch_shapes=list(scratch),
        compiler_params=pltpu.CompilerParams(vmem_limit_bytes=VMEM_BYTES),
        cost_estimate=pl.CostEstimate(flops=flops, bytes_accessed=nbytes, transcendentals=0),
    )(*arguments)


def send_rows_kernel(slabs, place, moving, template, stiffness, fetch, tissue, *refs):
    images, weights, wide = refs[:slabs], refs[slabs:-1], refs[-1]
    planes, rows, x_length = moving.shape
    share = rows // slabs
    blocks = x_length // BLOCK
    me = place[0]

    def by_row(ref):
        cells = jnp.concatenate([ref[z].astype(jnp.float32) for z in range(planes)], axis=0)
        cells = jnp.concatenate([cells, jnp.zeros((cells.shape[0], BLOCK - rows), jnp.float32)], axis=1)
        cells = jnp.concatenate([cells, jnp.zeros((BLOCK - cells.shape[0], BLOCK), jnp.float32)], axis=0)
        return cells.T[:rows]

    names, marks = by_row(fetch), by_row(tissue)
    wide[3 * planes, :, 0:BLOCK] = names
    for z in range(planes):
        wide[z] = moving[z].astype(jnp.float32)
        wide[planes + z] = template[z].astype(jnp.float32)
        marked = jnp.concatenate(
            [
                jnp.broadcast_to(marks[:, z * blocks + b : z * blocks + b + 1], (rows, BLOCK))
                for b in range(blocks)
            ],
            axis=1,
        )
        wide[2 * planes + z] = marked * stiffness[z] * COEFFICIENT_UNIT + 0.5
    for step in range(slabs):
        part = pl.ds(pl.multiple_of(around(me + step, slabs) * share, share), share)
        for z in range(0, 2 * planes, 2):
            both = jnp.concatenate([wide[z, part, :], wide[z + 1, part, :]], axis=0)
            images[step][z * share : (z + 2) * share] = both.astype(jnp.bfloat16)
        asked = jnp.concatenate([wide[3 * planes, part, 0:BLOCK]] * blocks, axis=1)
        images[step][2 * planes * share : (2 * planes + 1) * share] = asked.astype(jnp.bfloat16)
        for z in range(0, planes, 2):
            both = jnp.concatenate([wide[2 * planes + z, part, :], wide[2 * planes + z + 1, part, :]], axis=0)
            weights[step][z * share : (z + 2) * share] = both.astype(jnp.int32).astype(jnp.int16)


def pick_kernel(slabs, planes, place, *refs):
    received, sends = refs[:slabs], refs[slabs : 2 * slabs]
    image, residual, first, last, edges = refs[2 * slabs :]
    total, share, x_length = image.shape
    blocks = x_length // BLOCK
    me = place[0]
    group = 2
    for step in range(slabs):
        base = around(me - step, slabs) * planes
        names = received[step][2 * planes * share : (2 * planes + 1) * share, 0:BLOCK].astype(jnp.float32)
        for start in range(0, planes, group):
            wanted = [
                jnp.concatenate(
                    [
                        jnp.broadcast_to(names[:, z * blocks + b : z * blocks + b + 1], (share, BLOCK))
                        for b in range(blocks)
                    ],
                    axis=1,
                )
                for z in range(start, start + group)
            ]
            found = [jnp.zeros((share, x_length), jnp.float32) for _ in range(group)]
            for other in range(slabs):
                name = (around(me - other, slabs) * planes).astype(jnp.float32)
                for plane in range(0, planes, 2):
                    both = received[other][plane * share : (plane + 2) * share].astype(jnp.float32)
                    for k in range(2):
                        values = both[k * share : (k + 1) * share]
                        found = [
                            jnp.where(w == name + float(plane + k), values, f) for w, f in zip(wanted, found)
                        ]
            both = received[step][(planes + start) * share : (planes + start + 2) * share].astype(jnp.float32)
            for k in range(group):
                z = base + (start + k)
                image[z] = found[k]
                residual[z] = found[k] - both[k * share : (k + 1) * share]
                edges[0, pl.ds(z, 1), :] = found[k][0:1]
                edges[1, pl.ds(z, 1), :] = found[k][share - 1 : share]
    first[...] = edges[0].astype(jnp.bfloat16)
    last[...] = edges[1].astype(jnp.bfloat16)
    for step, send in enumerate(sends):
        base = around(me + step, slabs) * planes
        for z in range(0, planes, 2):
            both = jnp.concatenate([image[base + z], image[base + (z + 1)]], axis=0)
            send[z * share : (z + 2) * share] = both.astype(jnp.bfloat16)


def force_kernel(slabs, place, *refs):
    weights = refs[:slabs]
    above, below, image, residual, basis_x, basis_z, spectra, edges, force = refs[slabs:]
    total, share, x_length = image.shape
    planes = total // slabs
    me = place[0]
    edges[0] = above[...].astype(jnp.float32)
    edges[1] = below[...].astype(jnp.float32)
    row = lax.broadcasted_iota(jnp.int32, (share, x_length), 0)
    for step in range(slabs):
        base = around(me - step, slabs) * planes
        for start in range(0, planes, 2):
            both = weights[step][start * share : (start + 2) * share].astype(jnp.int32).astype(jnp.float32)
            for k in range(2):
                z = base + (start + k)
                here = image[z]
                weight = both[k * share : (k + 1) * share] * (residual[z] * (0.5 / COEFFICIENT_UNIT))
                before = jnp.where(row == 0, edges[0, pl.ds(z, 1), :], pltpu.roll(here, 1, 0))
                after = jnp.where(row == share - 1, edges[1, pl.ds(z, 1), :], pltpu.roll(here, share - 1, 0))
                force[0, z] = weight * (image[around(z + 1, total)] - image[around(z - 1, total)])
                force[1, z] = weight * (after - before)
                force[2, z] = weight * (pltpu.roll(here, x_length - 1, 1) - pltpu.roll(here, 1, 1))
    devices, part = spectra.shape[:2]
    part //= 3
    for a in range(3):
        own = split(force[a].reshape(total * share, x_length))
        own = split(times((basis_z[0], basis_z[1]), own, ((1,), (0,))))
        own = times((basis_x[0], basis_x[1]), own, ((1,), (1,)))
        spectra[:, a * part : (a + 1) * part, :] = own.reshape(devices, part, total * share)


def solve_kernel(subs, place, spectra, basis_z, basis_y, out, cells):
    devices, lanes_used, area = spectra.shape
    total_z, total_y, lanes = cells.shape
    slabs = devices // subs
    planes, rows = total_z // slabs, total_y // subs
    share = rows // slabs
    pad = jnp.zeros((lanes - lanes_used, area), jnp.float32)
    for d in range(devices):
        s, q = d // subs, d % subs
        block = jnp.concatenate([spectra[d], pad], axis=0).T.reshape(total_z, share, lanes)
        cells[:, q * rows + s * share : q * rows + (s + 1) * share, :] = block
    tables_z, tables_y = (basis_z[0], basis_z[1]), (basis_y[0], basis_y[1])
    part = lanes_used // 3
    lane = lax.broadcasted_iota(jnp.int32, (1, lanes), 1)
    x_sq = wave_sq(place[0] * part + lax.rem(lane, part), part * devices)
    y_sq = wave_sq(lax.broadcasted_iota(jnp.int32, (total_y, 1), 0), total_y)
    xy = (x_sq + y_sq) * 256.0 + 1.0
    for z in range(0, total_z, 2):
        own = jnp.concatenate([cells[z], cells[z + 1]], axis=1)
        own = times(tables_y, split(own), ((1,), (0,)))
        scale = []
        for k in range(2):
            wave = 2.0 * np.pi / total_z * (z + k if z + k <= total_z // 2 else z + k - total_z // 2)
            scale.append(xy + 256.0 * wave * wave)
        own = own / jnp.concatenate(scale, axis=1)
        own = times(tables_y, split(own), ((0,), (0,)))
        cells[z] = own[:, :lanes]
        cells[z + 1] = own[:, lanes:]
    for g in range(0, total_y, 2 * share):
        own = jnp.concatenate(
            [cells[:, y : y + share, :].reshape(area, lanes) for y in (g, g + share)], axis=1
        )
        own = times(tables_z, split(own), ((0,), (0,)))
        cells[:, g : g + share, :] = own[:, :lanes].reshape(total_z, share, lanes)
        cells[:, g + share : g + 2 * share, :] = own[:, lanes:].reshape(total_z, share, lanes)
    for d in range(devices):
        s, q = d // subs, d % subs
        block = cells[s * planes : (s + 1) * planes, q * rows : (q + 1) * rows, :]
        out[d] = block.reshape(area, lanes).T[:lanes_used]


def update_kernel(slabs, place, spectra, velocity, basis, *refs):
    received, (out, warped, wide) = refs[:slabs], refs[slabs:]
    devices, part, area = spectra.shape
    part //= 3
    _, planes, rows, x_length = velocity.shape
    share = rows // slabs
    for step in range(slabs):
        place_of = pl.ds(pl.multiple_of(around(place[0] - step, slabs) * share, share), share)
        for z in range(0, planes, 2):
            both = received[step][z * share : (z + 2) * share].astype(jnp.float32)
            wide[z, place_of, :] = both[:share]
            wide[z + 1, place_of, :] = both[share:]
    warped[...] = wide[...].astype(jnp.bfloat16)
    for a in range(3):
        own = spectra[:, a * part : (a + 1) * part, :].reshape(x_length, area).T
        smoothed = times(split(own), (basis[0], basis[1]), ((1,), (0,)))
        out[a] = 0.5 * (velocity[a] - 32.0 * smoothed.reshape(planes, rows, x_length))


def local_rows(velocity, template, moving, stiffness, fetch_plane, tissue):
    planes, rows, x_length = moving.shape
    slabs, subs = lax.axis_size("slab"), lax.axis_size("sub")
    total_z, total_y = planes * slabs, rows * subs
    devices = slabs * subs
    part = x_length // devices
    area = planes * rows
    share = rows // slabs
    both_axes = ("slab", "sub")
    my_slab = lax.axis_index("slab")
    my_place = my_slab * subs + lax.axis_index("sub")
    slab_id, place_id = my_slab.reshape(1), my_place.reshape(1)
    bf16, f32 = jnp.bfloat16, jnp.float32

    def shape(dims, kind=f32):
        return jax.ShapeDtypeStruct(dims, kind)

    def scatter(sends):
        return [sends[0]] + [
            lax.ppermute(sends[d], "slab", [(i, (i + d) % slabs) for i in range(slabs)])
            for d in range(1, slabs)
        ]

    def exchange(values):
        values = values.astype(jnp.float16)
        return lax.all_to_all(values, both_axes, split_axis=0, concat_axis=0, tiled=True)

    images = shape(((2 * planes + 1) * share, x_length), bf16)
    weights = shape((planes * share, x_length), jnp.int16)
    sends = call(
        functools.partial(send_rows_kernel, slabs),
        [images] * slabs + [weights] * slabs,
        (slab_id, moving, template, stiffness, fetch_plane.swapaxes(1, 2), tissue.swapaxes(1, 2)),
        [pltpu.VMEM((3 * planes + 1, rows, x_length), f32)],
    )
    images, weights = scatter(sends[:slabs]), scatter(sends[slabs:])
    *sends, image, residual, first, last = call(
        functools.partial(pick_kernel, slabs, planes),
        [shape((planes * share, x_length), bf16)] * slabs
        + [shape((total_z, share, x_length))] * 2
        + [shape((total_z, x_length), bf16)] * 2,
        (slab_id, *images),
        [pltpu.VMEM((2, total_z, x_length), f32)],
    )
    ring = [s * subs + q for q in range(subs) for s in range(slabs)]
    onward = [(ring[i], ring[(i + 1) % devices]) for i in range(devices)]
    above = lax.ppermute(last, both_axes, onward)
    below = lax.ppermute(first, both_axes, [(b, a) for a, b in onward])
    basis_z = in_two(np.kron(real_basis(total_z), np.eye(share)))
    spectra = call(
        functools.partial(force_kernel, slabs),
        shape((devices, 3 * part, area)),
        (slab_id, *weights, above, below, image, residual, in_two(8.0 * real_basis(x_length)), basis_z),
        [pltpu.VMEM((2, total_z, x_length), f32), pltpu.VMEM((3, total_z, share, x_length), f32)],
    )
    spectra = exchange(spectra)
    spectra, sends = lax.optimization_barrier((spectra, sends))
    warped = scatter(sends)
    spectra = call(
        functools.partial(solve_kernel, subs),
        shape((devices, 3 * part, area)),
        (place_id, spectra.astype(f32), basis_z, in_two(real_basis(total_y))),
        [pltpu.VMEM((total_z, total_y, 128), f32)],
    )
    spectra = exchange(spectra)
    return tuple(
        call(
            functools.partial(update_kernel, slabs),
            [shape(velocity.shape), shape(moving.shape, bf16)],
            (slab_id, spectra.astype(f32), velocity, in_two(real_basis(x_length)), *warped),
            [pltpu.VMEM((planes, rows, x_length), f32)],
        )
    )


def local(velocity, template, moving, stiffness, fetch_plane, tissue):
    planes, rows, x_length = moving.shape
    slabs, subs = lax.axis_size("slab"), lax.axis_size("sub")
    part = x_length // (slabs * subs)
    fits = (
        planes == 8
        and rows == 8 * slabs
        and part % 8 == 0
        and 3 * part <= BLOCK
        and planes * slabs * 8 == 256
        and rows * subs == BLOCK
        and planes * (x_length // BLOCK) <= BLOCK
    )
    run = local_rows if fits else local_general
    return run(velocity, template, moving, stiffness, fetch_plane, tissue)


def solution(mesh):
    placed = (
        P(None, ("groups", "slab"), "sub", None),
        P(("groups", "slab"), "sub", None),
        P(("groups", "slab"), "sub", None),
        P(("groups", "slab"), "sub", None),
        P(("groups", "slab"), "sub", None),
        P(("groups", "slab"), "sub", None),
    )
    return jax.shard_map(
        local,
        mesh=mesh,
        in_specs=placed,
        out_specs=(P(None, ("groups", "slab"), "sub", None), P(("groups", "slab"), "sub", None)),
        check_vma=False,
    )
```

```python
import functools

import jax
import jax.numpy as jnp
import numpy as np
from jax import lax
from jax.experimental import pallas as pl
from jax.experimental.pallas import tpu as pltpu
from jax.sharding import PartitionSpec as P

BLOCK = 128


def extended(cells, sides, width):
    for axis, dim in sides:
        count = lax.axis_size(axis)
        head = lax.slice_in_dim(cells, 0, width, axis=dim)
        tail = lax.slice_in_dim(cells, cells.shape[dim] - width, cells.shape[dim], axis=dim)
        cells = jnp.concatenate(
            [
                lax.ppermute(tail, axis, [(i, (i + 1) % count) for i in range(count)]),
                cells,
                lax.ppermute(head, axis, [((i + 1) % count, i) for i in range(count)]),
            ],
            axis=dim,
        )
    return cells


def tables(length):
    wave_ids = jnp.arange(length, dtype=jnp.int32)
    phase = wave_ids[:, None] * wave_ids[None, :] % length
    angle = 2.0 * jnp.pi / length * phase.astype(jnp.float32)
    return (jnp.cos(angle), jnp.sin(angle))


def apply_along(values, matrix, axis_id):
    result = lax.dot_general(
        values,
        matrix,
        (((axis_id,), (0,)), ((), ())),
        precision=lax.Precision.HIGHEST,
        preferred_element_type=jnp.float32,
    )
    return jnp.moveaxis(result, -1, axis_id)


def forward_along(values_pair, axis_id):
    real_part, imag_part = values_pair
    cosine, sine = tables(real_part.shape[axis_id])
    return (
        apply_along(real_part, cosine, axis_id) + apply_along(imag_part, sine, axis_id),
        apply_along(imag_part, cosine, axis_id) - apply_along(real_part, sine, axis_id),
    )


def inverse_along(values_pair, axis_id):
    real_part, imag_part = values_pair
    length = real_part.shape[axis_id]
    cosine, sine = tables(length)
    scale = 1.0 / length
    return (
        (apply_along(real_part, cosine, axis_id) - apply_along(imag_part, sine, axis_id)) * scale,
        (apply_along(imag_part, cosine, axis_id) + apply_along(real_part, sine, axis_id)) * scale,
    )


def symbol_sq(length, first_id, span):
    wave_ids = first_id + jnp.arange(span, dtype=jnp.int32)
    signed = jnp.where(wave_ids < length // 2, wave_ids, wave_ids - length).astype(jnp.float32)
    wave = 2.0 * jnp.pi / length * signed
    return wave * wave


def local_general(velocity, template, moving, stiffness, fetch_plane, tissue):
    planes_dev, rows_dev, x_length = moving.shape
    blocks_x = x_length // BLOCK
    slabs = lax.axis_size("slab")
    subs = lax.axis_size("sub")
    my_slab = lax.axis_index("slab")
    my_sub = lax.axis_index("sub")
    per_dev = planes_dev * rows_dev * blocks_x
    capacity = 2 * per_dev // slabs
    source_plane = fetch_plane.reshape(-1)
    block_ids = jnp.arange(per_dev, dtype=jnp.int32)
    row_of = block_ids // blocks_x % rows_dev
    column_of = block_ids % blocks_x
    moving_rows = moving.reshape(per_dev, BLOCK)
    holder = source_plane // planes_dev
    within = (source_plane % planes_dev * rows_dev + row_of) * blocks_x + column_of
    matches = (holder[:, None] == jnp.arange(slabs, dtype=jnp.int32)[None, :]).astype(jnp.int32)
    earlier = jnp.sum((jnp.cumsum(matches, axis=0) - matches) * matches, axis=1)
    target = holder * capacity + earlier
    wanted = (
        jnp.zeros((slabs * capacity,), jnp.int32).at[target].set(within).reshape(slabs, capacity)
    )
    asked = lax.all_to_all(wanted, "slab", split_axis=0, concat_axis=0, tiled=True)
    fetched = moving_rows[asked.reshape(-1)].reshape(asked.shape + (BLOCK,))
    replies = lax.all_to_all(fetched, "slab", split_axis=0, concat_axis=0, tiled=True)
    warped_rows = replies.reshape(slabs * capacity, BLOCK)[target]
    warped = warped_rows.reshape(planes_dev, rows_dev, x_length)
    padded = extended(warped, (("slab", 0), ("sub", 1)), 1).astype(jnp.float32)
    image = padded[1:-1, 1:-1]
    grad_z = 0.5 * (padded[2:, 1:-1] - padded[:-2, 1:-1])
    grad_y = 0.5 * (padded[1:-1, 2:] - padded[1:-1, :-2])
    grad_x = 0.5 * (jnp.roll(image, -1, 2) - jnp.roll(image, 1, 2))
    residual = image - template.astype(jnp.float32)
    tissue_vox = jnp.repeat(tissue.astype(jnp.float32), BLOCK, axis=2)
    weight_field = tissue_vox * stiffness * residual
    force = jnp.stack([weight_field * grad_z, weight_field * grad_y, weight_field * grad_x])
    cos_x, sin_x = tables(x_length)
    real_part = apply_along(force, cos_x, 3)
    imag_part = -apply_along(force, sin_x, 3)
    moved = (
        lax.all_to_all(real_part, "sub", split_axis=3, concat_axis=2, tiled=True),
        lax.all_to_all(imag_part, "sub", split_axis=3, concat_axis=2, tiled=True),
    )
    moved = forward_along(moved, 2)
    moved = (
        lax.all_to_all(moved[0], "slab", split_axis=2, concat_axis=1, tiled=True),
        lax.all_to_all(moved[1], "slab", split_axis=2, concat_axis=1, tiled=True),
    )
    moved = forward_along(moved, 1)
    total_z = moved[0].shape[1]
    y_span = moved[0].shape[2]
    x_span = moved[0].shape[3]
    factor = 1.0 / (
        symbol_sq(total_z, 0, total_z)[:, None, None]
        + symbol_sq(y_span * slabs, my_slab * y_span, y_span)[None, :, None]
        + symbol_sq(x_span * subs, my_sub * x_span, x_span)[None, None, :]
        + 1.0 / 256.0
    )
    moved = (moved[0] * factor, moved[1] * factor)
    moved = inverse_along(moved, 1)
    moved = (
        lax.all_to_all(moved[0], "slab", split_axis=1, concat_axis=2, tiled=True),
        lax.all_to_all(moved[1], "slab", split_axis=1, concat_axis=2, tiled=True),
    )
    moved = inverse_along(moved, 2)
    real_part, imag_part = (
        lax.all_to_all(moved[0], "sub", split_axis=2, concat_axis=3, tiled=True),
        lax.all_to_all(moved[1], "sub", split_axis=2, concat_axis=3, tiled=True),
    )
    smoothed = (apply_along(real_part, cos_x, 3) - apply_along(imag_part, sin_x, 3)) * (
        1.0 / x_length
    )
    new_velocity = 0.5 * (velocity - smoothed)
    return (new_velocity, warped)


VMEM_BYTES = 24 * 1024 * 1024
COEFFICIENT_UNIT = 8191.0


def real_basis(length):
    index = np.arange(length)
    half = length // 2
    wave = np.where(index <= half, index, index - half)[:, None]
    angle = 2.0 * np.pi / length * (wave * index[None, :] % length)
    rows = np.where(index[:, None] <= half, np.cos(angle), np.sin(angle)) * np.sqrt(2.0 / length)
    rows[0] /= np.sqrt(2.0)
    rows[half] /= np.sqrt(2.0)
    return rows


def in_two(table):
    high = np.asarray(table, np.float32).astype(jnp.bfloat16)
    low = (np.asarray(table, np.float64) - high.astype(np.float64)).astype(jnp.bfloat16)
    return np.stack([high, low])


def split(values):
    high = values.astype(jnp.bfloat16)
    return high, (values - high.astype(jnp.float32)).astype(jnp.bfloat16)


def times(left, right, dims):
    def one(a, b):
        return lax.dot_general(a, b, (dims, ((), ())), preferred_element_type=jnp.float32)

    return one(left[0], right[0]) + (one(left[0], right[1]) + one(left[1], right[0]))


def wave_sq(index, length):
    wave = jnp.where(index <= length // 2, index, index - length // 2).astype(jnp.float32)
    wave = wave * (2.0 * np.pi / length)
    return wave * wave


def around(value, count):
    return lax.rem(value + 2 * count, count)


def call(kernel, out_shape, *arguments, scratch=(), flops=0):
    places = [
        pl.BlockSpec(memory_space=pl.ANY if isinstance(a, tuple) else pltpu.SMEM if a.ndim == 1 else pltpu.VMEM)
        for a in arguments
    ]
    arguments = [a[0] if isinstance(a, tuple) else a for a in arguments]
    vmem = pl.BlockSpec(memory_space=pltpu.VMEM)
    nbytes = sum(a.size * a.dtype.itemsize for a in arguments + jax.tree.leaves(out_shape))
    return pl.pallas_call(
        kernel,
        out_shape=out_shape,
        in_specs=places,
        out_specs=jax.tree.map(lambda _: vmem, out_shape),
        scratch_shapes=list(scratch),
        compiler_params=pltpu.CompilerParams(vmem_limit_bytes=VMEM_BYTES),
        cost_estimate=pl.CostEstimate(flops=flops, bytes_accessed=nbytes, transcendentals=0),
    )(*arguments)


def fetch_all(pairs, done):
    copies = [pltpu.make_async_copy(src, dst, done.at[k]) for k, (src, dst) in enumerate(pairs)]
    for copy in copies:
        copy.start()
    for copy in copies:
        copy.wait()


def by_row(ref, rows):
    cells = jnp.concatenate([ref[z].astype(jnp.float32) for z in range(ref.shape[0])], axis=0)
    cells = jnp.concatenate([cells, jnp.zeros((cells.shape[0], BLOCK - rows), jnp.float32)], axis=1)
    cells = jnp.concatenate([cells, jnp.zeros((BLOCK - cells.shape[0], BLOCK), jnp.float32)], axis=0)
    return cells.T[:rows]


def names_at(fetch, row):
    planes, blocks, rows = fetch.shape
    lane = lax.broadcasted_iota(jnp.int32, (planes, rows), 1)
    wide = []
    for b in range(blocks):
        own = jnp.concatenate([fetch[z, b : b + 1, :] for z in range(planes)], axis=0).astype(jnp.float32)
        own = jnp.sum(jnp.where(lane == row, own, 0.0), axis=1, keepdims=True)
        wide.append(jnp.broadcast_to(own, (planes, BLOCK)))
    return jnp.concatenate(wide, axis=1)


def edge_rows_kernel(moving_in, fetch_in, first, last, moving, fetch, done):
    fetch_all([(moving_in, moving), (fetch_in, fetch)], done)
    planes, rows, _ = moving.shape
    for row, out in ((0, first), (rows - 1, last)):
        own = jnp.concatenate(
            [moving[z].astype(jnp.float32)[row : row + 1] for z in range(planes)], axis=0
        )
        out[...] = jnp.concatenate([own, names_at(fetch, row)], axis=0).astype(jnp.bfloat16)


def send_weights_kernel(slabs, place, stiffness_in, tissue_in, *refs):
    weights, (wide, stiffness, tissue, done) = refs[:slabs], refs[slabs:]
    fetch_all([(stiffness_in, stiffness), (tissue_in, tissue)], done)
    planes, rows, x_length = stiffness.shape
    share = rows // slabs
    blocks = x_length // BLOCK
    marks = by_row(tissue, rows)
    for z in range(planes):
        marked = jnp.concatenate(
            [
                jnp.broadcast_to(marks[:, z * blocks + b : z * blocks + b + 1], (rows, BLOCK))
                for b in range(blocks)
            ],
            axis=1,
        )
        wide[z] = marked * stiffness[z] * COEFFICIENT_UNIT + 0.5
    for step in range(slabs):
        part = pl.ds(pl.multiple_of(around(place[0] + step, slabs) * share, share), share)
        for z in range(0, planes, 2):
            both = jnp.concatenate([wide[z, part, :], wide[z + 1, part, :]], axis=0)
            weights[step][z * share : (z + 2) * share] = both.astype(jnp.int32).astype(jnp.int16)


def send_images_kernel(slabs, place, moving_in, template_in, fetch_in, above, below, *refs):
    images, (wide, names, moving, template, fetch, done) = refs[:slabs], refs[slabs:]
    fetch_all([(moving_in, moving), (template_in, template), (fetch_in, fetch)], done)
    planes, rows, x_length = moving.shape
    share = rows // slabs
    blocks = x_length // BLOCK
    lane = lax.broadcasted_iota(jnp.int32, (planes, BLOCK), 1)
    names[...] = by_row(fetch, rows)
    over, under = above[...].astype(jnp.float32), below[...].astype(jnp.float32)
    for z in range(planes):
        wide[z, share : share + rows, :] = moving[z].astype(jnp.float32)
        wide[z, share - 1 : share, :] = over[z : z + 1]
        wide[z, share + rows : share + rows + 1, :] = under[z : z + 1]
        wide[planes + z, 0:rows, :] = template[z].astype(jnp.float32)

    def narrow(cells):
        packed = jnp.zeros((planes, BLOCK), jnp.float32)
        for b in range(blocks):
            packed = jnp.where(lane == b, cells[:, b * BLOCK : (b + 1) * BLOCK], packed)
        return packed

    for step in range(slabs):
        to = around(place[0] + step, slabs)
        first = pl.multiple_of(to * share, share)
        for z in range(0, planes, 2):
            part = pl.ds(first + share, share)
            both = jnp.concatenate([wide[z, part, :], wide[z + 1, part, :]], axis=0)
            images[step][z * share : (z + 2) * share] = both.astype(jnp.bfloat16)
            part = pl.ds(first, share)
            both = jnp.concatenate([wide[planes + z, part, :], wide[planes + z + 1, part, :]], axis=0)
            images[step][(planes + z) * share : (planes + z + 2) * share] = both.astype(jnp.bfloat16)
        before = jnp.where(to == 0, over[planes:], names_at(fetch, first - 1))
        after = jnp.where(to == slabs - 1, under[planes:], names_at(fetch, first + share))
        asked = [names[pl.ds(first, share), :], narrow(before), narrow(after)]
        asked = jnp.concatenate(asked + [asked[0]] * (blocks - 3), axis=1)
        row_over = jnp.concatenate([wide[z, pl.ds(first + (share - 1), 1), :] for z in range(planes)], axis=0)
        row_under = jnp.concatenate([wide[z, pl.ds(first + 2 * share, 1), :] for z in range(planes)], axis=0)
        base = 2 * planes * share
        images[step][base : base + 16] = jnp.concatenate([asked, row_over], axis=0).astype(jnp.bfloat16)
        images[step][base + 16 : base + 24] = row_under.astype(jnp.bfloat16)


def pick_kernel(slabs, planes, place, *refs):
    received, sends = refs[:slabs], refs[slabs : 2 * slabs]
    image, residual, edges = refs[2 * slabs :]
    total, share, x_length = image.shape
    blocks = x_length // BLOCK
    base = 2 * planes * share
    me = place[0]
    group = 2

    def spread(cells, first):
        return jnp.concatenate(
            [jnp.broadcast_to(cells[:, k : k + 1], (share, BLOCK)) for k in range(first, first + blocks)], axis=1
        )

    asked = [r[base : base + 16].astype(jnp.float32) for r in received]
    rows_of = [[a[8:16] for a in asked], [r[base + 16 : base + 24].astype(jnp.float32) for r in received]]
    asked = [a[0:8] for a in asked]
    for step in range(slabs):
        mine = around(me - step, slabs) * planes
        for start in range(0, planes, group):
            wanted = [spread(asked[step], z * blocks) for z in range(start, start + group)]
            found = [jnp.zeros((share, x_length), jnp.float32) for _ in range(group)]
            for other in range(slabs):
                name = (around(me - other, slabs) * planes).astype(jnp.float32)
                for plane in range(0, planes, 2):
                    both = received[other][plane * share : (plane + 2) * share].astype(jnp.float32)
                    for k in range(2):
                        values = both[k * share : (k + 1) * share]
                        found = [
                            jnp.where(w == name + float(plane + k), values, f) for w, f in zip(wanted, found)
                        ]
            both = received[step][(planes + start) * share : (planes + start + 2) * share].astype(jnp.float32)
            for k in range(group):
                z = mine + (start + k)
                image[z] = found[k]
                residual[z] = found[k] - both[k * share : (k + 1) * share]
        wanted = [spread(asked[step], (1 + side) * BLOCK) for side in range(2)]
        found = [jnp.zeros((planes, x_length), jnp.float32) for _ in range(2)]
        for other in range(slabs):
            name = (around(me - other, slabs) * planes).astype(jnp.float32)
            for plane in range(planes):
                found = [
                    jnp.where(w == name + float(plane), rows_of[side][other][plane : plane + 1], f)
                    for side, (w, f) in enumerate(zip(wanted, found))
                ]
        for side in range(2):
            edges[side, pl.ds(pl.multiple_of(mine, planes), planes), :] = found[side]
    for step, send in enumerate(sends):
        mine = around(me + step, slabs) * planes
        for z in range(0, planes, 2):
            both = jnp.concatenate([image[mine + z], image[mine + (z + 1)]], axis=0)
            send[z * share : (z + 2) * share] = both.astype(jnp.bfloat16)


def force_kernel(slabs, place, *refs):
    weights = refs[:slabs]
    image, residual, edges, basis_x, basis_z, spectra, force = refs[slabs:]
    total, share, x_length = image.shape
    planes = total // slabs
    me = place[0]
    row = lax.broadcasted_iota(jnp.int32, (share, x_length), 0)
    for step in range(slabs):
        base = around(me - step, slabs) * planes
        for start in range(0, planes, 2):
            both = weights[step][start * share : (start + 2) * share].astype(jnp.int32).astype(jnp.float32)
            for k in range(2):
                z = base + (start + k)
                here = image[z]
                weight = both[k * share : (k + 1) * share] * (residual[z] * (0.5 / COEFFICIENT_UNIT))
                before = jnp.where(row == 0, edges[0, pl.ds(z, 1), :], pltpu.roll(here, 1, 0))
                after = jnp.where(row == share - 1, edges[1, pl.ds(z, 1), :], pltpu.roll(here, share - 1, 0))
                force[0, z] = weight * (image[around(z + 1, total)] - image[around(z - 1, total)])
                force[1, z] = weight * (after - before)
                force[2, z] = weight * (pltpu.roll(here, x_length - 1, 1) - pltpu.roll(here, 1, 1))
    devices, part = spectra.shape[:2]
    part //= 3
    for a in range(3):
        own = split(force[a].reshape(total * share, x_length))
        own = split(times((basis_z[0], basis_z[1]), own, ((1,), (0,))))
        own = times((basis_x[0], basis_x[1]), own, ((1,), (1,)))
        spectra[:, a * part : (a + 1) * part, :] = own.reshape(devices, part, total * share)


def solve_kernel(subs, place, spectra, basis_z, basis_y, out, cells):
    devices, lanes_used, area = spectra.shape
    total_z, total_y, lanes = cells.shape
    slabs = devices // subs
    planes, rows = total_z // slabs, total_y // subs
    share = rows // slabs
    pad = jnp.zeros((lanes - lanes_used, area), jnp.float32)
    for d in range(devices):
        s, q = d // subs, d % subs
        block = jnp.concatenate([spectra[d], pad], axis=0).T.reshape(total_z, share, lanes)
        cells[:, q * rows + s * share : q * rows + (s + 1) * share, :] = block
    tables_z, tables_y = (basis_z[0], basis_z[1]), (basis_y[0], basis_y[1])
    part = lanes_used // 3
    lane = lax.broadcasted_iota(jnp.int32, (1, lanes), 1)
    x_sq = wave_sq(place[0] * part + lax.rem(lane, part), part * devices)
    y_sq = wave_sq(lax.broadcasted_iota(jnp.int32, (total_y, 1), 0), total_y)
    xy = (x_sq + y_sq) * 256.0 + 1.0
    for z in range(0, total_z, 2):
        own = jnp.concatenate([cells[z], cells[z + 1]], axis=1)
        own = times(tables_y, split(own), ((1,), (0,)))
        scale = []
        for k in range(2):
            wave = 2.0 * np.pi / total_z * (z + k if z + k <= total_z // 2 else z + k - total_z // 2)
            scale.append(xy + 256.0 * wave * wave)
        own = own / jnp.concatenate(scale, axis=1)
        own = times(tables_y, split(own), ((0,), (0,)))
        cells[z] = own[:, :lanes]
        cells[z + 1] = own[:, lanes:]
    for g in range(0, total_y, 2 * share):
        own = jnp.concatenate(
            [cells[:, y : y + share, :].reshape(area, lanes) for y in (g, g + share)], axis=1
        )
        own = times(tables_z, split(own), ((0,), (0,)))
        cells[:, g : g + share, :] = own[:, :lanes].reshape(total_z, share, lanes)
        cells[:, g + share : g + 2 * share, :] = own[:, lanes:].reshape(total_z, share, lanes)
    for d in range(devices):
        s, q = d // subs, d % subs
        block = cells[s * planes : (s + 1) * planes, q * rows : (q + 1) * rows, :]
        out[d] = block.reshape(area, lanes).T[:lanes_used]


def update_kernel(slabs, place, spectra, velocity, basis, *refs):
    received, (out, warped, wide) = refs[:slabs], refs[slabs:]
    devices, part, area = spectra.shape
    part //= 3
    _, planes, rows, x_length = velocity.shape
    share = rows // slabs
    for step in range(slabs):
        place_of = pl.ds(pl.multiple_of(around(place[0] - step, slabs) * share, share), share)
        for z in range(0, planes, 2):
            both = received[step][z * share : (z + 2) * share].astype(jnp.float32)
            wide[z, place_of, :] = both[:share]
            wide[z + 1, place_of, :] = both[share:]
    warped[...] = wide[...].astype(jnp.bfloat16)
    for a in range(3):
        own = spectra[:, a * part : (a + 1) * part, :].reshape(x_length, area).T
        smoothed = times(split(own), (basis[0], basis[1]), ((1,), (0,)))
        out[a] = 0.5 * (velocity[a] - 32.0 * smoothed.reshape(planes, rows, x_length))


def local_rows(velocity, template, moving, stiffness, fetch_plane, tissue):
    planes, rows, x_length = moving.shape
    slabs, subs = lax.axis_size("slab"), lax.axis_size("sub")
    total_z, total_y = planes * slabs, rows * subs
    devices = slabs * subs
    part = x_length // devices
    area = planes * rows
    share = rows // slabs
    both_axes = ("slab", "sub")
    my_slab = lax.axis_index("slab")
    my_place = my_slab * subs + lax.axis_index("sub")
    slab_id, place_id = my_slab.reshape(1), my_place.reshape(1)
    bf16, f32 = jnp.bfloat16, jnp.float32

    def shape(dims, kind=f32):
        return jax.ShapeDtypeStruct(dims, kind)

    def scatter(sends):
        return [sends[0]] + [
            lax.ppermute(sends[d], "slab", [(i, (i + d) % slabs) for i in range(slabs)])
            for d in range(1, slabs)
        ]

    def exchange(values):
        return lax.all_to_all(values, both_axes, split_axis=0, concat_axis=0, tiled=True)

    fetch, marks = fetch_plane.swapaxes(1, 2), tissue.swapaxes(1, 2)
    brick, field = pltpu.VMEM(moving.shape, bf16), pltpu.VMEM(stiffness.shape, f32)
    small = pltpu.VMEM(fetch.shape, jnp.int32)
    first, last = call(
        edge_rows_kernel,
        [shape((2 * planes, x_length), bf16)] * 2,
        (moving,),
        (fetch,),
        scratch=[brick, small, pltpu.SemaphoreType.DMA((2,))],
    )
    above = lax.ppermute(last, "sub", [(i, (i + 1) % subs) for i in range(subs)])
    below = lax.ppermute(first, "sub", [((i + 1) % subs, i) for i in range(subs)])
    weights = call(
        functools.partial(send_weights_kernel, slabs),
        [shape((planes * share, x_length), jnp.int16)] * slabs,
        slab_id,
        (stiffness,),
        (marks,),
        scratch=[field, field, small, pltpu.SemaphoreType.DMA((2,))],
    )
    weights = scatter(weights)
    images = call(
        functools.partial(send_images_kernel, slabs),
        [shape(((2 * planes + 3) * share, x_length), bf16)] * slabs,
        slab_id,
        (moving,),
        (template,),
        (fetch,),
        above,
        below,
        scratch=[
            pltpu.VMEM((2 * planes, rows + 2 * share, x_length), f32),
            pltpu.VMEM((rows, BLOCK), f32),
            brick,
            brick,
            small,
            pltpu.SemaphoreType.DMA((3,)),
        ],
    )
    images = scatter(images)
    *sends, image, residual, edges = call(
        functools.partial(pick_kernel, slabs, planes),
        [shape((planes * share, x_length), bf16)] * slabs
        + [shape((total_z, share, x_length))] * 2
        + [shape((2, total_z, x_length))],
        slab_id,
        *images,
        flops=1 << 30,
    )
    warped = scatter(sends)
    basis_z = in_two(np.kron(real_basis(total_z), np.eye(share)))
    spectra = call(
        functools.partial(force_kernel, slabs),
        shape((devices, 3 * part, area)),
        slab_id,
        *weights,
        image,
        residual,
        edges,
        in_two(8.0 * real_basis(x_length)),
        basis_z,
        scratch=[pltpu.VMEM((3, total_z, share, x_length), f32)],
        flops=3 << 30,
    )
    spectra = spectra.astype(jnp.float16)
    spectra, warped = lax.optimization_barrier((spectra, warped))
    spectra = exchange(spectra)
    spectra = call(
        functools.partial(solve_kernel, subs),
        shape((devices, 3 * part, area)),
        place_id,
        spectra.astype(f32),
        basis_z,
        in_two(real_basis(total_y)),
        scratch=[pltpu.VMEM((total_z, total_y, 128), f32)],
        flops=3 << 30,
    )
    spectra = exchange(spectra.astype(jnp.float16))
    return tuple(
        call(
            functools.partial(update_kernel, slabs),
            [shape(velocity.shape), shape(moving.shape, bf16)],
            slab_id,
            spectra.astype(f32),
            velocity,
            in_two(real_basis(x_length)),
            *warped,
            scratch=[pltpu.VMEM((planes, rows, x_length), f32)],
            flops=3 << 30,
        )
    )


def local(velocity, template, moving, stiffness, fetch_plane, tissue):
    planes, rows, x_length = moving.shape
    slabs, subs = lax.axis_size("slab"), lax.axis_size("sub")
    part = x_length // (slabs * subs)
    fits = (
        planes == 8
        and rows == 8 * slabs
        and part % 8 == 0
        and 3 * part <= BLOCK
        and planes * slabs * 8 == 256
        and rows * subs == BLOCK
        and planes * (x_length // BLOCK) <= BLOCK
        and 3 <= x_length // BLOCK <= BLOCK
    )
    run = local_rows if fits else local_general
    return run(velocity, template, moving, stiffness, fetch_plane, tissue)


def solution(mesh):
    placed = (
        P(None, ("groups", "slab"), "sub", None),
        P(("groups", "slab"), "sub", None),
        P(("groups", "slab"), "sub", None),
        P(("groups", "slab"), "sub", None),
        P(("groups", "slab"), "sub", None),
        P(("groups", "slab"), "sub", None),
    )
    return jax.shard_map(
        local,
        mesh=mesh,
        in_specs=placed,
        out_specs=(P(None, ("groups", "slab"), "sub", None), P(("groups", "slab"), "sub", None)),
        check_vma=False,
    )
```

```python
import functools

import jax
import jax.numpy as jnp
import numpy as np
from jax import lax
from jax.experimental import pallas as pl
from jax.experimental.pallas import tpu as pltpu
from jax.sharding import PartitionSpec as P

BLOCK = 128


def extended(cells, sides, width):
    for axis, dim in sides:
        count = lax.axis_size(axis)
        head = lax.slice_in_dim(cells, 0, width, axis=dim)
        tail = lax.slice_in_dim(cells, cells.shape[dim] - width, cells.shape[dim], axis=dim)
        cells = jnp.concatenate(
            [
                lax.ppermute(tail, axis, [(i, (i + 1) % count) for i in range(count)]),
                cells,
                lax.ppermute(head, axis, [((i + 1) % count, i) for i in range(count)]),
            ],
            axis=dim,
        )
    return cells


def tables(length):
    wave_ids = jnp.arange(length, dtype=jnp.int32)
    phase = wave_ids[:, None] * wave_ids[None, :] % length
    angle = 2.0 * jnp.pi / length * phase.astype(jnp.float32)
    return (jnp.cos(angle), jnp.sin(angle))


def apply_along(values, matrix, axis_id):
    result = lax.dot_general(
        values,
        matrix,
        (((axis_id,), (0,)), ((), ())),
        precision=lax.Precision.HIGHEST,
        preferred_element_type=jnp.float32,
    )
    return jnp.moveaxis(result, -1, axis_id)


def forward_along(values_pair, axis_id):
    real_part, imag_part = values_pair
    cosine, sine = tables(real_part.shape[axis_id])
    return (
        apply_along(real_part, cosine, axis_id) + apply_along(imag_part, sine, axis_id),
        apply_along(imag_part, cosine, axis_id) - apply_along(real_part, sine, axis_id),
    )


def inverse_along(values_pair, axis_id):
    real_part, imag_part = values_pair
    length = real_part.shape[axis_id]
    cosine, sine = tables(length)
    scale = 1.0 / length
    return (
        (apply_along(real_part, cosine, axis_id) - apply_along(imag_part, sine, axis_id)) * scale,
        (apply_along(imag_part, cosine, axis_id) + apply_along(real_part, sine, axis_id)) * scale,
    )


def symbol_sq(length, first_id, span):
    wave_ids = first_id + jnp.arange(span, dtype=jnp.int32)
    signed = jnp.where(wave_ids < length // 2, wave_ids, wave_ids - length).astype(jnp.float32)
    wave = 2.0 * jnp.pi / length * signed
    return wave * wave


def local_general(velocity, template, moving, stiffness, fetch_plane, tissue):
    planes_dev, rows_dev, x_length = moving.shape
    blocks_x = x_length // BLOCK
    slabs = lax.axis_size("slab")
    subs = lax.axis_size("sub")
    my_slab = lax.axis_index("slab")
    my_sub = lax.axis_index("sub")
    per_dev = planes_dev * rows_dev * blocks_x
    capacity = 2 * per_dev // slabs
    source_plane = fetch_plane.reshape(-1)
    block_ids = jnp.arange(per_dev, dtype=jnp.int32)
    row_of = block_ids // blocks_x % rows_dev
    column_of = block_ids % blocks_x
    moving_rows = moving.reshape(per_dev, BLOCK)
    holder = source_plane // planes_dev
    within = (source_plane % planes_dev * rows_dev + row_of) * blocks_x + column_of
    matches = (holder[:, None] == jnp.arange(slabs, dtype=jnp.int32)[None, :]).astype(jnp.int32)
    earlier = jnp.sum((jnp.cumsum(matches, axis=0) - matches) * matches, axis=1)
    target = holder * capacity + earlier
    wanted = (
        jnp.zeros((slabs * capacity,), jnp.int32).at[target].set(within).reshape(slabs, capacity)
    )
    asked = lax.all_to_all(wanted, "slab", split_axis=0, concat_axis=0, tiled=True)
    fetched = moving_rows[asked.reshape(-1)].reshape(asked.shape + (BLOCK,))
    replies = lax.all_to_all(fetched, "slab", split_axis=0, concat_axis=0, tiled=True)
    warped_rows = replies.reshape(slabs * capacity, BLOCK)[target]
    warped = warped_rows.reshape(planes_dev, rows_dev, x_length)
    padded = extended(warped, (("slab", 0), ("sub", 1)), 1).astype(jnp.float32)
    image = padded[1:-1, 1:-1]
    grad_z = 0.5 * (padded[2:, 1:-1] - padded[:-2, 1:-1])
    grad_y = 0.5 * (padded[1:-1, 2:] - padded[1:-1, :-2])
    grad_x = 0.5 * (jnp.roll(image, -1, 2) - jnp.roll(image, 1, 2))
    residual = image - template.astype(jnp.float32)
    tissue_vox = jnp.repeat(tissue.astype(jnp.float32), BLOCK, axis=2)
    weight_field = tissue_vox * stiffness * residual
    force = jnp.stack([weight_field * grad_z, weight_field * grad_y, weight_field * grad_x])
    cos_x, sin_x = tables(x_length)
    real_part = apply_along(force, cos_x, 3)
    imag_part = -apply_along(force, sin_x, 3)
    moved = (
        lax.all_to_all(real_part, "sub", split_axis=3, concat_axis=2, tiled=True),
        lax.all_to_all(imag_part, "sub", split_axis=3, concat_axis=2, tiled=True),
    )
    moved = forward_along(moved, 2)
    moved = (
        lax.all_to_all(moved[0], "slab", split_axis=2, concat_axis=1, tiled=True),
        lax.all_to_all(moved[1], "slab", split_axis=2, concat_axis=1, tiled=True),
    )
    moved = forward_along(moved, 1)
    total_z = moved[0].shape[1]
    y_span = moved[0].shape[2]
    x_span = moved[0].shape[3]
    factor = 1.0 / (
        symbol_sq(total_z, 0, total_z)[:, None, None]
        + symbol_sq(y_span * slabs, my_slab * y_span, y_span)[None, :, None]
        + symbol_sq(x_span * subs, my_sub * x_span, x_span)[None, None, :]
        + 1.0 / 256.0
    )
    moved = (moved[0] * factor, moved[1] * factor)
    moved = inverse_along(moved, 1)
    moved = (
        lax.all_to_all(moved[0], "slab", split_axis=1, concat_axis=2, tiled=True),
        lax.all_to_all(moved[1], "slab", split_axis=1, concat_axis=2, tiled=True),
    )
    moved = inverse_along(moved, 2)
    real_part, imag_part = (
        lax.all_to_all(moved[0], "sub", split_axis=2, concat_axis=3, tiled=True),
        lax.all_to_all(moved[1], "sub", split_axis=2, concat_axis=3, tiled=True),
    )
    smoothed = (apply_along(real_part, cos_x, 3) - apply_along(imag_part, sin_x, 3)) * (
        1.0 / x_length
    )
    new_velocity = 0.5 * (velocity - smoothed)
    return (new_velocity, warped)


VMEM_BYTES = 24 * 1024 * 1024
WHOLE_VMEM_BYTES = 63 * 1024 * 1024
COEFFICIENT_UNIT = 8191.0


def real_basis(length):
    index = np.arange(length)
    half = length // 2
    wave = np.where(index <= half, index, index - half)[:, None]
    angle = 2.0 * np.pi / length * (wave * index[None, :] % length)
    rows = np.where(index[:, None] <= half, np.cos(angle), np.sin(angle)) * np.sqrt(2.0 / length)
    rows[0] /= np.sqrt(2.0)
    rows[half] /= np.sqrt(2.0)
    return rows


def in_two(table):
    high = np.asarray(table, np.float32).astype(jnp.bfloat16)
    low = (np.asarray(table, np.float64) - high.astype(np.float64)).astype(jnp.bfloat16)
    return np.stack([high, low])


def split(values):
    high = values.astype(jnp.bfloat16)
    return high, (values - high.astype(jnp.float32)).astype(jnp.bfloat16)


def times(left, right, dims):
    def one(a, b):
        return lax.dot_general(a, b, (dims, ((), ())), preferred_element_type=jnp.float32)

    return one(left[0], right[0]) + (one(left[0], right[1]) + one(left[1], right[0]))


def wave_sq(index, length):
    wave = jnp.where(index <= length // 2, index, index - length // 2).astype(jnp.float32)
    wave = wave * (2.0 * np.pi / length)
    return wave * wave


def around(value, count):
    return lax.rem(value + 2 * count, count)


def call(kernel, out_shape, *arguments, scratch=(), flops=0, stays=0, limit=VMEM_BYTES):
    places = [
        pl.BlockSpec(memory_space=pltpu.HBM if isinstance(a, tuple) else pltpu.SMEM if a.ndim == 1 else pltpu.VMEM)
        for a in arguments
    ]
    arguments = [a[0] if isinstance(a, tuple) else a for a in arguments]
    out_places = [
        pl.BlockSpec(memory_space=pltpu.HBM if k < stays else pltpu.VMEM)
        for k in range(len(jax.tree.leaves(out_shape)))
    ]
    nbytes = sum(a.size * a.dtype.itemsize for a in arguments + jax.tree.leaves(out_shape))
    return pl.pallas_call(
        kernel,
        out_shape=out_shape,
        in_specs=places,
        out_specs=jax.tree.unflatten(jax.tree.structure(out_shape), out_places),
        scratch_shapes=list(scratch),
        compiler_params=pltpu.CompilerParams(vmem_limit_bytes=limit),
        cost_estimate=pl.CostEstimate(flops=flops, bytes_accessed=nbytes, transcendentals=0),
    )(*arguments)


def fetch_all(pairs, done):
    copies = [pltpu.make_async_copy(src, dst, done.at[k]) for k, (src, dst) in enumerate(pairs)]
    for copy in copies:
        copy.start()
    for copy in copies:
        copy.wait()


def by_row(ref, rows):
    cells = jnp.concatenate([ref[z].astype(jnp.float32) for z in range(ref.shape[0])], axis=0)
    cells = jnp.concatenate([cells, jnp.zeros((cells.shape[0], BLOCK - rows), jnp.float32)], axis=1)
    cells = jnp.concatenate([cells, jnp.zeros((BLOCK - cells.shape[0], BLOCK), jnp.float32)], axis=0)
    return cells.T[:rows]


def names_at(fetch, row):
    planes, blocks, rows = fetch.shape
    lane = lax.broadcasted_iota(jnp.int32, (planes, rows), 1)
    wide = []
    for b in range(blocks):
        own = jnp.concatenate([fetch[z, b : b + 1, :] for z in range(planes)], axis=0).astype(jnp.float32)
        own = jnp.sum(jnp.where(lane == row, own, 0.0), axis=1, keepdims=True)
        wide.append(jnp.broadcast_to(own, (planes, BLOCK)))
    return jnp.concatenate(wide, axis=1)


def send_rows_kernel(slabs, place, *refs):
    arguments, refs = refs[:5], refs[5:]
    images, weights, edges = refs[:slabs], refs[slabs : 2 * slabs], refs[2 * slabs : 3 * slabs]
    (first, last), refs = refs[3 * slabs : -8], refs[-8:]
    wide, names, (moving, template, fetch, stiffness, tissue), done = refs[0], refs[1], refs[2:7], refs[7]
    fetch_all(list(zip(arguments, (moving, template, fetch, stiffness, tissue))), done)
    planes, rows, x_length = moving.shape
    share = rows // slabs
    blocks = x_length // BLOCK
    names[...] = by_row(fetch, rows)
    marks = by_row(tissue, rows)
    for z in range(planes):
        wide[z] = moving[z].astype(jnp.float32)
        wide[planes + z] = template[z].astype(jnp.float32)
        marked = jnp.concatenate(
            [
                jnp.broadcast_to(marks[:, z * blocks + b : z * blocks + b + 1], (rows, BLOCK))
                for b in range(blocks)
            ],
            axis=1,
        )
        wide[2 * planes + z] = marked * stiffness[z] * COEFFICIENT_UNIT + 0.5
    def edge(row):
        own = [wide[z, pl.ds(row, 1), :] for z in range(planes)]
        return jnp.concatenate(own, axis=0), names_at(fetch, row)

    for row, out in ((0, first), (rows - 1, last)):
        out[...] = jnp.concatenate(edge(row), axis=0).astype(jnp.bfloat16)
    for step in range(slabs):
        to = around(place[0] + step, slabs)
        over, over_names = edge(jnp.maximum(to * share - 1, 0))
        under, under_names = edge(jnp.minimum((to + 1) * share, rows - 1))
        edges[step][0:16] = jnp.concatenate([over, under], axis=0).astype(jnp.bfloat16)
        edges[step][16:32] = jnp.concatenate([over_names, under_names], axis=0).astype(jnp.bfloat16)
    for step in range(slabs):
        part = pl.ds(pl.multiple_of(around(place[0] + step, slabs) * share, share), share)
        for z in range(0, 2 * planes, 2):
            both = jnp.concatenate([wide[z, part, :], wide[z + 1, part, :]], axis=0)
            images[step][z * share : (z + 2) * share] = both.astype(jnp.bfloat16)
        asked = jnp.concatenate([names[part, :]] * blocks, axis=1)
        images[step][2 * planes * share : (2 * planes + 1) * share] = asked.astype(jnp.bfloat16)
        for z in range(0, planes, 2):
            both = jnp.concatenate([wide[2 * planes + z, part, :], wide[2 * planes + z + 1, part, :]], axis=0)
            weights[step][z * share : (z + 2) * share] = both.astype(jnp.int32).astype(jnp.int16)


def send_edges_kernel(slabs, place, above, below, *refs):
    edges, sends = refs[:slabs], refs[slabs:]
    planes = above.shape[0] // 2
    over, under = above[...].astype(jnp.float32), below[...].astype(jnp.float32)
    for step in range(slabs):
        to = around(place[0] + step, slabs)
        for half in range(2):
            own = edges[step][2 * planes * half : 2 * planes * (half + 1)].astype(jnp.float32)
            part = slice(planes * half, planes * (half + 1))
            before = jnp.where(to == 0, over[part], own[:planes])
            after = jnp.where(to == slabs - 1, under[part], own[planes:])
            own = jnp.concatenate([before, after], axis=0)
            sends[step][2 * planes * half : 2 * planes * (half + 1)] = own.astype(jnp.bfloat16)


def pick_kernel(slabs, planes, place, *refs):
    received, sides, sends = refs[:slabs], refs[slabs : 2 * slabs], refs[2 * slabs : 3 * slabs]
    image, residual, edges = refs[3 * slabs :]
    total, share, x_length = image.shape
    blocks = x_length // BLOCK
    base = 2 * planes * share
    me = place[0]
    group = 2

    def spread(cells, first):
        return jnp.concatenate(
            [jnp.broadcast_to(cells[:, k : k + 1], (share, BLOCK)) for k in range(first, first + blocks)], axis=1
        )

    asked = [r[base : base + 8].astype(jnp.float32) for r in received]
    beside = [s[0:16].astype(jnp.float32) for s in sides]
    rows_of = [[b[0:8] for b in beside], [b[8:16] for b in beside]]
    beside = [s[16:32].astype(jnp.float32) for s in sides]
    for step in range(slabs):
        mine = around(me - step, slabs) * planes
        for start in range(0, planes, group):
            wanted = [spread(asked[step], z * blocks) for z in range(start, start + group)]
            found = [jnp.zeros((share, x_length), jnp.float32) for _ in range(group)]
            for other in range(slabs):
                name = (around(me - other, slabs) * planes).astype(jnp.float32)
                for plane in range(0, planes, 2):
                    both = received[other][plane * share : (plane + 2) * share].astype(jnp.float32)
                    for k in range(2):
                        values = both[k * share : (k + 1) * share]
                        found = [
                            jnp.where(w == name + float(plane + k), values, f) for w, f in zip(wanted, found)
                        ]
            both = received[step][(planes + start) * share : (planes + start + 2) * share].astype(jnp.float32)
            for k in range(group):
                z = mine + (start + k)
                image[z] = found[k]
                residual[z] = found[k] - both[k * share : (k + 1) * share]
        wanted = [beside[step][side * planes : (side + 1) * planes] for side in range(2)]
        found = [jnp.zeros((planes, x_length), jnp.float32) for _ in range(2)]
        for other in range(slabs):
            name = (around(me - other, slabs) * planes).astype(jnp.float32)
            for plane in range(planes):
                found = [
                    jnp.where(w == name + float(plane), rows_of[side][other][plane : plane + 1], f)
                    for side, (w, f) in enumerate(zip(wanted, found))
                ]
        for side in range(2):
            edges[side, pl.ds(pl.multiple_of(mine, planes), planes), :] = found[side]
    for step, send in enumerate(sends):
        mine = around(me + step, slabs) * planes
        for z in range(0, planes, 2):
            both = jnp.concatenate([image[mine + z], image[mine + (z + 1)]], axis=0)
            send[z * share : (z + 2) * share] = both.astype(jnp.bfloat16)


def force_kernel(slabs, place, *refs):
    weights = refs[:slabs]
    image, residual, edges, basis_x, basis_z, spectra, force = refs[slabs:]
    total, share, x_length = image.shape
    planes = total // slabs
    me = place[0]
    row = lax.broadcasted_iota(jnp.int32, (share, x_length), 0)
    for step in range(slabs):
        base = around(me - step, slabs) * planes
        for start in range(0, planes, 2):
            both = weights[step][start * share : (start + 2) * share].astype(jnp.int32).astype(jnp.float32)
            for k in range(2):
                z = base + (start + k)
                here = image[z]
                weight = both[k * share : (k + 1) * share] * (residual[z] * (0.5 / COEFFICIENT_UNIT))
                before = jnp.where(row == 0, edges[0, pl.ds(z, 1), :], pltpu.roll(here, 1, 0))
                after = jnp.where(row == share - 1, edges[1, pl.ds(z, 1), :], pltpu.roll(here, share - 1, 0))
                force[0, z] = weight * (image[around(z + 1, total)] - image[around(z - 1, total)])
                force[1, z] = weight * (after - before)
                force[2, z] = weight * (pltpu.roll(here, x_length - 1, 1) - pltpu.roll(here, 1, 1))
    devices, part = spectra.shape[:2]
    part //= 3
    for a in range(3):
        own = split(force[a].reshape(total * share, x_length))
        own = split(times((basis_z[0], basis_z[1]), own, ((1,), (0,))))
        own = times((basis_x[0], basis_x[1]), own, ((1,), (1,)))
        spectra[:, a * part : (a + 1) * part, :] = own.reshape(devices, part, total * share)


def solve_kernel(subs, place, spectra, basis_z, basis_y, out, cells):
    devices, lanes_used, area = spectra.shape
    total_z, total_y, lanes = cells.shape
    slabs = devices // subs
    planes, rows = total_z // slabs, total_y // subs
    share = rows // slabs
    pad = jnp.zeros((lanes - lanes_used, area), jnp.float32)
    for d in range(devices):
        s, q = d // subs, d % subs
        block = jnp.concatenate([spectra[d], pad], axis=0).T.reshape(total_z, share, lanes)
        cells[:, q * rows + s * share : q * rows + (s + 1) * share, :] = block
    tables_z, tables_y = (basis_z[0], basis_z[1]), (basis_y[0], basis_y[1])
    part = lanes_used // 3
    lane = lax.broadcasted_iota(jnp.int32, (1, lanes), 1)
    x_sq = wave_sq(place[0] * part + lax.rem(lane, part), part * devices)
    y_sq = wave_sq(lax.broadcasted_iota(jnp.int32, (total_y, 1), 0), total_y)
    xy = (x_sq + y_sq) * 256.0 + 1.0
    for z in range(0, total_z, 2):
        own = jnp.concatenate([cells[z], cells[z + 1]], axis=1)
        own = times(tables_y, split(own), ((1,), (0,)))
        scale = []
        for k in range(2):
            wave = 2.0 * np.pi / total_z * (z + k if z + k <= total_z // 2 else z + k - total_z // 2)
            scale.append(xy + 256.0 * wave * wave)
        own = own / jnp.concatenate(scale, axis=1)
        own = times(tables_y, split(own), ((0,), (0,)))
        cells[z] = own[:, :lanes]
        cells[z + 1] = own[:, lanes:]
    for g in range(0, total_y, 2 * share):
        own = jnp.concatenate(
            [cells[:, y : y + share, :].reshape(area, lanes) for y in (g, g + share)], axis=1
        )
        own = times(tables_z, split(own), ((0,), (0,)))
        cells[:, g : g + share, :] = own[:, :lanes].reshape(total_z, share, lanes)
        cells[:, g + share : g + 2 * share, :] = own[:, lanes:].reshape(total_z, share, lanes)
    for d in range(devices):
        s, q = d // subs, d % subs
        block = cells[s * planes : (s + 1) * planes, q * rows : (q + 1) * rows, :]
        out[d] = block.reshape(area, lanes).T[:lanes_used]


def update_kernel(slabs, place, velocity_in, spectra, basis, *refs):
    received, (out, warped, wide, velocity, result, done) = refs[:slabs], refs[slabs:]
    devices, part, area = spectra.shape
    part //= 3
    _, planes, rows, x_length = velocity.shape
    share = rows // slabs
    arriving = [pltpu.make_async_copy(velocity_in.at[a], velocity.at[a], done.at[a]) for a in range(3)]
    leaving = [pltpu.make_async_copy(result.at[a], out.at[a], done.at[3 + a]) for a in range(3)]
    for copy in arriving:
        copy.start()
    for a in range(3):
        own = spectra[:, a * part : (a + 1) * part, :].reshape(x_length, area).T
        smoothed = times(split(own), (basis[0], basis[1]), ((1,), (0,)))
        arriving[a].wait()
        result[a] = 0.5 * (velocity[a] - 32.0 * smoothed.reshape(planes, rows, x_length))
        leaving[a].start()
    for step in range(slabs):
        place_of = pl.ds(pl.multiple_of(around(place[0] - step, slabs) * share, share), share)
        for z in range(0, planes, 2):
            both = received[step][z * share : (z + 2) * share].astype(jnp.float32)
            wide[z, place_of, :] = both[:share]
            wide[z + 1, place_of, :] = both[share:]
    warped[...] = wide[...].astype(jnp.bfloat16)
    for copy in leaving:
        copy.wait()


def local_rows(velocity, template, moving, stiffness, fetch_plane, tissue):
    planes, rows, x_length = moving.shape
    slabs, subs = lax.axis_size("slab"), lax.axis_size("sub")
    total_z, total_y = planes * slabs, rows * subs
    devices = slabs * subs
    part = x_length // devices
    area = planes * rows
    share = rows // slabs
    both_axes = ("slab", "sub")
    my_slab = lax.axis_index("slab")
    my_place = my_slab * subs + lax.axis_index("sub")
    slab_id, place_id = my_slab.reshape(1), my_place.reshape(1)
    bf16, f32 = jnp.bfloat16, jnp.float32

    def shape(dims, kind=f32):
        return jax.ShapeDtypeStruct(dims, kind)

    def scatter(sends):
        return [sends[0]] + [
            lax.ppermute(sends[d], "slab", [(i, (i + d) % slabs) for i in range(slabs)])
            for d in range(1, slabs)
        ]

    def exchange(values):
        return lax.all_to_all(values, both_axes, split_axis=0, concat_axis=0, tiled=True)

    fetch, marks = fetch_plane.swapaxes(1, 2), tissue.swapaxes(1, 2)
    brick, field = pltpu.VMEM(moving.shape, bf16), pltpu.VMEM(stiffness.shape, f32)
    small = pltpu.VMEM(fetch.shape, jnp.int32)
    sends = call(
        functools.partial(send_rows_kernel, slabs),
        [shape(((2 * planes + 1) * share, x_length), bf16)] * slabs
        + [shape((planes * share, x_length), jnp.int16)] * slabs
        + [shape((4 * planes, x_length), bf16)] * slabs
        + [shape((2 * planes, x_length), bf16)] * 2,
        slab_id,
        (moving,),
        (template,),
        (fetch,),
        (stiffness,),
        (marks,),
        scratch=[
            pltpu.VMEM((3 * planes, rows, x_length), f32),
            pltpu.VMEM((rows, BLOCK), f32),
            brick,
            brick,
            small,
            field,
            small,
            pltpu.SemaphoreType.DMA((5,)),
        ],
        limit=WHOLE_VMEM_BYTES,
    )
    images, weights, edges = sends[:slabs], sends[slabs : 2 * slabs], sends[2 * slabs : 3 * slabs]
    first, last = sends[3 * slabs :]
    images = scatter(images)
    above = lax.ppermute(last, "sub", [(i, (i + 1) % subs) for i in range(subs)])
    below = lax.ppermute(first, "sub", [((i + 1) % subs, i) for i in range(subs)])
    edges = call(
        functools.partial(send_edges_kernel, slabs),
        [shape((4 * planes, x_length), bf16)] * slabs,
        slab_id,
        above,
        below,
        *edges,
    )
    edges = scatter(edges)
    weights = scatter(weights)
    images, edges, weights = lax.optimization_barrier((images, edges, weights))
    *sends, image, residual, edges = call(
        functools.partial(pick_kernel, slabs, planes),
        [shape((planes * share, x_length), bf16)] * slabs
        + [shape((total_z, share, x_length))] * 2
        + [shape((2, total_z, x_length))],
        slab_id,
        *images,
        *edges,
        flops=1 << 30,
    )
    basis_z = in_two(np.kron(real_basis(total_z), np.eye(share)))
    spectra = call(
        functools.partial(force_kernel, slabs),
        shape((devices, 3 * part, area)),
        slab_id,
        *weights,
        image,
        residual,
        edges,
        in_two(8.0 * real_basis(x_length)),
        basis_z,
        scratch=[pltpu.VMEM((3, total_z, share, x_length), f32)],
        flops=3 << 30,
    )
    spectra = exchange(spectra.astype(jnp.float16))
    spectra, sends = lax.optimization_barrier((spectra, sends))
    warped = scatter(sends)
    spectra = call(
        functools.partial(solve_kernel, subs),
        shape((devices, 3 * part, area)),
        place_id,
        spectra.astype(f32),
        basis_z,
        in_two(real_basis(total_y)),
        scratch=[pltpu.VMEM((total_z, total_y, 128), f32)],
        flops=3 << 30,
    )
    spectra, warped = lax.optimization_barrier((spectra.astype(jnp.float16), warped))
    spectra = exchange(spectra)
    return tuple(
        call(
            functools.partial(update_kernel, slabs),
            [shape(velocity.shape), shape(moving.shape, bf16)],
            slab_id,
            (velocity,),
            spectra.astype(f32),
            in_two(real_basis(x_length)),
            *warped,
            scratch=[field, pltpu.VMEM(velocity.shape, f32), pltpu.VMEM(velocity.shape, f32)]
            + [pltpu.SemaphoreType.DMA((6,))],
            flops=3 << 30,
            stays=1,
        )
    )


def local(velocity, template, moving, stiffness, fetch_plane, tissue):
    planes, rows, x_length = moving.shape
    slabs, subs = lax.axis_size("slab"), lax.axis_size("sub")
    part = x_length // (slabs * subs)
    fits = (
        planes == 8
        and rows == 8 * slabs
        and part % 8 == 0
        and 3 * part <= BLOCK
        and planes * slabs * 8 == 256
        and rows * subs == BLOCK
        and planes * (x_length // BLOCK) <= BLOCK
        and 3 <= x_length // BLOCK <= BLOCK
    )
    run = local_rows if fits else local_general
    return run(velocity, template, moving, stiffness, fetch_plane, tissue)


def solution(mesh):
    placed = (
        P(None, ("groups", "slab"), "sub", None),
        P(("groups", "slab"), "sub", None),
        P(("groups", "slab"), "sub", None),
        P(("groups", "slab"), "sub", None),
        P(("groups", "slab"), "sub", None),
        P(("groups", "slab"), "sub", None),
    )
    return jax.shard_map(
        local,
        mesh=mesh,
        in_specs=placed,
        out_specs=(P(None, ("groups", "slab"), "sub", None), P(("groups", "slab"), "sub", None)),
        check_vma=False,
    )
```

```python
import functools

import jax
import jax.numpy as jnp
import numpy as np
from jax import lax
from jax.experimental import pallas as pl
from jax.experimental.pallas import tpu as pltpu
from jax.sharding import PartitionSpec as P

BLOCK = 128


def extended(cells, sides, width):
    for axis, dim in sides:
        count = lax.axis_size(axis)
        head = lax.slice_in_dim(cells, 0, width, axis=dim)
        tail = lax.slice_in_dim(cells, cells.shape[dim] - width, cells.shape[dim], axis=dim)
        cells = jnp.concatenate(
            [
                lax.ppermute(tail, axis, [(i, (i + 1) % count) for i in range(count)]),
                cells,
                lax.ppermute(head, axis, [((i + 1) % count, i) for i in range(count)]),
            ],
            axis=dim,
        )
    return cells


def tables(length):
    wave_ids = jnp.arange(length, dtype=jnp.int32)
    phase = wave_ids[:, None] * wave_ids[None, :] % length
    angle = 2.0 * jnp.pi / length * phase.astype(jnp.float32)
    return (jnp.cos(angle), jnp.sin(angle))


def apply_along(values, matrix, axis_id):
    result = lax.dot_general(
        values,
        matrix,
        (((axis_id,), (0,)), ((), ())),
        precision=lax.Precision.HIGHEST,
        preferred_element_type=jnp.float32,
    )
    return jnp.moveaxis(result, -1, axis_id)


def forward_along(values_pair, axis_id):
    real_part, imag_part = values_pair
    cosine, sine = tables(real_part.shape[axis_id])
    return (
        apply_along(real_part, cosine, axis_id) + apply_along(imag_part, sine, axis_id),
        apply_along(imag_part, cosine, axis_id) - apply_along(real_part, sine, axis_id),
    )


def inverse_along(values_pair, axis_id):
    real_part, imag_part = values_pair
    length = real_part.shape[axis_id]
    cosine, sine = tables(length)
    scale = 1.0 / length
    return (
        (apply_along(real_part, cosine, axis_id) - apply_along(imag_part, sine, axis_id)) * scale,
        (apply_along(imag_part, cosine, axis_id) + apply_along(real_part, sine, axis_id)) * scale,
    )


def symbol_sq(length, first_id, span):
    wave_ids = first_id + jnp.arange(span, dtype=jnp.int32)
    signed = jnp.where(wave_ids < length // 2, wave_ids, wave_ids - length).astype(jnp.float32)
    wave = 2.0 * jnp.pi / length * signed
    return wave * wave


def local_general(velocity, template, moving, stiffness, fetch_plane, tissue):
    planes_dev, rows_dev, x_length = moving.shape
    blocks_x = x_length // BLOCK
    slabs = lax.axis_size("slab")
    subs = lax.axis_size("sub")
    my_slab = lax.axis_index("slab")
    my_sub = lax.axis_index("sub")
    per_dev = planes_dev * rows_dev * blocks_x
    capacity = 2 * per_dev // slabs
    source_plane = fetch_plane.reshape(-1)
    block_ids = jnp.arange(per_dev, dtype=jnp.int32)
    row_of = block_ids // blocks_x % rows_dev
    column_of = block_ids % blocks_x
    moving_rows = moving.reshape(per_dev, BLOCK)
    holder = source_plane // planes_dev
    within = (source_plane % planes_dev * rows_dev + row_of) * blocks_x + column_of
    matches = (holder[:, None] == jnp.arange(slabs, dtype=jnp.int32)[None, :]).astype(jnp.int32)
    earlier = jnp.sum((jnp.cumsum(matches, axis=0) - matches) * matches, axis=1)
    target = holder * capacity + earlier
    wanted = (
        jnp.zeros((slabs * capacity,), jnp.int32).at[target].set(within).reshape(slabs, capacity)
    )
    asked = lax.all_to_all(wanted, "slab", split_axis=0, concat_axis=0, tiled=True)
    fetched = moving_rows[asked.reshape(-1)].reshape(asked.shape + (BLOCK,))
    replies = lax.all_to_all(fetched, "slab", split_axis=0, concat_axis=0, tiled=True)
    warped_rows = replies.reshape(slabs * capacity, BLOCK)[target]
    warped = warped_rows.reshape(planes_dev, rows_dev, x_length)
    padded = extended(warped, (("slab", 0), ("sub", 1)), 1).astype(jnp.float32)
    image = padded[1:-1, 1:-1]
    grad_z = 0.5 * (padded[2:, 1:-1] - padded[:-2, 1:-1])
    grad_y = 0.5 * (padded[1:-1, 2:] - padded[1:-1, :-2])
    grad_x = 0.5 * (jnp.roll(image, -1, 2) - jnp.roll(image, 1, 2))
    residual = image - template.astype(jnp.float32)
    tissue_vox = jnp.repeat(tissue.astype(jnp.float32), BLOCK, axis=2)
    weight_field = tissue_vox * stiffness * residual
    force = jnp.stack([weight_field * grad_z, weight_field * grad_y, weight_field * grad_x])
    cos_x, sin_x = tables(x_length)
    real_part = apply_along(force, cos_x, 3)
    imag_part = -apply_along(force, sin_x, 3)
    moved = (
        lax.all_to_all(real_part, "sub", split_axis=3, concat_axis=2, tiled=True),
        lax.all_to_all(imag_part, "sub", split_axis=3, concat_axis=2, tiled=True),
    )
    moved = forward_along(moved, 2)
    moved = (
        lax.all_to_all(moved[0], "slab", split_axis=2, concat_axis=1, tiled=True),
        lax.all_to_all(moved[1], "slab", split_axis=2, concat_axis=1, tiled=True),
    )
    moved = forward_along(moved, 1)
    total_z = moved[0].shape[1]
    y_span = moved[0].shape[2]
    x_span = moved[0].shape[3]
    factor = 1.0 / (
        symbol_sq(total_z, 0, total_z)[:, None, None]
        + symbol_sq(y_span * slabs, my_slab * y_span, y_span)[None, :, None]
        + symbol_sq(x_span * subs, my_sub * x_span, x_span)[None, None, :]
        + 1.0 / 256.0
    )
    moved = (moved[0] * factor, moved[1] * factor)
    moved = inverse_along(moved, 1)
    moved = (
        lax.all_to_all(moved[0], "slab", split_axis=1, concat_axis=2, tiled=True),
        lax.all_to_all(moved[1], "slab", split_axis=1, concat_axis=2, tiled=True),
    )
    moved = inverse_along(moved, 2)
    real_part, imag_part = (
        lax.all_to_all(moved[0], "sub", split_axis=2, concat_axis=3, tiled=True),
        lax.all_to_all(moved[1], "sub", split_axis=2, concat_axis=3, tiled=True),
    )
    smoothed = (apply_along(real_part, cos_x, 3) - apply_along(imag_part, sin_x, 3)) * (
        1.0 / x_length
    )
    new_velocity = 0.5 * (velocity - smoothed)
    return (new_velocity, warped)


VMEM_BYTES = 24 * 1024 * 1024


def real_basis(length):
    index = np.arange(length)
    half = length // 2
    wave = np.where(index <= half, index, index - half)[:, None]
    angle = 2.0 * np.pi / length * (wave * index[None, :] % length)
    rows = np.where(index[:, None] <= half, np.cos(angle), np.sin(angle)) * np.sqrt(2.0 / length)
    rows[0] /= np.sqrt(2.0)
    rows[half] /= np.sqrt(2.0)
    return rows


def in_two(table):
    high = np.asarray(table, np.float32).astype(jnp.bfloat16)
    low = (np.asarray(table, np.float64) - high.astype(np.float64)).astype(jnp.bfloat16)
    return np.stack([high, low])


def split(values):
    high = values.astype(jnp.bfloat16)
    return high, (values - high.astype(jnp.float32)).astype(jnp.bfloat16)


def times(left, right, dims):
    def one(a, b):
        return lax.dot_general(a, b, (dims, ((), ())), preferred_element_type=jnp.float32)

    return one(left[0], right[0]) + (one(left[0], right[1]) + one(left[1], right[0]))


def wave_sq(index, length):
    wave = jnp.where(index <= length // 2, index, index - length // 2).astype(jnp.float32)
    wave = wave * (2.0 * np.pi / length)
    return wave * wave


def around(value, count):
    return lax.rem(value + 2 * count, count)


def call(kernel, out_shape, *arguments, scratch=(), flops=0, stays=0):
    places = [
        pl.BlockSpec(memory_space=pltpu.HBM if isinstance(a, tuple) else pltpu.SMEM if a.ndim == 1 else pltpu.VMEM)
        for a in arguments
    ]
    arguments = [a[0] if isinstance(a, tuple) else a for a in arguments]
    out_places = [
        pl.BlockSpec(memory_space=pltpu.HBM if k < stays else pltpu.VMEM)
        for k in range(len(jax.tree.leaves(out_shape)))
    ]
    nbytes = sum(a.size * a.dtype.itemsize for a in arguments + jax.tree.leaves(out_shape))
    return pl.pallas_call(
        kernel,
        out_shape=out_shape,
        in_specs=places,
        out_specs=jax.tree.unflatten(jax.tree.structure(out_shape), out_places),
        scratch_shapes=list(scratch),
        compiler_params=pltpu.CompilerParams(vmem_limit_bytes=VMEM_BYTES),
        cost_estimate=pl.CostEstimate(flops=flops, bytes_accessed=nbytes, transcendentals=0),
    )(*arguments)


def by_row(ref, rows):
    cells = jnp.concatenate([ref[z].astype(jnp.float32) for z in range(ref.shape[0])], axis=0)
    cells = jnp.concatenate([cells, jnp.zeros((cells.shape[0], BLOCK - rows), jnp.float32)], axis=1)
    cells = jnp.concatenate([cells, jnp.zeros((BLOCK - cells.shape[0], BLOCK), jnp.float32)], axis=0)
    return cells.T[:rows]


def send_columns_kernel(slabs, place, moving, fetch, *sends):
    planes, rows, _ = moving.shape
    for step, send in enumerate(sends):
        to = around(place[0] + step, slabs)
        send[0:planes] = moving[:, :, pl.ds(pl.multiple_of(to * BLOCK, BLOCK), BLOCK)]
        wanted = jnp.concatenate([fetch[z, pl.ds(to, 1), :] for z in range(planes)], axis=0).astype(jnp.float32)
        wanted = jnp.concatenate([wanted, jnp.zeros((planes, BLOCK - rows), jnp.float32)], axis=1)
        wanted = jnp.concatenate([wanted, jnp.zeros((BLOCK - planes, BLOCK), jnp.float32)], axis=0)
        send[planes] = wanted.T[:rows].astype(jnp.bfloat16)


def pick_kernel(slabs, place, *refs):
    received, sends, picked = refs[:slabs], refs[slabs:-1], refs[-1]
    planes = received[0].shape[0] - 1
    rows = received[0].shape[1]
    me = place[0]
    total = slabs * planes
    group = 4
    for step in range(slabs):
        first = around(me - step, slabs) * planes
        names = received[step][planes].astype(jnp.float32)
        for start in range(0, planes, group):
            wanted = [
                jnp.broadcast_to(names[:, z : z + 1], (rows, BLOCK)) for z in range(start, start + group)
            ]
            found = [jnp.zeros((rows, BLOCK), jnp.float32) for _ in range(group)]
            for other in range(slabs):
                base = (around(me - other, slabs) * planes).astype(jnp.float32)
                for plane in range(planes):
                    values = received[other][plane].astype(jnp.float32)
                    found = [
                        jnp.where(w == base + float(plane), values, f) for w, f in zip(wanted, found)
                    ]
            for z in range(group):
                picked[first + start + z] = found[z].astype(jnp.bfloat16)
    for step, send in enumerate(sends):
        first = around(me + step, slabs) * planes
        for k in range(planes + 2):
            send[k] = picked[around(first + (k - 1), total)]


def edge_rows_kernel(slabs, *refs):
    received, (first, last) = refs[1 : 1 + slabs], refs[1 + slabs :]
    planes, rows, _ = received[0].shape
    for d in range(slabs):
        cells = [received[d][z].astype(jnp.float32) for z in range(1, planes - 1)]
        first[d] = jnp.concatenate([c[0:1] for c in cells], axis=0).astype(jnp.bfloat16)
        last[d] = jnp.concatenate([c[rows - 1 : rows] for c in cells], axis=0).astype(jnp.bfloat16)


def force_z_kernel(slabs, subs, place, *refs):
    received, refs = refs[:slabs], refs[slabs:]
    template, stiffness, tissue, basis, warped, image, weight, spectra, planes_of, wide = refs
    planes, rows, x_length = template.shape
    blocks = x_length // BLOCK
    for step in range(slabs):
        block = pl.ds(pl.multiple_of(around(place[0] - step, slabs) * BLOCK, BLOCK), BLOCK)
        planes_of[:, :, block] = received[step][...].astype(jnp.float32)
        warped[:, :, block] = received[step][1:-1]
    marks = by_row(tissue, rows)
    force = []
    for z in range(planes):
        here = planes_of[z + 1]
        marked = jnp.concatenate(
            [
                jnp.broadcast_to(marks[:, z * blocks + b : z * blocks + b + 1], (rows, BLOCK))
                for b in range(blocks)
            ],
            axis=1,
        )
        own = 0.5 * (marked * stiffness[z] * (here - template[z].astype(jnp.float32)))
        image[z] = here
        weight[z] = own
        force.append(own * (planes_of[z + 2] - planes_of[z]))
    force = split(jnp.concatenate(force, axis=0))
    wide[...] = times((basis[0], basis[1]), force, ((1,), (1,)))
    part = x_length // (slabs * subs)
    for d in range(slabs):
        for e in range(subs):
            first = (around(place[0] + d, slabs) * subs + around(place[1] + e, subs)) * part
            spectra[d, e] = wide[pl.ds(pl.multiple_of(first, part), part), :]


def force_xy_kernel(slabs, place, above, below, image, weight, basis, spectra, edges):
    planes, rows, x_length = image.shape
    for step in range(slabs):
        block = pl.ds(pl.multiple_of(around(place[0] - step, slabs) * BLOCK, BLOCK), BLOCK)
        edges[0, :, block] = above[step].astype(jnp.float32)
        edges[1, :, block] = below[step].astype(jnp.float32)
    row = lax.broadcasted_iota(jnp.int32, (rows, x_length), 0)
    forces = [[], []]
    for z in range(planes):
        here, own = image[z], weight[z]
        before = jnp.where(row == 0, edges[0, z : z + 1, :], pltpu.roll(here, 1, 0))
        after = jnp.where(row == rows - 1, edges[1, z : z + 1, :], pltpu.roll(here, rows - 1, 0))
        forces[0].append(own * (after - before))
        forces[1].append(own * (pltpu.roll(here, x_length - 1, 1) - pltpu.roll(here, 1, 1)))
    devices, part = spectra.shape[:2]
    part //= 2
    for a in range(2):
        force = split(jnp.concatenate(forces[a], axis=0))
        spectrum = times((basis[0], basis[1]), force, ((1,), (1,)))
        spectra[:, a * part : (a + 1) * part, :] = spectrum.reshape(devices, part, planes * rows)


def solve(first, x_length, part, subs, spectra, basis_z, basis_y, cells):
    devices, used, area = spectra.shape
    total_z, _, total_y = cells.shape
    slabs = devices // subs
    planes, rows = total_z // slabs, total_y // subs
    tile = 8

    def along_y(k):
        high, low = basis_y[2 * k], basis_y[2 * k + 1]
        both = jnp.concatenate([high, high], axis=0)

        def run(values):
            parts = split(values)
            sums = jnp.dot(jnp.concatenate(parts, axis=1), both, preferred_element_type=jnp.float32)
            return sums + jnp.dot(parts[0], low, preferred_element_type=jnp.float32)

        return run

    run = along_y(0)
    for s in range(slabs):
        own = []
        for z in range(planes):
            lanes = slice(z * rows, (z + 1) * rows)
            own.append(jnp.concatenate([spectra[s * subs + q][:, lanes] for q in range(subs)], axis=1))
        own = run(jnp.concatenate(own, axis=0))
        cells[s * planes : (s + 1) * planes] = own.reshape(planes, used, total_y)
    index = lax.broadcasted_iota(jnp.int32, (total_z * tile, 1), 0)
    z_sq = wave_sq(index // tile, total_z)
    y_sq = wave_sq(lax.broadcasted_iota(jnp.int32, (1, total_y), 1), total_y)
    table = (basis_z[0], basis_z[1])
    for g in range(0, used, 2 * tile):
        own, scale = [], []
        for start in (g, g + tile):
            own.append(cells[:, start : start + tile, :].reshape(total_z * tile, total_y))
            x_sq = wave_sq(first + start % part + lax.rem(index, tile), x_length)
            scale.append((z_sq + x_sq + y_sq) * 256.0 + 1.0)
        own = times(table, split(jnp.concatenate(own, axis=1)), ((1,), (0,)))
        own = own / jnp.concatenate(scale, axis=1)
        own = times(table, split(own), ((0,), (0,)))
        for k, start in enumerate((g, g + tile)):
            half = own[:, k * total_y : (k + 1) * total_y]
            cells[:, start : start + tile, :] = half.reshape(total_z, tile, total_y)
    run = along_y(1)
    for s in range(slabs):
        own = run(cells[s * planes : (s + 1) * planes].reshape(planes * used, total_y))
        for q in range(subs):
            lanes = slice(q * rows, (q + 1) * rows)
            spectra[s * subs + q] = jnp.concatenate(
                [own[z * used : (z + 1) * used, lanes] for z in range(planes)], axis=1
            )


def solve_xy_kernel(subs, x_length, place, spectra, basis_z, basis_y, out, cells):
    devices = out.shape[0]
    part = x_length // devices
    out[...] = spectra[...]
    solve((place[0] * subs + place[1]) * part, x_length, part, subs, out, basis_z, basis_y, cells)


def solve_z_kernel(slabs, subs, x_length, place, *refs):
    received, refs = refs[:subs], refs[subs:]
    basis_z, basis_y, sends, (spectra, cells) = refs[0], refs[1], refs[2 : 2 + slabs], refs[2 + slabs :]
    part = x_length // (slabs * subs)
    for e in range(subs):
        for d in range(slabs):
            spectra[around(place[0] - d, slabs) * subs + around(place[1] - e, subs)] = received[e][d]
    solve((place[0] * subs + place[1]) * part, x_length, part, subs, spectra, basis_z, basis_y, cells)
    for d in range(slabs):
        for e in range(subs):
            sends[d][e] = spectra[around(place[0] + d, slabs) * subs + around(place[1] + e, subs)]


def moved(spectra, velocity, basis):
    smoothed = times(split(spectra.T), (basis[0], basis[1]), ((1,), (0,)))
    return 0.5 * (velocity - 32.0 * smoothed.reshape(velocity.shape))


def update_z_kernel(slabs, subs, place, basis, velocity_in, *refs):
    received, (out, gathered, velocity, done) = refs[:subs], refs[subs:]
    part = received[0].shape[1]
    arriving = pltpu.make_async_copy(velocity_in.at[0], velocity, done.at[0])
    arriving.start()
    for e in range(subs):
        for d in range(slabs):
            first = (around(place[0] - d, slabs) * subs + around(place[1] - e, subs)) * part
            gathered[pl.ds(pl.multiple_of(first, part), part), :] = received[e][d]
    arriving.wait()
    out[...] = moved(gathered[...], velocity[...], basis)


def update_kernel(place, velocity_in, spectra, basis, updated, out, velocity, result, done):
    devices, part, area = spectra.shape
    part //= 2
    arriving = [pltpu.make_async_copy(velocity_in.at[a], velocity.at[a - 1], done.at[a]) for a in (1, 2)]
    leaving = [pltpu.make_async_copy(result.at[a - 1], out.at[a], done.at[2 + a]) for a in (1, 2)]
    leaving.append(pltpu.make_async_copy(updated, out.at[0], done.at[0]))
    leaving[2].start()
    for copy in arriving:
        copy.start()
    for a in range(2):
        own = spectra[:, a * part : (a + 1) * part, :].reshape(devices * part, area)
        arriving[a].wait()
        result[a] = moved(own, velocity[a], basis)
        leaving[a].start()
    for copy in leaving:
        copy.wait()


def local_blocks(velocity, template, moving, stiffness, fetch_plane, tissue):
    planes, rows, x_length = moving.shape
    slabs, subs = lax.axis_size("slab"), lax.axis_size("sub")
    total_z, total_y = planes * slabs, rows * subs
    devices = slabs * subs
    part = x_length // devices
    area = planes * rows
    place = jnp.stack([lax.axis_index("slab"), lax.axis_index("sub")])
    bf16, f16, f32 = jnp.bfloat16, jnp.float16, jnp.float32

    def shape(dims, kind=f32):
        return jax.ShapeDtypeStruct(dims, kind)

    def scatter(sends, axis):
        count = lax.axis_size(axis)
        return [sends[0]] + [
            lax.ppermute(sends[d], axis, [(i, (i + d) % count) for i in range(count)]) for d in range(1, count)
        ]

    def exchange(values):
        return lax.all_to_all(values, ("slab", "sub"), split_axis=0, concat_axis=0, tiled=True)

    fetch, marks = fetch_plane.swapaxes(1, 2), tissue.swapaxes(1, 2)
    sends = call(
        functools.partial(send_columns_kernel, slabs),
        [shape((planes + 1, rows, BLOCK), bf16)] * slabs,
        place,
        moving,
        fetch,
    )
    sends = call(
        functools.partial(pick_kernel, slabs),
        [shape((planes + 2, rows, BLOCK), bf16)] * slabs,
        place,
        *scatter(sends, "slab"),
        scratch=[pltpu.VMEM((total_z, rows, BLOCK), bf16)],
        flops=1 << 30,
    )
    received = scatter(sends, "slab")
    first, last = call(
        functools.partial(edge_rows_kernel, slabs),
        [shape((slabs, planes, BLOCK), bf16)] * 2,
        place,
        *received,
    )
    above = lax.ppermute(last, "sub", [(i, (i + 1) % subs) for i in range(subs)])
    below = lax.ppermute(first, "sub", [((i + 1) % subs, i) for i in range(subs)])
    basis_x = in_two(8.0 * real_basis(x_length))
    basis_z = in_two(np.kron(real_basis(total_z), np.eye(8)))
    basis_y = np.concatenate([in_two(real_basis(total_y).T), in_two(real_basis(total_y))])
    warped, image, weight, spectra_z = call(
        functools.partial(force_z_kernel, slabs, subs),
        [
            shape(moving.shape, bf16),
            shape(moving.shape),
            shape(moving.shape),
            shape((slabs, subs, part, area)),
        ],
        place,
        *received,
        template,
        stiffness,
        marks,
        basis_x,
        scratch=[pltpu.VMEM((planes + 2, rows, x_length), f32), pltpu.VMEM((x_length, area), f32)],
        flops=2 << 30,
    )
    spectra_z = spectra_z.astype(f16)
    spectra_z = scatter([spectra_z[d] for d in range(slabs)], "slab")
    spectra_z = scatter([jnp.stack([r[e] for r in spectra_z]) for e in range(subs)], "sub")
    spectra_xy = call(
        functools.partial(force_xy_kernel, slabs),
        shape((devices, 2 * part, area)),
        place,
        above,
        below,
        image,
        weight,
        basis_x,
        scratch=[pltpu.VMEM((2, planes, x_length), f32)],
        flops=3 << 30,
    )
    spectra_xy = exchange(spectra_xy.astype(f16))
    spectra_z = call(
        functools.partial(solve_z_kernel, slabs, subs, x_length),
        [shape((subs, part, area))] * slabs,
        place,
        *[r.astype(f32) for r in spectra_z],
        basis_z,
        basis_y,
        scratch=[pltpu.VMEM((devices, part, area), f32), pltpu.VMEM((total_z, part, total_y), f32)],
        flops=2 << 30,
    )
    _, spectra_xy = lax.optimization_barrier((spectra_z, spectra_xy))
    spectra_z = scatter([r.astype(f16) for r in spectra_z], "slab")
    spectra_z = scatter([jnp.stack([r[e] for r in spectra_z]) for e in range(subs)], "sub")
    spectra_xy = call(
        functools.partial(solve_xy_kernel, subs, x_length),
        shape((devices, 2 * part, area)),
        place,
        spectra_xy.astype(f32),
        basis_z,
        basis_y,
        scratch=[pltpu.VMEM((total_z, 2 * part, total_y), f32)],
        flops=3 << 30,
    )
    spectra_xy = exchange(spectra_xy.astype(f16))
    basis_x = in_two(real_basis(x_length))
    updated = call(
        functools.partial(update_z_kernel, slabs, subs),
        shape(moving.shape),
        place,
        basis_x,
        (velocity,),
        *[r.astype(f32) for r in spectra_z],
        scratch=[
            pltpu.VMEM((x_length, area), f32),
            pltpu.VMEM(moving.shape, f32),
            pltpu.SemaphoreType.DMA((1,)),
        ],
        flops=1 << 30,
    )
    new_velocity = call(
        update_kernel,
        shape(velocity.shape),
        place,
        (velocity,),
        spectra_xy.astype(f32),
        basis_x,
        updated,
        scratch=[
            pltpu.VMEM((2,) + moving.shape, f32),
            pltpu.VMEM((2,) + moving.shape, f32),
            pltpu.SemaphoreType.DMA((5,)),
        ],
        flops=2 << 30,
        stays=1,
    )
    return (new_velocity, warped)


def local(velocity, template, moving, stiffness, fetch_plane, tissue):
    planes, rows, x_length = moving.shape
    slabs, subs = lax.axis_size("slab"), lax.axis_size("sub")
    fits = (
        x_length == slabs * BLOCK
        and planes == 8
        and planes * slabs * 8 == 256
        and rows % 16 == 0
        and rows * subs == BLOCK
        and x_length % (16 * slabs * subs) == 0
    )
    run = local_blocks if fits else local_general
    return run(velocity, template, moving, stiffness, fetch_plane, tissue)


def solution(mesh):
    placed = (
        P(None, ("groups", "slab"), "sub", None),
        P(("groups", "slab"), "sub", None),
        P(("groups", "slab"), "sub", None),
        P(("groups", "slab"), "sub", None),
        P(("groups", "slab"), "sub", None),
        P(("groups", "slab"), "sub", None),
    )
    return jax.shard_map(
        local,
        mesh=mesh,
        in_specs=placed,
        out_specs=(P(None, ("groups", "slab"), "sub", None), P(("groups", "slab"), "sub", None)),
        check_vma=False,
    )
```

```python
import functools

import jax
import jax.numpy as jnp
import numpy as np
from jax import lax
from jax.experimental import pallas as pl
from jax.experimental.pallas import tpu as pltpu
from jax.sharding import PartitionSpec as P

BLOCK = 128


def extended(cells, sides, width):
    for axis, dim in sides:
        count = lax.axis_size(axis)
        head = lax.slice_in_dim(cells, 0, width, axis=dim)
        tail = lax.slice_in_dim(cells, cells.shape[dim] - width, cells.shape[dim], axis=dim)
        cells = jnp.concatenate(
            [
                lax.ppermute(tail, axis, [(i, (i + 1) % count) for i in range(count)]),
                cells,
                lax.ppermute(head, axis, [((i + 1) % count, i) for i in range(count)]),
            ],
            axis=dim,
        )
    return cells


def tables(length):
    wave_ids = jnp.arange(length, dtype=jnp.int32)
    phase = wave_ids[:, None] * wave_ids[None, :] % length
    angle = 2.0 * jnp.pi / length * phase.astype(jnp.float32)
    return (jnp.cos(angle), jnp.sin(angle))


def apply_along(values, matrix, axis_id):
    result = lax.dot_general(
        values,
        matrix,
        (((axis_id,), (0,)), ((), ())),
        precision=lax.Precision.HIGHEST,
        preferred_element_type=jnp.float32,
    )
    return jnp.moveaxis(result, -1, axis_id)


def forward_along(values_pair, axis_id):
    real_part, imag_part = values_pair
    cosine, sine = tables(real_part.shape[axis_id])
    return (
        apply_along(real_part, cosine, axis_id) + apply_along(imag_part, sine, axis_id),
        apply_along(imag_part, cosine, axis_id) - apply_along(real_part, sine, axis_id),
    )


def inverse_along(values_pair, axis_id):
    real_part, imag_part = values_pair
    length = real_part.shape[axis_id]
    cosine, sine = tables(length)
    scale = 1.0 / length
    return (
        (apply_along(real_part, cosine, axis_id) - apply_along(imag_part, sine, axis_id)) * scale,
        (apply_along(imag_part, cosine, axis_id) + apply_along(real_part, sine, axis_id)) * scale,
    )


def symbol_sq(length, first_id, span):
    wave_ids = first_id + jnp.arange(span, dtype=jnp.int32)
    signed = jnp.where(wave_ids < length // 2, wave_ids, wave_ids - length).astype(jnp.float32)
    wave = 2.0 * jnp.pi / length * signed
    return wave * wave


def local_general(velocity, template, moving, stiffness, fetch_plane, tissue):
    planes_dev, rows_dev, x_length = moving.shape
    blocks_x = x_length // BLOCK
    slabs = lax.axis_size("slab")
    subs = lax.axis_size("sub")
    my_slab = lax.axis_index("slab")
    my_sub = lax.axis_index("sub")
    per_dev = planes_dev * rows_dev * blocks_x
    capacity = 2 * per_dev // slabs
    source_plane = fetch_plane.reshape(-1)
    block_ids = jnp.arange(per_dev, dtype=jnp.int32)
    row_of = block_ids // blocks_x % rows_dev
    column_of = block_ids % blocks_x
    moving_rows = moving.reshape(per_dev, BLOCK)
    holder = source_plane // planes_dev
    within = (source_plane % planes_dev * rows_dev + row_of) * blocks_x + column_of
    matches = (holder[:, None] == jnp.arange(slabs, dtype=jnp.int32)[None, :]).astype(jnp.int32)
    earlier = jnp.sum((jnp.cumsum(matches, axis=0) - matches) * matches, axis=1)
    target = holder * capacity + earlier
    wanted = (
        jnp.zeros((slabs * capacity,), jnp.int32).at[target].set(within).reshape(slabs, capacity)
    )
    asked = lax.all_to_all(wanted, "slab", split_axis=0, concat_axis=0, tiled=True)
    fetched = moving_rows[asked.reshape(-1)].reshape(asked.shape + (BLOCK,))
    replies = lax.all_to_all(fetched, "slab", split_axis=0, concat_axis=0, tiled=True)
    warped_rows = replies.reshape(slabs * capacity, BLOCK)[target]
    warped = warped_rows.reshape(planes_dev, rows_dev, x_length)
    padded = extended(warped, (("slab", 0), ("sub", 1)), 1).astype(jnp.float32)
    image = padded[1:-1, 1:-1]
    grad_z = 0.5 * (padded[2:, 1:-1] - padded[:-2, 1:-1])
    grad_y = 0.5 * (padded[1:-1, 2:] - padded[1:-1, :-2])
    grad_x = 0.5 * (jnp.roll(image, -1, 2) - jnp.roll(image, 1, 2))
    residual = image - template.astype(jnp.float32)
    tissue_vox = jnp.repeat(tissue.astype(jnp.float32), BLOCK, axis=2)
    weight_field = tissue_vox * stiffness * residual
    force = jnp.stack([weight_field * grad_z, weight_field * grad_y, weight_field * grad_x])
    cos_x, sin_x = tables(x_length)
    real_part = apply_along(force, cos_x, 3)
    imag_part = -apply_along(force, sin_x, 3)
    moved = (
        lax.all_to_all(real_part, "sub", split_axis=3, concat_axis=2, tiled=True),
        lax.all_to_all(imag_part, "sub", split_axis=3, concat_axis=2, tiled=True),
    )
    moved = forward_along(moved, 2)
    moved = (
        lax.all_to_all(moved[0], "slab", split_axis=2, concat_axis=1, tiled=True),
        lax.all_to_all(moved[1], "slab", split_axis=2, concat_axis=1, tiled=True),
    )
    moved = forward_along(moved, 1)
    total_z = moved[0].shape[1]
    y_span = moved[0].shape[2]
    x_span = moved[0].shape[3]
    factor = 1.0 / (
        symbol_sq(total_z, 0, total_z)[:, None, None]
        + symbol_sq(y_span * slabs, my_slab * y_span, y_span)[None, :, None]
        + symbol_sq(x_span * subs, my_sub * x_span, x_span)[None, None, :]
        + 1.0 / 256.0
    )
    moved = (moved[0] * factor, moved[1] * factor)
    moved = inverse_along(moved, 1)
    moved = (
        lax.all_to_all(moved[0], "slab", split_axis=1, concat_axis=2, tiled=True),
        lax.all_to_all(moved[1], "slab", split_axis=1, concat_axis=2, tiled=True),
    )
    moved = inverse_along(moved, 2)
    real_part, imag_part = (
        lax.all_to_all(moved[0], "sub", split_axis=2, concat_axis=3, tiled=True),
        lax.all_to_all(moved[1], "sub", split_axis=2, concat_axis=3, tiled=True),
    )
    smoothed = (apply_along(real_part, cos_x, 3) - apply_along(imag_part, sin_x, 3)) * (
        1.0 / x_length
    )
    new_velocity = 0.5 * (velocity - smoothed)
    return (new_velocity, warped)


VMEM_BYTES = 24 * 1024 * 1024


def real_basis(length):
    index = np.arange(length)
    half = length // 2
    wave = np.where(index <= half, index, index - half)[:, None]
    angle = 2.0 * np.pi / length * (wave * index[None, :] % length)
    rows = np.where(index[:, None] <= half, np.cos(angle), np.sin(angle)) * np.sqrt(2.0 / length)
    rows[0] /= np.sqrt(2.0)
    rows[half] /= np.sqrt(2.0)
    return rows


def in_two(table):
    high = np.asarray(table, np.float32).astype(jnp.bfloat16)
    low = (np.asarray(table, np.float64) - high.astype(np.float64)).astype(jnp.bfloat16)
    return np.stack([high, low])


def split(values):
    high = values.astype(jnp.bfloat16)
    return high, (values - high.astype(jnp.float32)).astype(jnp.bfloat16)


def times(left, right, dims):
    def one(a, b):
        return lax.dot_general(a, b, (dims, ((), ())), preferred_element_type=jnp.float32)

    return one(left[0], right[0]) + (one(left[0], right[1]) + one(left[1], right[0]))


def wave_sq(index, length):
    wave = jnp.where(index <= length // 2, index, index - length // 2).astype(jnp.float32)
    wave = wave * (2.0 * np.pi / length)
    return wave * wave


def around(value, count):
    return lax.rem(value + 2 * count, count)


def call(kernel, out_shape, *arguments, scratch=(), flops=0, stays=0):
    places = [
        pl.BlockSpec(memory_space=pltpu.HBM if isinstance(a, tuple) else pltpu.SMEM if a.ndim == 1 else pltpu.VMEM)
        for a in arguments
    ]
    arguments = [a[0] if isinstance(a, tuple) else a for a in arguments]
    out_places = [
        pl.BlockSpec(memory_space=pltpu.HBM if k < stays else pltpu.VMEM)
        for k in range(len(jax.tree.leaves(out_shape)))
    ]
    nbytes = sum(a.size * a.dtype.itemsize for a in arguments + jax.tree.leaves(out_shape))
    return pl.pallas_call(
        kernel,
        out_shape=out_shape,
        in_specs=places,
        out_specs=jax.tree.unflatten(jax.tree.structure(out_shape), out_places),
        scratch_shapes=list(scratch),
        compiler_params=pltpu.CompilerParams(vmem_limit_bytes=VMEM_BYTES),
        cost_estimate=pl.CostEstimate(flops=flops, bytes_accessed=nbytes, transcendentals=0),
    )(*arguments)


def by_row(ref, rows):
    cells = jnp.concatenate([ref[z].astype(jnp.float32) for z in range(ref.shape[0])], axis=0)
    cells = jnp.concatenate([cells, jnp.zeros((cells.shape[0], BLOCK - rows), jnp.float32)], axis=1)
    cells = jnp.concatenate([cells, jnp.zeros((BLOCK - cells.shape[0], BLOCK), jnp.float32)], axis=0)
    return cells.T[:rows]


def send_columns_kernel(slabs, place, moving, fetch, *sends):
    planes, rows, _ = moving.shape
    for step, send in enumerate(sends):
        to = around(place[0] + step, slabs)
        send[0:planes] = moving[:, :, pl.ds(pl.multiple_of(to * BLOCK, BLOCK), BLOCK)]
        wanted = jnp.concatenate([fetch[z, pl.ds(to, 1), :] for z in range(planes)], axis=0).astype(jnp.float32)
        wanted = jnp.concatenate([wanted, jnp.zeros((planes, BLOCK - rows), jnp.float32)], axis=1)
        wanted = jnp.concatenate([wanted, jnp.zeros((BLOCK - planes, BLOCK), jnp.float32)], axis=0)
        send[planes] = wanted.T[:rows].astype(jnp.bfloat16)


def pick_kernel(slabs, place, *refs):
    received, sends, picked = refs[:slabs], refs[slabs:-1], refs[-1]
    planes = received[0].shape[0] - 1
    rows = received[0].shape[1]
    me = place[0]
    total = slabs * planes
    group = 4
    for step in range(slabs):
        first = around(me - step, slabs) * planes
        names = received[step][planes].astype(jnp.float32)
        for start in range(0, planes, group):
            wanted = [
                jnp.broadcast_to(names[:, z : z + 1], (rows, BLOCK)) for z in range(start, start + group)
            ]
            found = [jnp.zeros((rows, BLOCK), jnp.float32) for _ in range(group)]
            for other in range(slabs):
                base = (around(me - other, slabs) * planes).astype(jnp.float32)
                for plane in range(planes):
                    values = received[other][plane].astype(jnp.float32)
                    found = [
                        jnp.where(w == base + float(plane), values, f) for w, f in zip(wanted, found)
                    ]
            for z in range(group):
                picked[first + start + z] = found[z].astype(jnp.bfloat16)
    for step, send in enumerate(sends):
        first = around(me + step, slabs) * planes
        for k in range(planes + 2):
            send[k] = picked[around(first + (k - 1), total)]


def edge_rows_kernel(slabs, *refs):
    received, (first, last) = refs[1 : 1 + slabs], refs[1 + slabs :]
    planes, rows, _ = received[0].shape
    for d in range(slabs):
        cells = [received[d][z].astype(jnp.float32) for z in range(1, planes - 1)]
        first[d] = jnp.concatenate([c[0:1] for c in cells], axis=0).astype(jnp.bfloat16)
        last[d] = jnp.concatenate([c[rows - 1 : rows] for c in cells], axis=0).astype(jnp.bfloat16)


def force_zx_kernel(slabs, subs, place, *refs):
    received, refs = refs[:slabs], refs[slabs:]
    template, stiffness, tissue, basis, warped, image, weight, spectra, kept, planes_of, wide = refs
    planes, rows, x_length = template.shape
    blocks = x_length // BLOCK
    for step in range(slabs):
        block = pl.ds(pl.multiple_of(around(place[0] - step, slabs) * BLOCK, BLOCK), BLOCK)
        planes_of[:, :, block] = received[step][...].astype(jnp.float32)
        warped[:, :, block] = received[step][1:-1]
    marks = by_row(tissue, rows)
    forces = [[], []]
    for z in range(planes):
        here = planes_of[z + 1]
        marked = jnp.concatenate(
            [
                jnp.broadcast_to(marks[:, z * blocks + b : z * blocks + b + 1], (rows, BLOCK))
                for b in range(blocks)
            ],
            axis=1,
        )
        own = 0.5 * (marked * stiffness[z] * (here - template[z].astype(jnp.float32)))
        image[z] = here
        weight[z] = own
        forces[0].append(own * (planes_of[z + 2] - planes_of[z]))
        forces[1].append(own * (pltpu.roll(here, x_length - 1, 1) - pltpu.roll(here, 1, 1)))
    for a in range(2):
        force = split(jnp.concatenate(forces[a], axis=0))
        wide[a] = times((basis[0], basis[1]), force, ((1,), (1,)))
    part = x_length // (slabs * subs)
    half = part // 2
    for d in range(slabs):
        for e in range(subs):
            first = (around(place[0] + d, slabs) * subs + around(place[1] + e, subs)) * part
            spectra[d, e, :part] = wide[0, pl.ds(pl.multiple_of(first, part), part), :]
            spectra[d, e, part:] = wide[1, pl.ds(pl.multiple_of(first + half, half), half), :]
    for k in range(slabs * subs):
        kept[k] = wide[1, k * part : k * part + half, :]


def force_y_kernel(slabs, place, above, below, image, weight, basis, kept, spectra, edges):
    planes, rows, x_length = image.shape
    for step in range(slabs):
        block = pl.ds(pl.multiple_of(around(place[0] - step, slabs) * BLOCK, BLOCK), BLOCK)
        edges[0, :, block] = above[step].astype(jnp.float32)
        edges[1, :, block] = below[step].astype(jnp.float32)
    row = lax.broadcasted_iota(jnp.int32, (rows, x_length), 0)
    force = []
    for z in range(planes):
        here = image[z]
        before = jnp.where(row == 0, edges[0, z : z + 1, :], pltpu.roll(here, 1, 0))
        after = jnp.where(row == rows - 1, edges[1, z : z + 1, :], pltpu.roll(here, rows - 1, 0))
        force.append(weight[z] * (after - before))
    devices = spectra.shape[0]
    part = x_length // devices
    spectrum = times((basis[0], basis[1]), split(jnp.concatenate(force, axis=0)), ((1,), (1,)))
    spectra[:, :part, :] = spectrum.reshape(devices, part, planes * rows)
    spectra[:, part:, :] = kept[...]


def solve(first, x_length, offsets, subs, spectra, basis_z, basis_y, cells):
    devices, used, area = spectra.shape
    total_z, _, total_y = cells.shape
    slabs = devices // subs
    planes, rows = total_z // slabs, total_y // subs
    tile = 8

    def along_y(k):
        high, low = basis_y[2 * k], basis_y[2 * k + 1]
        both = jnp.concatenate([high, high], axis=0)

        def run(values):
            parts = split(values)
            sums = jnp.dot(jnp.concatenate(parts, axis=1), both, preferred_element_type=jnp.float32)
            return sums + jnp.dot(parts[0], low, preferred_element_type=jnp.float32)

        return run

    run = along_y(0)
    for s in range(slabs):
        own = []
        for z in range(planes):
            lanes = slice(z * rows, (z + 1) * rows)
            own.append(jnp.concatenate([spectra[s * subs + q][:, lanes] for q in range(subs)], axis=1))
        own = run(jnp.concatenate(own, axis=0))
        cells[s * planes : (s + 1) * planes] = own.reshape(planes, used, total_y)
    index = lax.broadcasted_iota(jnp.int32, (total_z * tile, 1), 0)
    z_sq = wave_sq(index // tile, total_z)
    y_sq = wave_sq(lax.broadcasted_iota(jnp.int32, (1, total_y), 1), total_y)
    table = (basis_z[0], basis_z[1])
    for g in range(0, used, 2 * tile):
        own, scale = [], []
        for start in (g, g + tile):
            own.append(cells[:, start : start + tile, :].reshape(total_z * tile, total_y))
            x_sq = wave_sq(first + offsets[start // tile] + lax.rem(index, tile), x_length)
            scale.append((z_sq + x_sq + y_sq) * 256.0 + 1.0)
        own = times(table, split(jnp.concatenate(own, axis=1)), ((1,), (0,)))
        own = own / jnp.concatenate(scale, axis=1)
        own = times(table, split(own), ((0,), (0,)))
        for k, start in enumerate((g, g + tile)):
            half = own[:, k * total_y : (k + 1) * total_y]
            cells[:, start : start + tile, :] = half.reshape(total_z, tile, total_y)
    run = along_y(1)
    for s in range(slabs):
        own = run(cells[s * planes : (s + 1) * planes].reshape(planes * used, total_y))
        for q in range(subs):
            lanes = slice(q * rows, (q + 1) * rows)
            spectra[s * subs + q] = jnp.concatenate(
                [own[z * used : (z + 1) * used, lanes] for z in range(planes)], axis=1
            )


def solve_yx_kernel(subs, x_length, place, spectra, basis_z, basis_y, out, cells):
    devices = out.shape[0]
    part = x_length // devices
    offsets = list(range(0, part, 8)) + list(range(0, part // 2, 8))
    out[...] = spectra[...]
    solve((place[0] * subs + place[1]) * part, x_length, offsets, subs, out, basis_z, basis_y, cells)


def solve_zx_kernel(slabs, subs, x_length, place, *refs):
    received, refs = refs[:subs], refs[subs:]
    basis_z, basis_y, sends, (spectra, cells) = refs[0], refs[1], refs[2 : 2 + slabs], refs[2 + slabs :]
    part = x_length // (slabs * subs)
    offsets = list(range(0, part, 8)) + list(range(part // 2, part, 8))
    for e in range(subs):
        for d in range(slabs):
            spectra[around(place[0] - d, slabs) * subs + around(place[1] - e, subs)] = received[e][d]
    solve((place[0] * subs + place[1]) * part, x_length, offsets, subs, spectra, basis_z, basis_y, cells)
    for d in range(slabs):
        for e in range(subs):
            sends[d][e] = spectra[around(place[0] + d, slabs) * subs + around(place[1] + e, subs)]


def moved(spectra, velocity, basis):
    smoothed = times(split(spectra.T), (basis[0], basis[1]), ((1,), (0,)))
    return 0.5 * (velocity - 32.0 * smoothed.reshape(velocity.shape))


def update_z_kernel(slabs, subs, place, basis, velocity_in, *refs):
    received, (out, kept, gathered, velocity, done) = refs[:subs], refs[subs:]
    half = kept.shape[1]
    part = 2 * half
    arriving = pltpu.make_async_copy(velocity_in.at[0], velocity, done.at[0])
    arriving.start()
    for e in range(subs):
        for d in range(slabs):
            index = around(place[0] - d, slabs) * subs + around(place[1] - e, subs)
            gathered[pl.ds(pl.multiple_of(index * part, part), part), :] = received[e][d, :part]
            kept[index] = received[e][d, part:]
    arriving.wait()
    out[...] = moved(gathered[...], velocity[...], basis)


def update_kernel(place, velocity_in, spectra, basis, updated, kept, out, velocity, result, done):
    devices, half, area = kept.shape
    part = 2 * half
    arriving = [pltpu.make_async_copy(velocity_in.at[a], velocity.at[a - 1], done.at[a]) for a in (1, 2)]
    leaving = [pltpu.make_async_copy(result.at[a - 1], out.at[a], done.at[2 + a]) for a in (1, 2)]
    leaving.append(pltpu.make_async_copy(updated, out.at[0], done.at[0]))
    leaving[2].start()
    for copy in arriving:
        copy.start()
    for a in range(2):
        if a:
            own = jnp.concatenate([spectra[:, part:, :], kept[...]], axis=1)
        else:
            own = spectra[:, :part, :]
        own = own.reshape(devices * part, area)
        arriving[a].wait()
        result[a] = moved(own, velocity[a], basis)
        leaving[a].start()
    for copy in leaving:
        copy.wait()


def local_blocks(velocity, template, moving, stiffness, fetch_plane, tissue):
    planes, rows, x_length = moving.shape
    slabs, subs = lax.axis_size("slab"), lax.axis_size("sub")
    total_z, total_y = planes * slabs, rows * subs
    devices = slabs * subs
    part = x_length // devices
    area = planes * rows
    place = jnp.stack([lax.axis_index("slab"), lax.axis_index("sub")])
    bf16, f16, f32 = jnp.bfloat16, jnp.float16, jnp.float32

    def shape(dims, kind=f32):
        return jax.ShapeDtypeStruct(dims, kind)

    def scatter(sends, axis):
        count = lax.axis_size(axis)
        return [sends[0]] + [
            lax.ppermute(sends[d], axis, [(i, (i + d) % count) for i in range(count)]) for d in range(1, count)
        ]

    def exchange(values):
        return lax.all_to_all(values, ("slab", "sub"), split_axis=0, concat_axis=0, tiled=True)

    fetch, marks = fetch_plane.swapaxes(1, 2), tissue.swapaxes(1, 2)
    sends = call(
        functools.partial(send_columns_kernel, slabs),
        [shape((planes + 1, rows, BLOCK), bf16)] * slabs,
        place,
        moving,
        fetch,
    )
    sends = call(
        functools.partial(pick_kernel, slabs),
        [shape((planes + 2, rows, BLOCK), bf16)] * slabs,
        place,
        *scatter(sends, "slab"),
        scratch=[pltpu.VMEM((total_z, rows, BLOCK), bf16)],
        flops=1 << 30,
    )
    received = scatter(sends, "slab")
    first, last = call(
        functools.partial(edge_rows_kernel, slabs),
        [shape((slabs, planes, BLOCK), bf16)] * 2,
        place,
        *received,
    )
    above = lax.ppermute(last, "sub", [(i, (i + 1) % subs) for i in range(subs)])
    below = lax.ppermute(first, "sub", [((i + 1) % subs, i) for i in range(subs)])
    basis_x = in_two(8.0 * real_basis(x_length))
    basis_z = in_two(np.kron(real_basis(total_z), np.eye(8)))
    basis_y = np.concatenate([in_two(real_basis(total_y).T), in_two(real_basis(total_y))])
    each = part + part // 2
    warped, image, weight, chain, kept = call(
        functools.partial(force_zx_kernel, slabs, subs),
        [
            shape(moving.shape, bf16),
            shape(moving.shape),
            shape(moving.shape),
            shape((slabs, subs, each, area)),
            shape((devices, part // 2, area)),
        ],
        place,
        *received,
        template,
        stiffness,
        marks,
        basis_x,
        scratch=[pltpu.VMEM((planes + 2, rows, x_length), f32), pltpu.VMEM((2, x_length, area), f32)],
        flops=3 << 30,
    )
    chain = chain.astype(f16)
    chain = scatter([chain[d] for d in range(slabs)], "slab")
    chain = scatter([jnp.stack([r[e] for r in chain]) for e in range(subs)], "sub")
    spectra = call(
        functools.partial(force_y_kernel, slabs),
        shape((devices, each, area)),
        place,
        above,
        below,
        image,
        weight,
        basis_x,
        kept,
        scratch=[pltpu.VMEM((2, planes, x_length), f32)],
        flops=2 << 30,
    )
    spectra = exchange(spectra.astype(f16))
    chain = call(
        functools.partial(solve_zx_kernel, slabs, subs, x_length),
        [shape((subs, each, area))] * slabs,
        place,
        *[r.astype(f32) for r in chain],
        basis_z,
        basis_y,
        scratch=[pltpu.VMEM((devices, each, area), f32), pltpu.VMEM((total_z, each, total_y), f32)],
        flops=2 << 30,
    )
    chain, spectra = lax.optimization_barrier((chain, spectra))
    chain = scatter([r.astype(f16) for r in chain], "slab")
    chain = scatter([jnp.stack([r[e] for r in chain]) for e in range(subs)], "sub")
    spectra = call(
        functools.partial(solve_yx_kernel, subs, x_length),
        shape((devices, each, area)),
        place,
        spectra.astype(f32),
        basis_z,
        basis_y,
        scratch=[pltpu.VMEM((total_z, each, total_y), f32)],
        flops=2 << 30,
    )
    spectra = exchange(spectra.astype(f16))
    basis_x = in_two(real_basis(x_length))
    updated, kept = call(
        functools.partial(update_z_kernel, slabs, subs),
        [shape(moving.shape), shape((devices, part // 2, area))],
        place,
        basis_x,
        (velocity,),
        *[r.astype(f32) for r in chain],
        scratch=[
            pltpu.VMEM((x_length, area), f32),
            pltpu.VMEM(moving.shape, f32),
            pltpu.SemaphoreType.DMA((1,)),
        ],
        flops=1 << 30,
    )
    new_velocity = call(
        update_kernel,
        shape(velocity.shape),
        place,
        (velocity,),
        spectra.astype(f32),
        basis_x,
        updated,
        kept,
        scratch=[
            pltpu.VMEM((2,) + moving.shape, f32),
            pltpu.VMEM((2,) + moving.shape, f32),
            pltpu.SemaphoreType.DMA((5,)),
        ],
        flops=2 << 30,
        stays=1,
    )
    return (new_velocity, warped)


def local(velocity, template, moving, stiffness, fetch_plane, tissue):
    planes, rows, x_length = moving.shape
    slabs, subs = lax.axis_size("slab"), lax.axis_size("sub")
    fits = (
        x_length == slabs * BLOCK
        and planes == 8
        and planes * slabs * 8 == 256
        and rows % 16 == 0
        and rows * subs == BLOCK
        and x_length % (32 * slabs * subs) == 0
    )
    run = local_blocks if fits else local_general
    return run(velocity, template, moving, stiffness, fetch_plane, tissue)


def solution(mesh):
    placed = (
        P(None, ("groups", "slab"), "sub", None),
        P(("groups", "slab"), "sub", None),
        P(("groups", "slab"), "sub", None),
        P(("groups", "slab"), "sub", None),
        P(("groups", "slab"), "sub", None),
        P(("groups", "slab"), "sub", None),
    )
    return jax.shard_map(
        local,
        mesh=mesh,
        in_specs=placed,
        out_specs=(P(None, ("groups", "slab"), "sub", None), P(("groups", "slab"), "sub", None)),
        check_vma=False,
    )
```

```python
import functools

import jax
import jax.numpy as jnp
import numpy as np
from jax import lax
from jax.experimental import pallas as pl
from jax.experimental.pallas import tpu as pltpu
from jax.sharding import PartitionSpec as P

BLOCK = 128


def extended(cells, sides, width):
    for axis, dim in sides:
        count = lax.axis_size(axis)
        head = lax.slice_in_dim(cells, 0, width, axis=dim)
        tail = lax.slice_in_dim(cells, cells.shape[dim] - width, cells.shape[dim], axis=dim)
        cells = jnp.concatenate(
            [
                lax.ppermute(tail, axis, [(i, (i + 1) % count) for i in range(count)]),
                cells,
                lax.ppermute(head, axis, [((i + 1) % count, i) for i in range(count)]),
            ],
            axis=dim,
        )
    return cells


def tables(length):
    wave_ids = jnp.arange(length, dtype=jnp.int32)
    phase = wave_ids[:, None] * wave_ids[None, :] % length
    angle = 2.0 * jnp.pi / length * phase.astype(jnp.float32)
    return (jnp.cos(angle), jnp.sin(angle))


def apply_along(values, matrix, axis_id):
    result = lax.dot_general(
        values,
        matrix,
        (((axis_id,), (0,)), ((), ())),
        precision=lax.Precision.HIGHEST,
        preferred_element_type=jnp.float32,
    )
    return jnp.moveaxis(result, -1, axis_id)


def forward_along(values_pair, axis_id):
    real_part, imag_part = values_pair
    cosine, sine = tables(real_part.shape[axis_id])
    return (
        apply_along(real_part, cosine, axis_id) + apply_along(imag_part, sine, axis_id),
        apply_along(imag_part, cosine, axis_id) - apply_along(real_part, sine, axis_id),
    )


def inverse_along(values_pair, axis_id):
    real_part, imag_part = values_pair
    length = real_part.shape[axis_id]
    cosine, sine = tables(length)
    scale = 1.0 / length
    return (
        (apply_along(real_part, cosine, axis_id) - apply_along(imag_part, sine, axis_id)) * scale,
        (apply_along(imag_part, cosine, axis_id) + apply_along(real_part, sine, axis_id)) * scale,
    )


def symbol_sq(length, first_id, span):
    wave_ids = first_id + jnp.arange(span, dtype=jnp.int32)
    signed = jnp.where(wave_ids < length // 2, wave_ids, wave_ids - length).astype(jnp.float32)
    wave = 2.0 * jnp.pi / length * signed
    return wave * wave


def local_general(velocity, template, moving, stiffness, fetch_plane, tissue):
    planes_dev, rows_dev, x_length = moving.shape
    blocks_x = x_length // BLOCK
    slabs = lax.axis_size("slab")
    subs = lax.axis_size("sub")
    my_slab = lax.axis_index("slab")
    my_sub = lax.axis_index("sub")
    per_dev = planes_dev * rows_dev * blocks_x
    capacity = 2 * per_dev // slabs
    source_plane = fetch_plane.reshape(-1)
    block_ids = jnp.arange(per_dev, dtype=jnp.int32)
    row_of = block_ids // blocks_x % rows_dev
    column_of = block_ids % blocks_x
    moving_rows = moving.reshape(per_dev, BLOCK)
    holder = source_plane // planes_dev
    within = (source_plane % planes_dev * rows_dev + row_of) * blocks_x + column_of
    matches = (holder[:, None] == jnp.arange(slabs, dtype=jnp.int32)[None, :]).astype(jnp.int32)
    earlier = jnp.sum((jnp.cumsum(matches, axis=0) - matches) * matches, axis=1)
    target = holder * capacity + earlier
    wanted = (
        jnp.zeros((slabs * capacity,), jnp.int32).at[target].set(within).reshape(slabs, capacity)
    )
    asked = lax.all_to_all(wanted, "slab", split_axis=0, concat_axis=0, tiled=True)
    fetched = moving_rows[asked.reshape(-1)].reshape(asked.shape + (BLOCK,))
    replies = lax.all_to_all(fetched, "slab", split_axis=0, concat_axis=0, tiled=True)
    warped_rows = replies.reshape(slabs * capacity, BLOCK)[target]
    warped = warped_rows.reshape(planes_dev, rows_dev, x_length)
    padded = extended(warped, (("slab", 0), ("sub", 1)), 1).astype(jnp.float32)
    image = padded[1:-1, 1:-1]
    grad_z = 0.5 * (padded[2:, 1:-1] - padded[:-2, 1:-1])
    grad_y = 0.5 * (padded[1:-1, 2:] - padded[1:-1, :-2])
    grad_x = 0.5 * (jnp.roll(image, -1, 2) - jnp.roll(image, 1, 2))
    residual = image - template.astype(jnp.float32)
    tissue_vox = jnp.repeat(tissue.astype(jnp.float32), BLOCK, axis=2)
    weight_field = tissue_vox * stiffness * residual
    force = jnp.stack([weight_field * grad_z, weight_field * grad_y, weight_field * grad_x])
    cos_x, sin_x = tables(x_length)
    real_part = apply_along(force, cos_x, 3)
    imag_part = -apply_along(force, sin_x, 3)
    moved = (
        lax.all_to_all(real_part, "sub", split_axis=3, concat_axis=2, tiled=True),
        lax.all_to_all(imag_part, "sub", split_axis=3, concat_axis=2, tiled=True),
    )
    moved = forward_along(moved, 2)
    moved = (
        lax.all_to_all(moved[0], "slab", split_axis=2, concat_axis=1, tiled=True),
        lax.all_to_all(moved[1], "slab", split_axis=2, concat_axis=1, tiled=True),
    )
    moved = forward_along(moved, 1)
    total_z = moved[0].shape[1]
    y_span = moved[0].shape[2]
    x_span = moved[0].shape[3]
    factor = 1.0 / (
        symbol_sq(total_z, 0, total_z)[:, None, None]
        + symbol_sq(y_span * slabs, my_slab * y_span, y_span)[None, :, None]
        + symbol_sq(x_span * subs, my_sub * x_span, x_span)[None, None, :]
        + 1.0 / 256.0
    )
    moved = (moved[0] * factor, moved[1] * factor)
    moved = inverse_along(moved, 1)
    moved = (
        lax.all_to_all(moved[0], "slab", split_axis=1, concat_axis=2, tiled=True),
        lax.all_to_all(moved[1], "slab", split_axis=1, concat_axis=2, tiled=True),
    )
    moved = inverse_along(moved, 2)
    real_part, imag_part = (
        lax.all_to_all(moved[0], "sub", split_axis=2, concat_axis=3, tiled=True),
        lax.all_to_all(moved[1], "sub", split_axis=2, concat_axis=3, tiled=True),
    )
    smoothed = (apply_along(real_part, cos_x, 3) - apply_along(imag_part, sin_x, 3)) * (
        1.0 / x_length
    )
    new_velocity = 0.5 * (velocity - smoothed)
    return (new_velocity, warped)


VMEM_BYTES = 24 * 1024 * 1024


def real_basis(length):
    index = np.arange(length)
    half = length // 2
    wave = np.where(index <= half, index, index - half)[:, None]
    angle = 2.0 * np.pi / length * (wave * index[None, :] % length)
    rows = np.where(index[:, None] <= half, np.cos(angle), np.sin(angle)) * np.sqrt(2.0 / length)
    rows[0] /= np.sqrt(2.0)
    rows[half] /= np.sqrt(2.0)
    return rows


def in_two(table):
    high = np.asarray(table, np.float32).astype(jnp.bfloat16)
    low = (np.asarray(table, np.float64) - high.astype(np.float64)).astype(jnp.bfloat16)
    return np.stack([high, low])


def split(values):
    high = values.astype(jnp.bfloat16)
    return high, (values - high.astype(jnp.float32)).astype(jnp.bfloat16)


def times(left, right, dims):
    def one(a, b):
        return lax.dot_general(a, b, (dims, ((), ())), preferred_element_type=jnp.float32)

    return one(left[0], right[0]) + (one(left[0], right[1]) + one(left[1], right[0]))


def wave_sq(index, length):
    wave = jnp.where(index <= length // 2, index, index - length // 2).astype(jnp.float32)
    wave = wave * (2.0 * np.pi / length)
    return wave * wave


def around(value, count):
    return lax.rem(value + 2 * count, count)


def call(kernel, out_shape, *arguments, scratch=(), flops=0, stays=0):
    places = [
        pl.BlockSpec(memory_space=pltpu.HBM if isinstance(a, tuple) else pltpu.SMEM if a.ndim == 1 else pltpu.VMEM)
        for a in arguments
    ]
    arguments = [a[0] if isinstance(a, tuple) else a for a in arguments]
    out_places = [
        pl.BlockSpec(memory_space=pltpu.HBM if k < stays else pltpu.VMEM)
        for k in range(len(jax.tree.leaves(out_shape)))
    ]
    nbytes = sum(a.size * a.dtype.itemsize for a in arguments + jax.tree.leaves(out_shape))
    return pl.pallas_call(
        kernel,
        out_shape=out_shape,
        in_specs=places,
        out_specs=jax.tree.unflatten(jax.tree.structure(out_shape), out_places),
        scratch_shapes=list(scratch),
        compiler_params=pltpu.CompilerParams(vmem_limit_bytes=VMEM_BYTES),
        cost_estimate=pl.CostEstimate(flops=flops, bytes_accessed=nbytes, transcendentals=0),
    )(*arguments)


def by_row(ref, rows):
    cells = jnp.concatenate([ref[z].astype(jnp.float32) for z in range(ref.shape[0])], axis=0)
    cells = jnp.concatenate([cells, jnp.zeros((cells.shape[0], BLOCK - rows), jnp.float32)], axis=1)
    cells = jnp.concatenate([cells, jnp.zeros((BLOCK - cells.shape[0], BLOCK), jnp.float32)], axis=0)
    return cells.T[:rows]


def send_columns_kernel(slabs, place, moving, fetch, *sends):
    planes, rows, _ = moving.shape
    for step, send in enumerate(sends):
        to = around(place[0] + step, slabs)
        send[0:planes] = moving[:, :, pl.ds(pl.multiple_of(to * BLOCK, BLOCK), BLOCK)]
        wanted = jnp.concatenate([fetch[z, pl.ds(to, 1), :] for z in range(planes)], axis=0).astype(jnp.float32)
        wanted = jnp.concatenate([wanted, jnp.zeros((planes, BLOCK - rows), jnp.float32)], axis=1)
        wanted = jnp.concatenate([wanted, jnp.zeros((BLOCK - planes, BLOCK), jnp.float32)], axis=0)
        send[planes] = wanted.T[:rows].astype(jnp.bfloat16)


def pick_kernel(slabs, place, *refs):
    received, sends, picked = refs[:slabs], refs[slabs:-1], refs[-1]
    planes = received[0].shape[0] - 1
    rows = received[0].shape[1]
    me = place[0]
    total = slabs * planes
    group = 4

    def name(other, plane):
        number = (around(me - other, slabs) * planes).astype(jnp.float32) + float(plane)
        return jnp.full((rows, BLOCK), number, jnp.float32).astype(jnp.bfloat16)

    for step in range(slabs):
        first = around(me - step, slabs) * planes
        names = received[step][planes].astype(jnp.float32)
        for start in range(0, planes, group):
            wanted = [
                jnp.broadcast_to(names[:, z : z + 1], (rows, BLOCK)).astype(jnp.bfloat16)
                for z in range(start, start + group)
            ]
            found = [jnp.zeros((rows, BLOCK), jnp.bfloat16) for _ in range(group)]
            for other in range(slabs):
                for plane in range(planes):
                    values = received[other][plane]
                    own = name(other, plane)
                    found = [jnp.where(w == own, values, f) for w, f in zip(wanted, found)]
            for z in range(group):
                picked[first + start + z] = found[z]
    for step, send in enumerate(sends):
        first = around(me + step, slabs) * planes
        for k in range(planes + 2):
            send[k] = picked[around(first + (k - 1), total)]


def force_zx_kernel(slabs, subs, place, *refs):
    received, refs = refs[:slabs], refs[slabs:]
    template, stiffness, tissue, basis, first, last, image, weight, spectra, kept, planes_of, wide = refs
    planes, rows, x_length = template.shape
    blocks = x_length // BLOCK
    for step in range(slabs):
        block = pl.ds(pl.multiple_of(around(place[0] - step, slabs) * BLOCK, BLOCK), BLOCK)
        planes_of[:, :, block] = received[step][...].astype(jnp.float32)
    for edge, row in ((first, 0), (last, rows - 1)):
        own = [planes_of[z + 1, row : row + 1, :] for z in range(planes)]
        edge[...] = jnp.concatenate(own * 2, axis=0).astype(jnp.bfloat16)
    marks = by_row(tissue, rows)
    forces = [[], []]
    for z in range(planes):
        here = planes_of[z + 1]
        marked = jnp.concatenate(
            [
                jnp.broadcast_to(marks[:, z * blocks + b : z * blocks + b + 1], (rows, BLOCK))
                for b in range(blocks)
            ],
            axis=1,
        )
        own = 0.5 * (marked * stiffness[z] * (here - template[z].astype(jnp.float32)))
        image[z] = here
        weight[z] = own
        forces[0].append(own * (planes_of[z + 2] - planes_of[z]))
        forces[1].append(own * (pltpu.roll(here, x_length - 1, 1) - pltpu.roll(here, 1, 1)))
    for a in range(2):
        force = split(jnp.concatenate(forces[a], axis=0))
        wide[a] = times((basis[0], basis[1]), force, ((1,), (1,)))
    part = x_length // (slabs * subs)
    half = part // 2
    for d in range(slabs):
        for e in range(subs):
            start = (around(place[0] + d, slabs) * subs + around(place[1] + e, subs)) * part
            spectra[d, e, :part] = wide[0, pl.ds(pl.multiple_of(start, part), part), :]
            spectra[d, e, part:] = wide[1, pl.ds(pl.multiple_of(start + half, half), half), :]
    for k in range(slabs * subs):
        kept[k] = wide[1, k * part : k * part + half, :]


def force_y_kernel(above, below, image, weight, basis, kept, spectra):
    planes, rows, x_length = image.shape
    edges = above[...].astype(jnp.float32), below[...].astype(jnp.float32)
    row = lax.broadcasted_iota(jnp.int32, (rows, x_length), 0)
    force = []
    for z in range(planes):
        here = image[z]
        before = jnp.where(row == 0, edges[0][z : z + 1], pltpu.roll(here, 1, 0))
        after = jnp.where(row == rows - 1, edges[1][z : z + 1], pltpu.roll(here, rows - 1, 0))
        force.append(weight[z] * (after - before))
    devices = spectra.shape[0]
    part = x_length // devices
    spectrum = times((basis[0], basis[1]), split(jnp.concatenate(force, axis=0)), ((1,), (1,)))
    spectra[:, :part, :] = spectrum.reshape(devices, part, planes * rows)
    spectra[:, part:, :] = kept[...]


def swap_blocks(values):
    width = values[0].shape[1]
    lane = lax.broadcasted_iota(jnp.int32, values[0].shape, 1)
    lower, even = lane < width // 2, lax.rem(lane // (width // 4), 2) == 0

    def turn(own, count):
        return pltpu.roll(own, count * (width // 4), 1)

    a, b, c, d = values
    a, c = jnp.where(lower, a, turn(c, 2)), jnp.where(lower, turn(a, 2), c)
    b, d = jnp.where(lower, b, turn(d, 2)), jnp.where(lower, turn(b, 2), d)
    return [
        jnp.where(even, a, turn(b, 1)),
        jnp.where(even, turn(a, 3), b),
        jnp.where(even, c, turn(d, 1)),
        jnp.where(even, turn(c, 3), d),
    ]


def solve(first, x_length, offsets, subs, spectra, basis_z, basis_y, out, cells):
    devices, used, area = spectra.shape
    total_z, _, total_y = cells.shape
    slabs = devices // subs
    planes, rows = total_z // slabs, total_y // subs
    fold = total_y // rows
    tile = 8

    def along_y(k, values):
        high, low = basis_y[2 * k], basis_y[2 * k + 1]
        four = jnp.concatenate(
            [jnp.concatenate([high, low], axis=1), jnp.concatenate([high, jnp.zeros_like(low)], axis=1)], axis=0
        )
        sums = jnp.dot(jnp.concatenate(split(values), axis=1), four, preferred_element_type=jnp.float32)
        return sums[:, :total_y] + sums[:, total_y:]

    def along_z(k, values):
        high, low = basis_z[2 * k], basis_z[2 * k + 1]
        parts = split(values)
        return jnp.dot(
            jnp.concatenate([high, high, low], axis=1),
            jnp.concatenate([parts[0], parts[1], parts[0]], axis=0),
            preferred_element_type=jnp.float32,
        )

    for s in range(slabs):
        own = []
        for f in range(0, planes // fold):
            lanes = slice(f * total_y, (f + 1) * total_y)
            own += swap_blocks([spectra[s * subs + q][:, lanes] for q in range(subs)])
        own = along_y(0, jnp.concatenate(own, axis=0))
        cells[s * planes : (s + 1) * planes] = own.reshape(planes, used, total_y)
    index = lax.broadcasted_iota(jnp.int32, (total_z * tile, 1), 0)
    z_sq = wave_sq(index // tile, total_z)
    y_sq = wave_sq(lax.broadcasted_iota(jnp.int32, (1, total_y), 1), total_y)
    own, scale = [], []
    for start in range(0, used, tile):
        own.append(cells[:, start : start + tile, :].reshape(total_z * tile, total_y))
        x_sq = wave_sq(first + offsets[start // tile] + lax.rem(index, tile), x_length)
        scale.append((z_sq + x_sq + y_sq) * 256.0 + 1.0)
    own = along_z(0, jnp.concatenate(own, axis=1))
    own = along_z(1, own / jnp.concatenate(scale, axis=1))
    for k, start in enumerate(range(0, used, tile)):
        part = own[:, k * total_y : (k + 1) * total_y]
        cells[:, start : start + tile, :] = part.reshape(total_z, tile, total_y)
    for s in range(slabs):
        own = along_y(1, cells[s * planes : (s + 1) * planes].reshape(planes * used, total_y))
        for f in range(0, planes // fold):
            blocks = swap_blocks([own[z * used : (z + 1) * used] for z in range(f * fold, (f + 1) * fold)])
            for q in range(subs):
                out[s * subs + q, :, f * total_y : (f + 1) * total_y] = blocks[q]


def solve_yx_kernel(subs, x_length, place, spectra, basis_z, basis_y, out, cells):
    devices = out.shape[0]
    part = x_length // devices
    offsets = list(range(0, part, 8)) + list(range(0, part // 2, 8))
    solve((place[0] * subs + place[1]) * part, x_length, offsets, subs, spectra, basis_z, basis_y, out, cells)


def solve_zx_kernel(slabs, subs, x_length, place, *refs):
    received, refs = refs[:subs], refs[subs:]
    basis_z, basis_y, sends, (spectra, cells) = refs[0], refs[1], refs[2 : 2 + slabs], refs[2 + slabs :]
    part = x_length // (slabs * subs)
    offsets = list(range(0, part, 8)) + list(range(part // 2, part, 8))
    for e in range(subs):
        for d in range(slabs):
            spectra[around(place[0] - d, slabs) * subs + around(place[1] - e, subs)] = received[e][d]
    solve((place[0] * subs + place[1]) * part, x_length, offsets, subs, spectra, basis_z, basis_y, spectra, cells)
    for d in range(slabs):
        for e in range(subs):
            sends[d][e] = spectra[around(place[0] + d, slabs) * subs + around(place[1] + e, subs)]


def moved(spectra, velocity, basis):
    smoothed = times(split(spectra.T), (basis[0], basis[1]), ((1,), (0,)))
    return 0.5 * (velocity - 32.0 * smoothed.reshape(velocity.shape))


def update_z_kernel(slabs, subs, place, basis, velocity, *refs):
    received, (out, kept, gathered) = refs[:subs], refs[subs:]
    half = kept.shape[1]
    part = 2 * half
    for e in range(subs):
        for d in range(slabs):
            index = around(place[0] - d, slabs) * subs + around(place[1] - e, subs)
            gathered[pl.ds(pl.multiple_of(index * part, part), part), :] = received[e][d, :part]
            kept[index] = received[e][d, part:]
    out[...] = moved(gathered[...], velocity[0], basis)


def update_kernel(spectra, basis, velocity, updated, kept, out, result, done):
    devices, half, area = kept.shape
    part = 2 * half
    leaving = [pltpu.make_async_copy(updated, out.at[0], done.at[0])]
    leaving[0].start()
    for a in range(2):
        if a:
            own = jnp.concatenate([spectra[:, part:, :], kept[...]], axis=1)
        else:
            own = spectra[:, :part, :]
        result[a] = moved(own.reshape(devices * part, area), velocity[a + 1], basis)
        leaving.append(pltpu.make_async_copy(result.at[a], out.at[a + 1], done.at[a + 1]))
        leaving[-1].start()
    for copy in leaving:
        copy.wait()


def place_kernel(slabs, place, *refs):
    received, warped = refs[:slabs], refs[slabs]
    for step in range(slabs):
        block = pl.ds(pl.multiple_of(around(place[0] - step, slabs) * BLOCK, BLOCK), BLOCK)
        warped[:, :, block] = received[step][1:-1]


def local_blocks(velocity, template, moving, stiffness, fetch_plane, tissue):
    planes, rows, x_length = moving.shape
    slabs, subs = lax.axis_size("slab"), lax.axis_size("sub")
    total_z, total_y = planes * slabs, rows * subs
    devices = slabs * subs
    part = x_length // devices
    area = planes * rows
    place = jnp.stack([lax.axis_index("slab"), lax.axis_index("sub")])
    bf16, f16, f32 = jnp.bfloat16, jnp.float16, jnp.float32

    def shape(dims, kind=f32):
        return jax.ShapeDtypeStruct(dims, kind)

    def scatter(sends, axis):
        count = lax.axis_size(axis)
        return [sends[0]] + [
            lax.ppermute(sends[d], axis, [(i, (i + d) % count) for i in range(count)]) for d in range(1, count)
        ]

    def exchange(values):
        return lax.all_to_all(values, ("slab", "sub"), split_axis=0, concat_axis=0, tiled=True)

    fetch, marks = fetch_plane.swapaxes(1, 2), tissue.swapaxes(1, 2)
    sends = call(
        functools.partial(send_columns_kernel, slabs),
        [shape((planes + 1, rows, BLOCK), bf16)] * slabs,
        place,
        moving,
        fetch,
    )
    sends = call(
        functools.partial(pick_kernel, slabs),
        [shape((planes + 2, rows, BLOCK), bf16)] * slabs,
        place,
        *scatter(sends, "slab"),
        scratch=[pltpu.VMEM((total_z, rows, BLOCK), bf16)],
        flops=1 << 30,
    )
    received = scatter(sends, "slab")
    basis_x = in_two(8.0 * real_basis(x_length))
    basis_z = np.kron(real_basis(total_z), np.eye(8))
    basis_z = np.concatenate([in_two(basis_z), in_two(basis_z.T)])
    basis_y = np.concatenate([in_two(real_basis(total_y).T), in_two(real_basis(total_y))])
    each = part + part // 2
    first, last, image, weight, chain, kept = call(
        functools.partial(force_zx_kernel, slabs, subs),
        [
            shape((2 * planes, x_length), bf16),
            shape((2 * planes, x_length), bf16),
            shape(moving.shape),
            shape(moving.shape),
            shape((slabs, subs, each, area)),
            shape((devices, part // 2, area)),
        ],
        place,
        *received,
        template,
        stiffness,
        marks,
        basis_x,
        scratch=[pltpu.VMEM((planes + 2, rows, x_length), f32), pltpu.VMEM((2, x_length, area), f32)],
        flops=3 << 30,
    )
    above = lax.ppermute(last, "sub", [(i, (i + 1) % subs) for i in range(subs)])
    below = lax.ppermute(first, "sub", [((i + 1) % subs, i) for i in range(subs)])
    chain = chain.astype(f16)
    chain = scatter([chain[d] for d in range(slabs)], "slab")
    later, *chain = lax.optimization_barrier((place, *chain))
    warped = call(functools.partial(place_kernel, slabs), shape(moving.shape, bf16), later, *received)
    chain = scatter([jnp.stack([r[e] for r in chain]) for e in range(subs)], "sub")
    spectra = call(
        force_y_kernel,
        shape((devices, each, area)),
        above,
        below,
        image,
        weight,
        basis_x,
        kept,
        flops=2 << 30,
    )
    spectra = exchange(spectra.astype(f16))
    chain = call(
        functools.partial(solve_zx_kernel, slabs, subs, x_length),
        [shape((subs, each, area))] * slabs,
        place,
        *[r.astype(f32) for r in chain],
        basis_z,
        basis_y,
        scratch=[pltpu.VMEM((devices, each, area), f32), pltpu.VMEM((total_z, each, total_y), f32)],
        flops=2 << 30,
    )
    chain, spectra, warped = lax.optimization_barrier((chain, spectra, warped))
    chain = scatter([r.astype(f16) for r in chain], "slab")
    chain = scatter([jnp.stack([r[e] for r in chain]) for e in range(subs)], "sub")
    spectra = call(
        functools.partial(solve_yx_kernel, subs, x_length),
        shape((devices, each, area)),
        place,
        spectra.astype(f32),
        basis_z,
        basis_y,
        scratch=[pltpu.VMEM((total_z, each, total_y), f32)],
        flops=2 << 30,
    )
    spectra = exchange(spectra.astype(f16))
    basis_x = in_two(real_basis(x_length))
    updated, kept = call(
        functools.partial(update_z_kernel, slabs, subs),
        [shape(moving.shape), shape((devices, part // 2, area))],
        place,
        basis_x,
        velocity,
        *[r.astype(f32) for r in chain],
        scratch=[pltpu.VMEM((x_length, area), f32)],
        flops=1 << 30,
    )
    new_velocity = call(
        update_kernel,
        shape(velocity.shape),
        spectra.astype(f32),
        basis_x,
        velocity,
        updated,
        kept,
        scratch=[pltpu.VMEM((2,) + moving.shape, f32), pltpu.SemaphoreType.DMA((3,))],
        flops=2 << 30,
        stays=1,
    )
    return (new_velocity, warped)


def local(velocity, template, moving, stiffness, fetch_plane, tissue):
    planes, rows, x_length = moving.shape
    slabs, subs = lax.axis_size("slab"), lax.axis_size("sub")
    fits = (
        x_length == slabs * BLOCK
        and planes == 8
        and planes * slabs * 8 == 256
        and rows % 16 == 0
        and rows * subs == BLOCK
        and subs == 4
        and x_length % (32 * slabs * subs) == 0
    )
    run = local_blocks if fits else local_general
    return run(velocity, template, moving, stiffness, fetch_plane, tissue)


def solution(mesh):
    placed = (
        P(None, ("groups", "slab"), "sub", None),
        P(("groups", "slab"), "sub", None),
        P(("groups", "slab"), "sub", None),
        P(("groups", "slab"), "sub", None),
        P(("groups", "slab"), "sub", None),
        P(("groups", "slab"), "sub", None),
    )
    return jax.shard_map(
        local,
        mesh=mesh,
        in_specs=placed,
        out_specs=(P(None, ("groups", "slab"), "sub", None), P(("groups", "slab"), "sub", None)),
        check_vma=False,
    )
```

```python
import functools

import jax
import jax.numpy as jnp
import numpy as np
from jax import lax
from jax.experimental import pallas as pl
from jax.experimental.pallas import tpu as pltpu
from jax.sharding import PartitionSpec as P

BLOCK = 128


def extended(cells, sides, width):
    for axis, dim in sides:
        count = lax.axis_size(axis)
        head = lax.slice_in_dim(cells, 0, width, axis=dim)
        tail = lax.slice_in_dim(cells, cells.shape[dim] - width, cells.shape[dim], axis=dim)
        cells = jnp.concatenate(
            [
                lax.ppermute(tail, axis, [(i, (i + 1) % count) for i in range(count)]),
                cells,
                lax.ppermute(head, axis, [((i + 1) % count, i) for i in range(count)]),
            ],
            axis=dim,
        )
    return cells


def tables(length):
    wave_ids = jnp.arange(length, dtype=jnp.int32)
    phase = wave_ids[:, None] * wave_ids[None, :] % length
    angle = 2.0 * jnp.pi / length * phase.astype(jnp.float32)
    return (jnp.cos(angle), jnp.sin(angle))


def apply_along(values, matrix, axis_id):
    result = lax.dot_general(
        values,
        matrix,
        (((axis_id,), (0,)), ((), ())),
        precision=lax.Precision.HIGHEST,
        preferred_element_type=jnp.float32,
    )
    return jnp.moveaxis(result, -1, axis_id)


def forward_along(values_pair, axis_id):
    real_part, imag_part = values_pair
    cosine, sine = tables(real_part.shape[axis_id])
    return (
        apply_along(real_part, cosine, axis_id) + apply_along(imag_part, sine, axis_id),
        apply_along(imag_part, cosine, axis_id) - apply_along(real_part, sine, axis_id),
    )


def inverse_along(values_pair, axis_id):
    real_part, imag_part = values_pair
    length = real_part.shape[axis_id]
    cosine, sine = tables(length)
    scale = 1.0 / length
    return (
        (apply_along(real_part, cosine, axis_id) - apply_along(imag_part, sine, axis_id)) * scale,
        (apply_along(imag_part, cosine, axis_id) + apply_along(real_part, sine, axis_id)) * scale,
    )


def symbol_sq(length, first_id, span):
    wave_ids = first_id + jnp.arange(span, dtype=jnp.int32)
    signed = jnp.where(wave_ids < length // 2, wave_ids, wave_ids - length).astype(jnp.float32)
    wave = 2.0 * jnp.pi / length * signed
    return wave * wave


def local_general(velocity, template, moving, stiffness, fetch_plane, tissue):
    planes_dev, rows_dev, x_length = moving.shape
    blocks_x = x_length // BLOCK
    slabs = lax.axis_size("slab")
    subs = lax.axis_size("sub")
    my_slab = lax.axis_index("slab")
    my_sub = lax.axis_index("sub")
    per_dev = planes_dev * rows_dev * blocks_x
    capacity = 2 * per_dev // slabs
    source_plane = fetch_plane.reshape(-1)
    block_ids = jnp.arange(per_dev, dtype=jnp.int32)
    row_of = block_ids // blocks_x % rows_dev
    column_of = block_ids % blocks_x
    moving_rows = moving.reshape(per_dev, BLOCK)
    holder = source_plane // planes_dev
    within = (source_plane % planes_dev * rows_dev + row_of) * blocks_x + column_of
    matches = (holder[:, None] == jnp.arange(slabs, dtype=jnp.int32)[None, :]).astype(jnp.int32)
    earlier = jnp.sum((jnp.cumsum(matches, axis=0) - matches) * matches, axis=1)
    target = holder * capacity + earlier
    wanted = (
        jnp.zeros((slabs * capacity,), jnp.int32).at[target].set(within).reshape(slabs, capacity)
    )
    asked = lax.all_to_all(wanted, "slab", split_axis=0, concat_axis=0, tiled=True)
    fetched = moving_rows[asked.reshape(-1)].reshape(asked.shape + (BLOCK,))
    replies = lax.all_to_all(fetched, "slab", split_axis=0, concat_axis=0, tiled=True)
    warped_rows = replies.reshape(slabs * capacity, BLOCK)[target]
    warped = warped_rows.reshape(planes_dev, rows_dev, x_length)
    padded = extended(warped, (("slab", 0), ("sub", 1)), 1).astype(jnp.float32)
    image = padded[1:-1, 1:-1]
    grad_z = 0.5 * (padded[2:, 1:-1] - padded[:-2, 1:-1])
    grad_y = 0.5 * (padded[1:-1, 2:] - padded[1:-1, :-2])
    grad_x = 0.5 * (jnp.roll(image, -1, 2) - jnp.roll(image, 1, 2))
    residual = image - template.astype(jnp.float32)
    tissue_vox = jnp.repeat(tissue.astype(jnp.float32), BLOCK, axis=2)
    weight_field = tissue_vox * stiffness * residual
    force = jnp.stack([weight_field * grad_z, weight_field * grad_y, weight_field * grad_x])
    cos_x, sin_x = tables(x_length)
    real_part = apply_along(force, cos_x, 3)
    imag_part = -apply_along(force, sin_x, 3)
    moved = (
        lax.all_to_all(real_part, "sub", split_axis=3, concat_axis=2, tiled=True),
        lax.all_to_all(imag_part, "sub", split_axis=3, concat_axis=2, tiled=True),
    )
    moved = forward_along(moved, 2)
    moved = (
        lax.all_to_all(moved[0], "slab", split_axis=2, concat_axis=1, tiled=True),
        lax.all_to_all(moved[1], "slab", split_axis=2, concat_axis=1, tiled=True),
    )
    moved = forward_along(moved, 1)
    total_z = moved[0].shape[1]
    y_span = moved[0].shape[2]
    x_span = moved[0].shape[3]
    factor = 1.0 / (
        symbol_sq(total_z, 0, total_z)[:, None, None]
        + symbol_sq(y_span * slabs, my_slab * y_span, y_span)[None, :, None]
        + symbol_sq(x_span * subs, my_sub * x_span, x_span)[None, None, :]
        + 1.0 / 256.0
    )
    moved = (moved[0] * factor, moved[1] * factor)
    moved = inverse_along(moved, 1)
    moved = (
        lax.all_to_all(moved[0], "slab", split_axis=1, concat_axis=2, tiled=True),
        lax.all_to_all(moved[1], "slab", split_axis=1, concat_axis=2, tiled=True),
    )
    moved = inverse_along(moved, 2)
    real_part, imag_part = (
        lax.all_to_all(moved[0], "sub", split_axis=2, concat_axis=3, tiled=True),
        lax.all_to_all(moved[1], "sub", split_axis=2, concat_axis=3, tiled=True),
    )
    smoothed = (apply_along(real_part, cos_x, 3) - apply_along(imag_part, sin_x, 3)) * (
        1.0 / x_length
    )
    new_velocity = 0.5 * (velocity - smoothed)
    return (new_velocity, warped)


VMEM_BYTES = 24 * 1024 * 1024


def real_basis(length):
    index = np.arange(length)
    half = length // 2
    wave = np.where(index <= half, index, index - half)[:, None]
    angle = 2.0 * np.pi / length * (wave * index[None, :] % length)
    rows = np.where(index[:, None] <= half, np.cos(angle), np.sin(angle)) * np.sqrt(2.0 / length)
    rows[0] /= np.sqrt(2.0)
    rows[half] /= np.sqrt(2.0)
    return rows


def in_two(table):
    high = np.asarray(table, np.float32).astype(jnp.bfloat16)
    low = (np.asarray(table, np.float64) - high.astype(np.float64)).astype(jnp.bfloat16)
    return np.stack([high, low])


def split(values):
    high = values.astype(jnp.bfloat16)
    return high, (values - high.astype(jnp.float32)).astype(jnp.bfloat16)


def times(left, right, dims):
    def one(a, b):
        return lax.dot_general(a, b, (dims, ((), ())), preferred_element_type=jnp.float32)

    return one(left[0], right[0]) + (one(left[0], right[1]) + one(left[1], right[0]))


def wave_sq(index, length):
    wave = jnp.where(index <= length // 2, index, index - length // 2).astype(jnp.float32)
    wave = wave * (2.0 * np.pi / length)
    return wave * wave


def around(value, count):
    return lax.rem(value + 2 * count, count)


def call(kernel, out_shape, *arguments, scratch=(), flops=0, stays=0):
    places = [
        pl.BlockSpec(memory_space=pltpu.HBM if isinstance(a, tuple) else pltpu.SMEM if a.ndim == 1 else pltpu.VMEM)
        for a in arguments
    ]
    arguments = [a[0] if isinstance(a, tuple) else a for a in arguments]
    out_places = [
        pl.BlockSpec(memory_space=pltpu.HBM if k < stays else pltpu.VMEM)
        for k in range(len(jax.tree.leaves(out_shape)))
    ]
    nbytes = sum(a.size * a.dtype.itemsize for a in arguments + jax.tree.leaves(out_shape))
    return pl.pallas_call(
        kernel,
        out_shape=out_shape,
        in_specs=places,
        out_specs=jax.tree.unflatten(jax.tree.structure(out_shape), out_places),
        scratch_shapes=list(scratch),
        compiler_params=pltpu.CompilerParams(vmem_limit_bytes=VMEM_BYTES),
        cost_estimate=pl.CostEstimate(flops=flops, bytes_accessed=nbytes, transcendentals=0),
    )(*arguments)


def by_row(ref, rows):
    cells = jnp.concatenate([ref[z].astype(jnp.float32) for z in range(ref.shape[0])], axis=0)
    cells = jnp.concatenate([cells, jnp.zeros((cells.shape[0], BLOCK - rows), jnp.float32)], axis=1)
    cells = jnp.concatenate([cells, jnp.zeros((BLOCK - cells.shape[0], BLOCK), jnp.float32)], axis=0)
    return cells.T[:rows]


def send_columns_kernel(slabs, place, moving, fetch, *sends):
    planes, rows, _ = moving.shape
    for step, send in enumerate(sends):
        to = around(place[0] + step, slabs)
        block = pl.ds(pl.multiple_of(to * BLOCK, BLOCK), BLOCK)
        for z in range(planes):
            send[z * rows : (z + 1) * rows] = moving[z, :, block]
        asked = jnp.concatenate([fetch[z, pl.ds(to, 1), :] for z in range(planes)] * 2, axis=0).astype(jnp.float32)
        asked = jnp.concatenate([asked, jnp.zeros((2 * planes, BLOCK - rows), jnp.float32)], axis=1)
        send[planes * rows :] = asked.astype(jnp.bfloat16)


def pick_kernel(slabs, place, *refs):
    received, sends = refs[:slabs], refs[slabs:]
    planes, rows = sends[0].shape[0] - 2, sends[0].shape[1]
    me = place[0]
    group = 4

    def name(other, plane):
        number = (around(me - other, slabs) * planes).astype(jnp.float32) + float(plane)
        return jnp.full((rows, BLOCK), number, jnp.float32).astype(jnp.bfloat16)

    for step in range(slabs):
        names = received[step][planes * rows :].astype(jnp.float32)[:planes]
        names = jnp.concatenate([names, jnp.zeros((BLOCK - planes, BLOCK), jnp.float32)], axis=0).T[:rows]
        for start in range(0, planes, group):
            wanted = [
                jnp.broadcast_to(names[:, z : z + 1], (rows, BLOCK)).astype(jnp.bfloat16)
                for z in range(start, start + group)
            ]
            found = [jnp.zeros((rows, BLOCK), jnp.bfloat16) for _ in range(group)]
            for other in range(slabs):
                for plane in range(planes):
                    values = received[other][plane * rows : (plane + 1) * rows]
                    own = name(other, plane)
                    found = [jnp.where(w == own, values, f) for w, f in zip(wanted, found)]
            back = (slabs - step) % slabs
            for z in range(group):
                own = start + z
                sends[back][own + 1] = found[z]
                if own == 0:
                    sends[(back - 1) % slabs][planes + 1] = found[z]
                if own == planes - 1:
                    sends[(back + 1) % slabs][0] = found[z]


def coefficient_kernel(stiffness, tissue, out):
    planes, rows, x_length = stiffness.shape
    blocks = x_length // BLOCK
    marks = by_row(tissue, rows)
    for z in range(planes):
        marked = jnp.concatenate(
            [
                jnp.broadcast_to(marks[:, z * blocks + b : z * blocks + b + 1], (rows, BLOCK))
                for b in range(blocks)
            ],
            axis=1,
        )
        out[z] = 0.5 * marked * stiffness[z]


def force_zx_kernel(slabs, subs, place, *refs):
    received, refs = refs[:slabs], refs[slabs:]
    template, coefficient, basis, first, image, weight, spectra, kept, planes_of, wide = refs
    planes, rows, x_length = template.shape
    for step in range(slabs):
        block = pl.ds(pl.multiple_of(around(place[0] - step, slabs) * BLOCK, BLOCK), BLOCK)
        planes_of[:, :, block] = received[step][...].astype(jnp.float32)
    forces = [[], []]
    for z in range(planes):
        here = planes_of[z + 1]
        own = coefficient[z] * (here - template[z].astype(jnp.float32))
        image[z] = here
        weight[z] = own
        first[z : z + 1] = here[0:1]
        first[planes + z : planes + z + 1] = here[1:2]
        first[2 * planes + z : 2 * planes + z + 1] = own[0:1]
        forces[0].append(own * (planes_of[z + 2] - planes_of[z]))
        forces[1].append(own * (pltpu.roll(here, x_length - 1, 1) - pltpu.roll(here, 1, 1)))
    for a in range(2):
        force = split(jnp.concatenate(forces[a], axis=0))
        wide[a] = times((basis[0], basis[1]), force, ((1,), (1,)))
    part = x_length // (slabs * subs)
    cut = kept.shape[1]
    for d in range(slabs):
        for e in range(subs):
            start = (around(place[0] + d, slabs) * subs + around(place[1] + e, subs)) * part
            spectra[d, e, :part] = wide[0, pl.ds(pl.multiple_of(start, part), part), :]
            spectra[d, e, part:] = wide[1, pl.ds(pl.multiple_of(start + cut, 8), part - cut), :]
    for k in range(slabs * subs):
        kept[k] = wide[1, k * part : k * part + cut, :]


def force_y_kernel(beyond, image, weight, basis, kept, spectra):
    planes, rows, x_length = image.shape
    row = lax.broadcasted_iota(jnp.int32, (rows, x_length), 0)
    force = []
    for z in range(planes):
        here = image[z]
        after = jnp.where(row == rows - 2, beyond[z : z + 1, :], pltpu.roll(here, rows - 2, 0))
        after = jnp.where(row == rows - 1, beyond[planes + z : planes + z + 1, :], after)
        own = pltpu.roll(weight[z], rows - 1, 0)
        own = jnp.where(row == rows - 1, beyond[2 * planes + z : 2 * planes + z + 1, :], own)
        force.append(own * (after - here))
    devices = spectra.shape[0]
    part = x_length // devices
    spectrum = times((basis[0], basis[1]), split(jnp.concatenate(force, axis=0)), ((1,), (1,)))
    spectra[:, :part, :] = spectrum.reshape(devices, part, planes * rows)
    spectra[:, part:, :] = kept[...]


def swap_blocks(values):
    width = values[0].shape[1]
    lane = lax.broadcasted_iota(jnp.int32, values[0].shape, 1)
    lower, even = lane < width // 2, lax.rem(lane // (width // 4), 2) == 0

    def turn(own, count):
        return pltpu.roll(own, count * (width // 4), 1)

    a, b, c, d = values
    a, c = jnp.where(lower, a, turn(c, 2)), jnp.where(lower, turn(a, 2), c)
    b, d = jnp.where(lower, b, turn(d, 2)), jnp.where(lower, turn(b, 2), d)
    return [
        jnp.where(even, a, turn(b, 1)),
        jnp.where(even, turn(a, 3), b),
        jnp.where(even, c, turn(d, 1)),
        jnp.where(even, turn(c, 3), d),
    ]


def solve(first, x_length, offsets, shifted, subs, spectra, basis_z, basis_y, out, cells):
    devices, used, area = spectra.shape
    total_z, _, total_y = cells.shape
    slabs = devices // subs
    planes, rows = total_z // slabs, total_y // subs
    fold = total_y // rows
    tile = 8

    def along_y(k, values):
        high, low = basis_y[2 * k], basis_y[2 * k + 1]
        four = jnp.concatenate(
            [jnp.concatenate([high, low], axis=1), jnp.concatenate([high, jnp.zeros_like(low)], axis=1)], axis=0
        )
        sums = jnp.dot(jnp.concatenate(split(values), axis=1), four, preferred_element_type=jnp.float32)
        return sums[:, :total_y] + sums[:, total_y:]

    def along_z(k, values):
        high, low = basis_z[2 * k], basis_z[2 * k + 1]
        parts = split(values)
        return jnp.dot(
            jnp.concatenate([high, high, low], axis=1),
            jnp.concatenate([parts[0], parts[1], parts[0]], axis=0),
            preferred_element_type=jnp.float32,
        )

    for s in range(slabs):
        own = []
        for f in range(0, planes // fold):
            lanes = slice(f * total_y, (f + 1) * total_y)
            own += swap_blocks([spectra[s * subs + q][:, lanes] for q in range(subs)])
        for low, high, table in ((0, shifted, 2), (shifted, used, 0)):
            if low < high:
                some = along_y(table, jnp.concatenate([o[low:high] for o in own], axis=0))
                cells[s * planes : (s + 1) * planes, low:high] = some.reshape(planes, high - low, total_y)
    index = lax.broadcasted_iota(jnp.int32, (total_z * tile, 1), 0)
    z_sq = wave_sq(index // tile, total_z)
    y_sq = wave_sq(lax.broadcasted_iota(jnp.int32, (1, total_y), 1), total_y)
    own, scale = [], []
    for start in range(0, used, tile):
        own.append(cells[:, start : start + tile, :].reshape(total_z * tile, total_y))
        x_sq = wave_sq(first + offsets[start // tile] + lax.rem(index, tile), x_length)
        scale.append((z_sq + x_sq + y_sq) * 256.0 + 1.0)
    own = along_z(0, jnp.concatenate(own, axis=1))
    own = along_z(1, own / jnp.concatenate(scale, axis=1))
    for k, start in enumerate(range(0, used, tile)):
        part = own[:, k * total_y : (k + 1) * total_y]
        cells[:, start : start + tile, :] = part.reshape(total_z, tile, total_y)
    for s in range(slabs):
        own = along_y(1, cells[s * planes : (s + 1) * planes].reshape(planes * used, total_y))
        for f in range(0, planes // fold):
            blocks = swap_blocks([own[z * used : (z + 1) * used] for z in range(f * fold, (f + 1) * fold)])
            for q in range(subs):
                out[s * subs + q, :, f * total_y : (f + 1) * total_y] = blocks[q]


def solve_yx_kernel(subs, x_length, place, spectra, basis_z, basis_y, out, cells):
    devices = out.shape[0]
    part = x_length // devices
    offsets = list(range(0, part, 8)) + list(range(0, out.shape[1] - part, 8))
    solve((place[0] * subs + place[1]) * part, x_length, offsets, part, subs, spectra, basis_z, basis_y, out, cells)


def solve_zx_kernel(slabs, subs, x_length, place, *refs):
    received, refs = refs[:subs], refs[subs:]
    basis_z, basis_y, sends, (spectra, cells) = refs[0], refs[1], refs[2 : 2 + slabs], refs[2 + slabs :]
    part = x_length // (slabs * subs)
    offsets = list(range(0, part, 8)) + list(range(2 * part - received[0].shape[1], part, 8))
    for e in range(subs):
        for d in range(slabs):
            spectra[around(place[0] - d, slabs) * subs + around(place[1] - e, subs)] = received[e][d]
    solve((place[0] * subs + place[1]) * part, x_length, offsets, 0, subs, spectra, basis_z, basis_y, spectra, cells)
    for d in range(slabs):
        for e in range(subs):
            sends[d][e] = spectra[around(place[0] + d, slabs) * subs + around(place[1] + e, subs)]


def moved(spectra, velocity, basis):
    smoothed = times(split(spectra.T), (basis[0], basis[1]), ((1,), (0,)))
    return 0.5 * (velocity - 32.0 * smoothed.reshape(velocity.shape))


def update_z_kernel(slabs, subs, place, basis, velocity, *refs):
    received, (out, kept, gathered) = refs[:subs], refs[subs:]
    part = received[0].shape[1] - kept.shape[1]
    for e in range(subs):
        for d in range(slabs):
            index = around(place[0] - d, slabs) * subs + around(place[1] - e, subs)
            gathered[pl.ds(pl.multiple_of(index * part, part), part), :] = received[e][d, :part]
            kept[index] = received[e][d, part:]
    out[...] = moved(gathered[...], velocity[0], basis)


def update_kernel(spectra, basis, velocity, updated, kept, out, result, done):
    devices, _, area = kept.shape
    part = (spectra.shape[1] + kept.shape[1]) // 2
    leaving = [pltpu.make_async_copy(updated, out.at[0], done.at[0])]
    leaving[0].start()
    for a in range(2):
        if a:
            own = jnp.concatenate([spectra[:, part:, :], kept[...]], axis=1)
        else:
            own = spectra[:, :part, :]
        result[a] = moved(own.reshape(devices * part, area), velocity[a + 1], basis)
        leaving.append(pltpu.make_async_copy(result.at[a], out.at[a + 1], done.at[a + 1]))
        leaving[-1].start()
    for copy in leaving:
        copy.wait()


def place_kernel(slabs, place, *refs):
    received, warped = refs[:slabs], refs[slabs]
    for step in range(slabs):
        block = pl.ds(pl.multiple_of(around(place[0] - step, slabs) * BLOCK, BLOCK), BLOCK)
        warped[:, :, block] = received[step][1:-1]


def local_blocks(velocity, template, moving, stiffness, fetch_plane, tissue):
    planes, rows, x_length = moving.shape
    slabs, subs = lax.axis_size("slab"), lax.axis_size("sub")
    total_z, total_y = planes * slabs, rows * subs
    devices = slabs * subs
    part = x_length // devices
    area = planes * rows
    place = jnp.stack([lax.axis_index("slab"), lax.axis_index("sub")])
    bf16, f16, f32 = jnp.bfloat16, jnp.float16, jnp.float32

    def shape(dims, kind=f32):
        return jax.ShapeDtypeStruct(dims, kind)

    def scatter(sends, axis):
        count = lax.axis_size(axis)
        return [sends[0]] + [
            lax.ppermute(sends[d], axis, [(i, (i + d) % count) for i in range(count)]) for d in range(1, count)
        ]

    def exchange(values):
        return lax.all_to_all(values, ("slab", "sub"), split_axis=0, concat_axis=0, tiled=True)

    fetch, marks = fetch_plane.swapaxes(1, 2), tissue.swapaxes(1, 2)
    coefficient = call(coefficient_kernel, shape(moving.shape), stiffness, marks, flops=1 << 30)
    sends = call(
        functools.partial(send_columns_kernel, slabs),
        [shape(((rows + 2) * planes, BLOCK), bf16)] * slabs,
        place,
        moving,
        fetch,
    )
    sends = call(
        functools.partial(pick_kernel, slabs),
        [shape((planes + 2, rows, BLOCK), bf16)] * slabs,
        place,
        *scatter(sends, "slab"),
        flops=1 << 30,
    )
    received = scatter(sends, "slab")
    basis_x = in_two(8.0 * real_basis(x_length))
    basis_z = np.kron(real_basis(total_z), np.eye(8))
    basis_z = np.concatenate([in_two(basis_z), in_two(basis_z.T)])
    basis_y = real_basis(total_y)
    basis_y = np.concatenate([in_two(b) for b in (basis_y.T, basis_y, np.roll(basis_y.T, -1, 0))])
    cut = part // 2
    with_z, with_y = 2 * part - cut, part + cut
    first, image, weight, chain, kept = call(
        functools.partial(force_zx_kernel, slabs, subs),
        [
            shape((3 * planes, x_length)),
            shape(moving.shape),
            shape(moving.shape),
            shape((slabs, subs, with_z, area)),
            shape((devices, cut, area)),
        ],
        place,
        *received,
        template,
        coefficient,
        basis_x,
        scratch=[pltpu.VMEM((planes + 2, rows, x_length), f32), pltpu.VMEM((2, x_length, area), f32)],
        flops=3 << 30,
    )
    beyond = lax.ppermute(first, "sub", [((i + 1) % subs, i) for i in range(subs)])
    chain = chain.astype(f16)
    chain = scatter([chain[d] for d in range(slabs)], "slab")
    later, *chain = lax.optimization_barrier((place, *chain))
    warped = call(functools.partial(place_kernel, slabs), shape(moving.shape, bf16), later, *received)
    chain = scatter([jnp.stack([r[e] for r in chain]) for e in range(subs)], "sub")
    spectra = call(
        force_y_kernel,
        shape((devices, with_y, area)),
        beyond,
        image,
        weight,
        basis_x,
        kept,
        flops=2 << 30,
    )
    spectra = exchange(spectra.astype(f16))
    chain = call(
        functools.partial(solve_zx_kernel, slabs, subs, x_length),
        [shape((subs, with_z, area))] * slabs,
        place,
        *[r.astype(f32) for r in chain],
        basis_z,
        basis_y,
        scratch=[pltpu.VMEM((devices, with_z, area), f32), pltpu.VMEM((total_z, with_z, total_y), f32)],
        flops=2 << 30,
    )
    chain, spectra, warped = lax.optimization_barrier((chain, spectra, warped))
    chain = scatter([r.astype(f16) for r in chain], "slab")
    chain = scatter([jnp.stack([r[e] for r in chain]) for e in range(subs)], "sub")
    spectra = call(
        functools.partial(solve_yx_kernel, subs, x_length),
        shape((devices, with_y, area)),
        place,
        spectra.astype(f32),
        basis_z,
        basis_y,
        scratch=[pltpu.VMEM((total_z, with_y, total_y), f32)],
        flops=2 << 30,
    )
    spectra = exchange(spectra.astype(f16))
    basis_x = in_two(real_basis(x_length))
    updated, kept = call(
        functools.partial(update_z_kernel, slabs, subs),
        [shape(moving.shape), shape((devices, part - cut, area))],
        place,
        basis_x,
        velocity,
        *[r.astype(f32) for r in chain],
        scratch=[pltpu.VMEM((x_length, area), f32)],
        flops=1 << 30,
    )
    new_velocity = call(
        update_kernel,
        shape(velocity.shape),
        spectra.astype(f32),
        basis_x,
        velocity,
        updated,
        kept,
        scratch=[pltpu.VMEM((2,) + moving.shape, f32), pltpu.SemaphoreType.DMA((3,))],
        flops=2 << 30,
        stays=1,
    )
    return (new_velocity, warped)


def local(velocity, template, moving, stiffness, fetch_plane, tissue):
    planes, rows, x_length = moving.shape
    slabs, subs = lax.axis_size("slab"), lax.axis_size("sub")
    fits = (
        x_length == slabs * BLOCK
        and planes == 8
        and planes * slabs * 8 == 256
        and rows % 16 == 0
        and rows * subs == BLOCK
        and subs == 4
        and x_length % (32 * slabs * subs) == 0
    )
    run = local_blocks if fits else local_general
    return run(velocity, template, moving, stiffness, fetch_plane, tissue)


def solution(mesh):
    placed = (
        P(None, ("groups", "slab"), "sub", None),
        P(("groups", "slab"), "sub", None),
        P(("groups", "slab"), "sub", None),
        P(("groups", "slab"), "sub", None),
        P(("groups", "slab"), "sub", None),
        P(("groups", "slab"), "sub", None),
    )
    return jax.shard_map(
        local,
        mesh=mesh,
        in_specs=placed,
        out_specs=(P(None, ("groups", "slab"), "sub", None), P(("groups", "slab"), "sub", None)),
        check_vma=False,
    )
```

```python
import functools

import jax
import jax.numpy as jnp
import numpy as np
from jax import lax
from jax.experimental import pallas as pl
from jax.experimental.pallas import tpu as pltpu
from jax.sharding import PartitionSpec as P

BLOCK = 128


def extended(cells, sides, width):
    for axis, dim in sides:
        count = lax.axis_size(axis)
        head = lax.slice_in_dim(cells, 0, width, axis=dim)
        tail = lax.slice_in_dim(cells, cells.shape[dim] - width, cells.shape[dim], axis=dim)
        cells = jnp.concatenate(
            [
                lax.ppermute(tail, axis, [(i, (i + 1) % count) for i in range(count)]),
                cells,
                lax.ppermute(head, axis, [((i + 1) % count, i) for i in range(count)]),
            ],
            axis=dim,
        )
    return cells


def tables(length):
    wave_ids = jnp.arange(length, dtype=jnp.int32)
    phase = wave_ids[:, None] * wave_ids[None, :] % length
    angle = 2.0 * jnp.pi / length * phase.astype(jnp.float32)
    return (jnp.cos(angle), jnp.sin(angle))


def apply_along(values, matrix, axis_id):
    result = lax.dot_general(
        values,
        matrix,
        (((axis_id,), (0,)), ((), ())),
        precision=lax.Precision.HIGHEST,
        preferred_element_type=jnp.float32,
    )
    return jnp.moveaxis(result, -1, axis_id)


def forward_along(values_pair, axis_id):
    real_part, imag_part = values_pair
    cosine, sine = tables(real_part.shape[axis_id])
    return (
        apply_along(real_part, cosine, axis_id) + apply_along(imag_part, sine, axis_id),
        apply_along(imag_part, cosine, axis_id) - apply_along(real_part, sine, axis_id),
    )


def inverse_along(values_pair, axis_id):
    real_part, imag_part = values_pair
    length = real_part.shape[axis_id]
    cosine, sine = tables(length)
    scale = 1.0 / length
    return (
        (apply_along(real_part, cosine, axis_id) - apply_along(imag_part, sine, axis_id)) * scale,
        (apply_along(imag_part, cosine, axis_id) + apply_along(real_part, sine, axis_id)) * scale,
    )


def symbol_sq(length, first_id, span):
    wave_ids = first_id + jnp.arange(span, dtype=jnp.int32)
    signed = jnp.where(wave_ids < length // 2, wave_ids, wave_ids - length).astype(jnp.float32)
    wave = 2.0 * jnp.pi / length * signed
    return wave * wave


def local_general(velocity, template, moving, stiffness, fetch_plane, tissue):
    planes_dev, rows_dev, x_length = moving.shape
    blocks_x = x_length // BLOCK
    slabs = lax.axis_size("slab")
    subs = lax.axis_size("sub")
    my_slab = lax.axis_index("slab")
    my_sub = lax.axis_index("sub")
    per_dev = planes_dev * rows_dev * blocks_x
    capacity = 2 * per_dev // slabs
    source_plane = fetch_plane.reshape(-1)
    block_ids = jnp.arange(per_dev, dtype=jnp.int32)
    row_of = block_ids // blocks_x % rows_dev
    column_of = block_ids % blocks_x
    moving_rows = moving.reshape(per_dev, BLOCK)
    holder = source_plane // planes_dev
    within = (source_plane % planes_dev * rows_dev + row_of) * blocks_x + column_of
    matches = (holder[:, None] == jnp.arange(slabs, dtype=jnp.int32)[None, :]).astype(jnp.int32)
    earlier = jnp.sum((jnp.cumsum(matches, axis=0) - matches) * matches, axis=1)
    target = holder * capacity + earlier
    wanted = (
        jnp.zeros((slabs * capacity,), jnp.int32).at[target].set(within).reshape(slabs, capacity)
    )
    asked = lax.all_to_all(wanted, "slab", split_axis=0, concat_axis=0, tiled=True)
    fetched = moving_rows[asked.reshape(-1)].reshape(asked.shape + (BLOCK,))
    replies = lax.all_to_all(fetched, "slab", split_axis=0, concat_axis=0, tiled=True)
    warped_rows = replies.reshape(slabs * capacity, BLOCK)[target]
    warped = warped_rows.reshape(planes_dev, rows_dev, x_length)
    padded = extended(warped, (("slab", 0), ("sub", 1)), 1).astype(jnp.float32)
    image = padded[1:-1, 1:-1]
    grad_z = 0.5 * (padded[2:, 1:-1] - padded[:-2, 1:-1])
    grad_y = 0.5 * (padded[1:-1, 2:] - padded[1:-1, :-2])
    grad_x = 0.5 * (jnp.roll(image, -1, 2) - jnp.roll(image, 1, 2))
    residual = image - template.astype(jnp.float32)
    tissue_vox = jnp.repeat(tissue.astype(jnp.float32), BLOCK, axis=2)
    weight_field = tissue_vox * stiffness * residual
    force = jnp.stack([weight_field * grad_z, weight_field * grad_y, weight_field * grad_x])
    cos_x, sin_x = tables(x_length)
    real_part = apply_along(force, cos_x, 3)
    imag_part = -apply_along(force, sin_x, 3)
    moved = (
        lax.all_to_all(real_part, "sub", split_axis=3, concat_axis=2, tiled=True),
        lax.all_to_all(imag_part, "sub", split_axis=3, concat_axis=2, tiled=True),
    )
    moved = forward_along(moved, 2)
    moved = (
        lax.all_to_all(moved[0], "slab", split_axis=2, concat_axis=1, tiled=True),
        lax.all_to_all(moved[1], "slab", split_axis=2, concat_axis=1, tiled=True),
    )
    moved = forward_along(moved, 1)
    total_z = moved[0].shape[1]
    y_span = moved[0].shape[2]
    x_span = moved[0].shape[3]
    factor = 1.0 / (
        symbol_sq(total_z, 0, total_z)[:, None, None]
        + symbol_sq(y_span * slabs, my_slab * y_span, y_span)[None, :, None]
        + symbol_sq(x_span * subs, my_sub * x_span, x_span)[None, None, :]
        + 1.0 / 256.0
    )
    moved = (moved[0] * factor, moved[1] * factor)
    moved = inverse_along(moved, 1)
    moved = (
        lax.all_to_all(moved[0], "slab", split_axis=1, concat_axis=2, tiled=True),
        lax.all_to_all(moved[1], "slab", split_axis=1, concat_axis=2, tiled=True),
    )
    moved = inverse_along(moved, 2)
    real_part, imag_part = (
        lax.all_to_all(moved[0], "sub", split_axis=2, concat_axis=3, tiled=True),
        lax.all_to_all(moved[1], "sub", split_axis=2, concat_axis=3, tiled=True),
    )
    smoothed = (apply_along(real_part, cos_x, 3) - apply_along(imag_part, sin_x, 3)) * (
        1.0 / x_length
    )
    new_velocity = 0.5 * (velocity - smoothed)
    return (new_velocity, warped)


VMEM_BYTES = 24 * 1024 * 1024


def real_basis(length):
    index = np.arange(length)
    half = length // 2
    wave = np.where(index <= half, index, index - half)[:, None]
    angle = 2.0 * np.pi / length * (wave * index[None, :] % length)
    rows = np.where(index[:, None] <= half, np.cos(angle), np.sin(angle)) * np.sqrt(2.0 / length)
    rows[0] /= np.sqrt(2.0)
    rows[half] /= np.sqrt(2.0)
    return rows


def in_two(table):
    high = np.asarray(table, np.float32).astype(jnp.bfloat16)
    low = (np.asarray(table, np.float64) - high.astype(np.float64)).astype(jnp.bfloat16)
    return np.stack([high, low])


def split(values):
    high = values.astype(jnp.bfloat16)
    return high, (values - high.astype(jnp.float32)).astype(jnp.bfloat16)


def times(left, right, dims):
    def one(a, b):
        return lax.dot_general(a, b, (dims, ((), ())), preferred_element_type=jnp.float32)

    return one(left[0], right[0]) + (one(left[0], right[1]) + one(left[1], right[0]))


def wave_sq(index, length):
    wave = jnp.where(index <= length // 2, index, index - length // 2).astype(jnp.float32)
    wave = wave * (2.0 * np.pi / length)
    return wave * wave


def around(value, count):
    return lax.rem(value + 2 * count, count)


def call(kernel, out_shape, *arguments, scratch=(), flops=0, stays=0):
    places = [
        pl.BlockSpec(memory_space=pltpu.HBM if isinstance(a, tuple) else pltpu.SMEM if a.ndim == 1 else pltpu.VMEM)
        for a in arguments
    ]
    arguments = [a[0] if isinstance(a, tuple) else a for a in arguments]
    out_places = [
        pl.BlockSpec(memory_space=pltpu.HBM if k < stays else pltpu.VMEM)
        for k in range(len(jax.tree.leaves(out_shape)))
    ]
    nbytes = sum(a.size * a.dtype.itemsize for a in arguments + jax.tree.leaves(out_shape))
    return pl.pallas_call(
        kernel,
        out_shape=out_shape,
        in_specs=places,
        out_specs=jax.tree.unflatten(jax.tree.structure(out_shape), out_places),
        scratch_shapes=list(scratch),
        compiler_params=pltpu.CompilerParams(vmem_limit_bytes=VMEM_BYTES),
        cost_estimate=pl.CostEstimate(flops=flops, bytes_accessed=nbytes, transcendentals=0),
    )(*arguments)


def by_row(ref, rows):
    cells = jnp.concatenate([ref[z].astype(jnp.float32) for z in range(ref.shape[0])], axis=0)
    cells = jnp.concatenate([cells, jnp.zeros((cells.shape[0], BLOCK - rows), jnp.float32)], axis=1)
    cells = jnp.concatenate([cells, jnp.zeros((BLOCK - cells.shape[0], BLOCK), jnp.float32)], axis=0)
    return cells.T[:rows]


def send_columns_kernel(slabs, place, moving, fetch, *sends):
    planes, rows, _ = moving.shape
    for step, send in enumerate(sends):
        to = around(place[0] + step, slabs)
        block = pl.ds(pl.multiple_of(to * BLOCK, BLOCK), BLOCK)
        for z in range(planes):
            send[z * rows : (z + 1) * rows] = moving[z, :, block]
        asked = jnp.concatenate([fetch[z, pl.ds(to, 1), :] for z in range(planes)] * 2, axis=0).astype(jnp.float32)
        asked = jnp.concatenate([asked, jnp.zeros((2 * planes, BLOCK - rows), jnp.float32)], axis=1)
        send[planes * rows :] = asked.astype(jnp.bfloat16)


def pick_kernel(slabs, place, *refs):
    received, sends = refs[:slabs], refs[slabs:]
    planes, rows = sends[0].shape[0] - 2, sends[0].shape[1]
    me = place[0]
    group = 4

    def name(other, plane):
        number = (around(me - other, slabs) * planes).astype(jnp.float32) + float(plane)
        return jnp.full((rows, BLOCK), number, jnp.float32).astype(jnp.bfloat16)

    for step in range(slabs):
        names = received[step][planes * rows :].astype(jnp.float32)[:planes]
        names = jnp.concatenate([names, jnp.zeros((BLOCK - planes, BLOCK), jnp.float32)], axis=0).T[:rows]
        for start in range(0, planes, group):
            wanted = [
                jnp.broadcast_to(names[:, z : z + 1], (rows, BLOCK)).astype(jnp.bfloat16)
                for z in range(start, start + group)
            ]
            found = [jnp.zeros((rows, BLOCK), jnp.bfloat16) for _ in range(group)]
            for other in range(slabs):
                for plane in range(planes):
                    values = received[other][plane * rows : (plane + 1) * rows]
                    own = name(other, plane)
                    found = [jnp.where(w == own, values, f) for w, f in zip(wanted, found)]
            back = (slabs - step) % slabs
            for z in range(group):
                own = start + z
                sends[back][own + 1] = found[z]
                if own == 0:
                    sends[(back - 1) % slabs][planes + 1] = found[z]
                if own == planes - 1:
                    sends[(back + 1) % slabs][0] = found[z]


def coefficient_kernel(stiffness, tissue, out):
    planes, rows, x_length = stiffness.shape
    blocks = x_length // BLOCK
    marks = by_row(tissue, rows)
    for z in range(planes):
        marked = jnp.concatenate(
            [
                jnp.broadcast_to(marks[:, z * blocks + b : z * blocks + b + 1], (rows, BLOCK))
                for b in range(blocks)
            ],
            axis=1,
        )
        out[z] = 4.0 * marked * stiffness[z]


def force_zx_kernel(slabs, subs, place, *refs):
    received, refs = refs[:slabs], refs[slabs:]
    template, coefficient, basis, first, image, weight, spectra, kept, planes_of, wide = refs
    planes, rows, x_length = template.shape
    for step in range(slabs):
        block = pl.ds(pl.multiple_of(around(place[0] - step, slabs) * BLOCK, BLOCK), BLOCK)
        planes_of[:, :, block] = received[step][...].astype(jnp.float32)
    forces = [[], []]
    for z in range(planes):
        here = planes_of[z + 1]
        own = coefficient[z] * (here - template[z].astype(jnp.float32))
        image[z] = here
        weight[z] = own
        first[z : z + 1] = here[0:1]
        first[planes + z : planes + z + 1] = here[1:2]
        first[2 * planes + z : 2 * planes + z + 1] = own[0:1]
        forces[0].append(own * (planes_of[z + 2] - planes_of[z]))
        forces[1].append(own * (pltpu.roll(here, x_length - 1, 1) - pltpu.roll(here, 1, 1)))
    for a in range(2):
        force = split(jnp.concatenate(forces[a], axis=0))
        wide[a] = times((basis[0], basis[1]), force, ((1,), (1,)))
    part = x_length // (slabs * subs)
    cut = kept.shape[1]
    for d in range(slabs):
        for e in range(subs):
            start = (around(place[0] + d, slabs) * subs + around(place[1] + e, subs)) * part
            spectra[d, e, :part] = wide[0, pl.ds(pl.multiple_of(start, part), part), :]
            spectra[d, e, part:] = wide[1, pl.ds(pl.multiple_of(start + cut, 8), part - cut), :]
    for k in range(slabs * subs):
        kept[k] = wide[1, k * part : k * part + cut, :]


def force_y_kernel(beyond, image, weight, basis, kept, spectra):
    planes, rows, x_length = image.shape
    row = lax.broadcasted_iota(jnp.int32, (rows, x_length), 0)
    force = []
    for z in range(planes):
        here = image[z]
        after = jnp.where(row == rows - 2, beyond[z : z + 1, :], pltpu.roll(here, rows - 2, 0))
        after = jnp.where(row == rows - 1, beyond[planes + z : planes + z + 1, :], after)
        own = pltpu.roll(weight[z], rows - 1, 0)
        own = jnp.where(row == rows - 1, beyond[2 * planes + z : 2 * planes + z + 1, :], own)
        force.append(own * (after - here))
    devices = spectra.shape[0]
    part = x_length // devices
    spectrum = times((basis[0], basis[1]), split(jnp.concatenate(force, axis=0)), ((1,), (1,)))
    spectra[:, :part, :] = spectrum.reshape(devices, part, planes * rows)
    spectra[:, part:, :] = kept[...]


def swap_blocks(values):
    width = values[0].shape[1]
    lane = lax.broadcasted_iota(jnp.int32, values[0].shape, 1)
    lower, even = lane < width // 2, lax.rem(lane // (width // 4), 2) == 0

    def turn(own, count):
        return pltpu.roll(own, count * (width // 4), 1)

    a, b, c, d = values
    a, c = jnp.where(lower, a, turn(c, 2)), jnp.where(lower, turn(a, 2), c)
    b, d = jnp.where(lower, b, turn(d, 2)), jnp.where(lower, turn(b, 2), d)
    return [
        jnp.where(even, a, turn(b, 1)),
        jnp.where(even, turn(a, 3), b),
        jnp.where(even, c, turn(d, 1)),
        jnp.where(even, turn(c, 3), d),
    ]


def solve(first, x_length, offsets, shifted, subs, spectra, basis_z, basis_y, out, cells):
    devices, used, area = spectra.shape
    total_z, _, total_y = cells.shape
    slabs = devices // subs
    planes, rows = total_z // slabs, total_y // subs
    fold = total_y // rows
    tile = 8

    def along_y(k, values):
        high, low = basis_y[2 * k], basis_y[2 * k + 1]
        four = jnp.concatenate(
            [jnp.concatenate([high, low], axis=1), jnp.concatenate([high, jnp.zeros_like(low)], axis=1)], axis=0
        )
        sums = jnp.dot(jnp.concatenate(split(values), axis=1), four, preferred_element_type=jnp.float32)
        return sums[:, :total_y] + sums[:, total_y:]

    def along_z(k, values):
        high, low = basis_z[2 * k], basis_z[2 * k + 1]
        parts = split(values)
        return jnp.dot(
            jnp.concatenate([high, high, low], axis=1),
            jnp.concatenate([parts[0], parts[1], parts[0]], axis=0),
            preferred_element_type=jnp.float32,
        )

    for s in range(slabs):
        own = []
        for f in range(0, planes // fold):
            lanes = slice(f * total_y, (f + 1) * total_y)
            own += swap_blocks([spectra[s * subs + q][:, lanes] for q in range(subs)])
        for low, high, table in ((0, shifted, 2), (shifted, used, 0)):
            if low < high:
                some = along_y(table, jnp.concatenate([o[low:high] for o in own], axis=0))
                cells[s * planes : (s + 1) * planes, low:high] = some.reshape(planes, high - low, total_y)
    index = lax.broadcasted_iota(jnp.int32, (total_z * tile, 1), 0)
    z_sq = wave_sq(index // tile, total_z)
    y_sq = wave_sq(lax.broadcasted_iota(jnp.int32, (1, total_y), 1), total_y)
    own, scale = [], []
    for start in range(0, used, tile):
        own.append(cells[:, start : start + tile, :].reshape(total_z * tile, total_y))
        x_sq = wave_sq(first + offsets[start // tile] + lax.rem(index, tile), x_length)
        scale.append((z_sq + x_sq + y_sq) * 256.0 + 1.0)
    own = along_z(0, jnp.concatenate(own, axis=1))
    own = along_z(1, own / jnp.concatenate(scale, axis=1))
    for k, start in enumerate(range(0, used, tile)):
        part = own[:, k * total_y : (k + 1) * total_y]
        cells[:, start : start + tile, :] = part.reshape(total_z, tile, total_y)
    for s in range(slabs):
        own = along_y(1, cells[s * planes : (s + 1) * planes].reshape(planes * used, total_y))
        for f in range(0, planes // fold):
            blocks = swap_blocks([own[z * used : (z + 1) * used] for z in range(f * fold, (f + 1) * fold)])
            for q in range(subs):
                out[s * subs + q, :, f * total_y : (f + 1) * total_y] = blocks[q]


def solve_yx_kernel(subs, x_length, place, spectra, basis_z, basis_y, out, cells):
    devices = out.shape[0]
    part = x_length // devices
    offsets = list(range(0, part, 8)) + list(range(0, out.shape[1] - part, 8))
    solve((place[0] * subs + place[1]) * part, x_length, offsets, part, subs, spectra, basis_z, basis_y, out, cells)


def solve_zx_kernel(slabs, subs, x_length, place, *refs):
    received, refs = refs[:subs], refs[subs:]
    basis_z, basis_y, sends, (spectra, cells) = refs[0], refs[1], refs[2 : 2 + slabs], refs[2 + slabs :]
    part = x_length // (slabs * subs)
    offsets = list(range(0, part, 8)) + list(range(2 * part - received[0].shape[1], part, 8))
    for e in range(subs):
        for d in range(slabs):
            spectra[around(place[0] - d, slabs) * subs + around(place[1] - e, subs)] = received[e][d]
    solve((place[0] * subs + place[1]) * part, x_length, offsets, 0, subs, spectra, basis_z, basis_y, spectra, cells)
    for d in range(slabs):
        for e in range(subs):
            sends[d][e] = spectra[around(place[0] + d, slabs) * subs + around(place[1] + e, subs)]


def moved(spectra, velocity, basis):
    smoothed = times(split(spectra.T), (basis[0], basis[1]), ((1,), (0,)))
    return 0.5 * (velocity - 32.0 * smoothed.reshape(velocity.shape))


def update_z_kernel(slabs, subs, place, basis, velocity, *refs):
    received, (out, kept, gathered) = refs[:subs], refs[subs:]
    part = received[0].shape[1] - kept.shape[1]
    for e in range(subs):
        for d in range(slabs):
            index = around(place[0] - d, slabs) * subs + around(place[1] - e, subs)
            gathered[pl.ds(pl.multiple_of(index * part, part), part), :] = received[e][d, :part]
            kept[index] = received[e][d, part:]
    out[...] = moved(gathered[...], velocity[0], basis)


def update_kernel(spectra, basis, velocity, updated, kept, out, result, done):
    devices, _, area = kept.shape
    part = (spectra.shape[1] + kept.shape[1]) // 2
    leaving = [pltpu.make_async_copy(updated, out.at[0], done.at[0])]
    leaving[0].start()
    for a in range(2):
        if a:
            own = jnp.concatenate([spectra[:, part:, :], kept[...]], axis=1)
        else:
            own = spectra[:, :part, :]
        result[a] = moved(own.reshape(devices * part, area), velocity[a + 1], basis)
        leaving.append(pltpu.make_async_copy(result.at[a], out.at[a + 1], done.at[a + 1]))
        leaving[-1].start()
    for copy in leaving:
        copy.wait()


def place_kernel(slabs, place, *refs):
    received, warped = refs[:slabs], refs[slabs]
    for step in range(slabs):
        block = pl.ds(pl.multiple_of(around(place[0] - step, slabs) * BLOCK, BLOCK), BLOCK)
        warped[:, :, block] = received[step][1:-1]


def local_blocks(velocity, template, moving, stiffness, fetch_plane, tissue):
    planes, rows, x_length = moving.shape
    slabs, subs = lax.axis_size("slab"), lax.axis_size("sub")
    total_z, total_y = planes * slabs, rows * subs
    devices = slabs * subs
    part = x_length // devices
    area = planes * rows
    place = jnp.stack([lax.axis_index("slab"), lax.axis_index("sub")])
    bf16, f16, f32 = jnp.bfloat16, jnp.float16, jnp.float32

    def shape(dims, kind=f32):
        return jax.ShapeDtypeStruct(dims, kind)

    def scatter(sends, axis):
        count = lax.axis_size(axis)
        return [sends[0]] + [
            lax.ppermute(sends[d], axis, [(i, (i + d) % count) for i in range(count)]) for d in range(1, count)
        ]

    def exchange(values):
        return lax.all_to_all(values, ("slab", "sub"), split_axis=0, concat_axis=0, tiled=True)

    fetch, marks = fetch_plane.swapaxes(1, 2), tissue.swapaxes(1, 2)
    coefficient = call(coefficient_kernel, shape(moving.shape), stiffness, marks, flops=1 << 30)
    sends = call(
        functools.partial(send_columns_kernel, slabs),
        [shape(((rows + 2) * planes, BLOCK), bf16)] * slabs,
        place,
        moving,
        fetch,
    )
    sends = call(
        functools.partial(pick_kernel, slabs),
        [shape((planes + 2, rows, BLOCK), bf16)] * slabs,
        place,
        *scatter(sends, "slab"),
        flops=1 << 30,
    )
    received = scatter(sends, "slab")
    basis_x = in_two(real_basis(x_length))
    basis_z = np.kron(real_basis(total_z), np.eye(8))
    basis_z = np.concatenate([in_two(basis_z), in_two(basis_z.T)])
    basis_y = real_basis(total_y)
    basis_y = np.concatenate([in_two(b) for b in (basis_y.T, basis_y, np.roll(basis_y.T, -1, 0))])
    cut = part // 2
    with_z, with_y = 2 * part - cut, part + cut
    first, image, weight, chain, kept = call(
        functools.partial(force_zx_kernel, slabs, subs),
        [
            shape((3 * planes, x_length)),
            shape(moving.shape),
            shape(moving.shape),
            shape((slabs, subs, with_z, area)),
            shape((devices, cut, area)),
        ],
        place,
        *received,
        template,
        coefficient,
        basis_x,
        scratch=[pltpu.VMEM((planes + 2, rows, x_length), f32), pltpu.VMEM((2, x_length, area), f32)],
        flops=3 << 30,
    )
    beyond = lax.ppermute(first, "sub", [((i + 1) % subs, i) for i in range(subs)])
    chain = chain.astype(f16)
    chain = scatter([chain[d] for d in range(slabs)], "slab")
    later, *chain = lax.optimization_barrier((place, *chain))
    warped = call(functools.partial(place_kernel, slabs), shape(moving.shape, bf16), later, *received)
    chain = scatter([jnp.stack([r[e] for r in chain]) for e in range(subs)], "sub")
    spectra = call(
        force_y_kernel,
        shape((devices, with_y, area)),
        beyond,
        image,
        weight,
        basis_x,
        kept,
        flops=2 << 30,
    )
    spectra = exchange(spectra.astype(f16))
    chain = call(
        functools.partial(solve_zx_kernel, slabs, subs, x_length),
        [shape((subs, with_z, area))] * slabs,
        place,
        *[r.astype(f32) for r in chain],
        basis_z,
        basis_y,
        scratch=[pltpu.VMEM((devices, with_z, area), f32), pltpu.VMEM((total_z, with_z, total_y), f32)],
        flops=2 << 30,
    )
    chain, spectra, warped = lax.optimization_barrier((chain, spectra, warped))
    chain = scatter([r.astype(f16) for r in chain], "slab")
    chain = scatter([jnp.stack([r[e] for r in chain]) for e in range(subs)], "sub")
    spectra = call(
        functools.partial(solve_yx_kernel, subs, x_length),
        shape((devices, with_y, area)),
        place,
        spectra.astype(f32),
        basis_z,
        basis_y,
        scratch=[pltpu.VMEM((total_z, with_y, total_y), f32)],
        flops=2 << 30,
    )
    spectra = exchange(spectra.astype(f16))
    updated, kept = call(
        functools.partial(update_z_kernel, slabs, subs),
        [shape(moving.shape), shape((devices, part - cut, area))],
        place,
        basis_x,
        velocity,
        *[r.astype(f32) for r in chain],
        scratch=[pltpu.VMEM((x_length, area), f32)],
        flops=1 << 30,
    )
    new_velocity = call(
        update_kernel,
        shape(velocity.shape),
        spectra.astype(f32),
        basis_x,
        velocity,
        updated,
        kept,
        scratch=[pltpu.VMEM((2,) + moving.shape, f32), pltpu.SemaphoreType.DMA((3,))],
        flops=2 << 30,
        stays=1,
    )
    return (new_velocity, warped)


def local(velocity, template, moving, stiffness, fetch_plane, tissue):
    planes, rows, x_length = moving.shape
    slabs, subs = lax.axis_size("slab"), lax.axis_size("sub")
    fits = (
        x_length == slabs * BLOCK
        and planes == 8
        and planes * slabs * 8 == 256
        and rows % 16 == 0
        and rows * subs == BLOCK
        and subs == 4
        and x_length % (32 * slabs * subs) == 0
    )
    run = local_blocks if fits else local_general
    return run(velocity, template, moving, stiffness, fetch_plane, tissue)


def solution(mesh):
    placed = (
        P(None, ("groups", "slab"), "sub", None),
        P(("groups", "slab"), "sub", None),
        P(("groups", "slab"), "sub", None),
        P(("groups", "slab"), "sub", None),
        P(("groups", "slab"), "sub", None),
        P(("groups", "slab"), "sub", None),
    )
    return jax.shard_map(
        local,
        mesh=mesh,
        in_specs=placed,
        out_specs=(P(None, ("groups", "slab"), "sub", None), P(("groups", "slab"), "sub", None)),
        check_vma=False,
    )
```

```python
import functools

import jax
import jax.numpy as jnp
import numpy as np
from jax import lax
from jax.experimental import pallas as pl
from jax.experimental.pallas import tpu as pltpu
from jax.sharding import PartitionSpec as P

BLOCK = 128


def extended(cells, sides, width):
    for axis, dim in sides:
        count = lax.axis_size(axis)
        head = lax.slice_in_dim(cells, 0, width, axis=dim)
        tail = lax.slice_in_dim(cells, cells.shape[dim] - width, cells.shape[dim], axis=dim)
        cells = jnp.concatenate(
            [
                lax.ppermute(tail, axis, [(i, (i + 1) % count) for i in range(count)]),
                cells,
                lax.ppermute(head, axis, [((i + 1) % count, i) for i in range(count)]),
            ],
            axis=dim,
        )
    return cells


def tables(length):
    wave_ids = jnp.arange(length, dtype=jnp.int32)
    phase = wave_ids[:, None] * wave_ids[None, :] % length
    angle = 2.0 * jnp.pi / length * phase.astype(jnp.float32)
    return (jnp.cos(angle), jnp.sin(angle))


def apply_along(values, matrix, axis_id):
    result = lax.dot_general(
        values,
        matrix,
        (((axis_id,), (0,)), ((), ())),
        precision=lax.Precision.HIGHEST,
        preferred_element_type=jnp.float32,
    )
    return jnp.moveaxis(result, -1, axis_id)


def forward_along(values_pair, axis_id):
    real_part, imag_part = values_pair
    cosine, sine = tables(real_part.shape[axis_id])
    return (
        apply_along(real_part, cosine, axis_id) + apply_along(imag_part, sine, axis_id),
        apply_along(imag_part, cosine, axis_id) - apply_along(real_part, sine, axis_id),
    )


def inverse_along(values_pair, axis_id):
    real_part, imag_part = values_pair
    length = real_part.shape[axis_id]
    cosine, sine = tables(length)
    scale = 1.0 / length
    return (
        (apply_along(real_part, cosine, axis_id) - apply_along(imag_part, sine, axis_id)) * scale,
        (apply_along(imag_part, cosine, axis_id) + apply_along(real_part, sine, axis_id)) * scale,
    )


def symbol_sq(length, first_id, span):
    wave_ids = first_id + jnp.arange(span, dtype=jnp.int32)
    signed = jnp.where(wave_ids < length // 2, wave_ids, wave_ids - length).astype(jnp.float32)
    wave = 2.0 * jnp.pi / length * signed
    return wave * wave


def local_general(velocity, template, moving, stiffness, fetch_plane, tissue):
    planes_dev, rows_dev, x_length = moving.shape
    blocks_x = x_length // BLOCK
    slabs = lax.axis_size("slab")
    subs = lax.axis_size("sub")
    my_slab = lax.axis_index("slab")
    my_sub = lax.axis_index("sub")
    per_dev = planes_dev * rows_dev * blocks_x
    capacity = 2 * per_dev // slabs
    source_plane = fetch_plane.reshape(-1)
    block_ids = jnp.arange(per_dev, dtype=jnp.int32)
    row_of = block_ids // blocks_x % rows_dev
    column_of = block_ids % blocks_x
    moving_rows = moving.reshape(per_dev, BLOCK)
    holder = source_plane // planes_dev
    within = (source_plane % planes_dev * rows_dev + row_of) * blocks_x + column_of
    matches = (holder[:, None] == jnp.arange(slabs, dtype=jnp.int32)[None, :]).astype(jnp.int32)
    earlier = jnp.sum((jnp.cumsum(matches, axis=0) - matches) * matches, axis=1)
    target = holder * capacity + earlier
    wanted = (
        jnp.zeros((slabs * capacity,), jnp.int32).at[target].set(within).reshape(slabs, capacity)
    )
    asked = lax.all_to_all(wanted, "slab", split_axis=0, concat_axis=0, tiled=True)
    fetched = moving_rows[asked.reshape(-1)].reshape(asked.shape + (BLOCK,))
    replies = lax.all_to_all(fetched, "slab", split_axis=0, concat_axis=0, tiled=True)
    warped_rows = replies.reshape(slabs * capacity, BLOCK)[target]
    warped = warped_rows.reshape(planes_dev, rows_dev, x_length)
    padded = extended(warped, (("slab", 0), ("sub", 1)), 1).astype(jnp.float32)
    image = padded[1:-1, 1:-1]
    grad_z = 0.5 * (padded[2:, 1:-1] - padded[:-2, 1:-1])
    grad_y = 0.5 * (padded[1:-1, 2:] - padded[1:-1, :-2])
    grad_x = 0.5 * (jnp.roll(image, -1, 2) - jnp.roll(image, 1, 2))
    residual = image - template.astype(jnp.float32)
    tissue_vox = jnp.repeat(tissue.astype(jnp.float32), BLOCK, axis=2)
    weight_field = tissue_vox * stiffness * residual
    force = jnp.stack([weight_field * grad_z, weight_field * grad_y, weight_field * grad_x])
    cos_x, sin_x = tables(x_length)
    real_part = apply_along(force, cos_x, 3)
    imag_part = -apply_along(force, sin_x, 3)
    moved = (
        lax.all_to_all(real_part, "sub", split_axis=3, concat_axis=2, tiled=True),
        lax.all_to_all(imag_part, "sub", split_axis=3, concat_axis=2, tiled=True),
    )
    moved = forward_along(moved, 2)
    moved = (
        lax.all_to_all(moved[0], "slab", split_axis=2, concat_axis=1, tiled=True),
        lax.all_to_all(moved[1], "slab", split_axis=2, concat_axis=1, tiled=True),
    )
    moved = forward_along(moved, 1)
    total_z = moved[0].shape[1]
    y_span = moved[0].shape[2]
    x_span = moved[0].shape[3]
    factor = 1.0 / (
        symbol_sq(total_z, 0, total_z)[:, None, None]
        + symbol_sq(y_span * slabs, my_slab * y_span, y_span)[None, :, None]
        + symbol_sq(x_span * subs, my_sub * x_span, x_span)[None, None, :]
        + 1.0 / 256.0
    )
    moved = (moved[0] * factor, moved[1] * factor)
    moved = inverse_along(moved, 1)
    moved = (
        lax.all_to_all(moved[0], "slab", split_axis=1, concat_axis=2, tiled=True),
        lax.all_to_all(moved[1], "slab", split_axis=1, concat_axis=2, tiled=True),
    )
    moved = inverse_along(moved, 2)
    real_part, imag_part = (
        lax.all_to_all(moved[0], "sub", split_axis=2, concat_axis=3, tiled=True),
        lax.all_to_all(moved[1], "sub", split_axis=2, concat_axis=3, tiled=True),
    )
    smoothed = (apply_along(real_part, cos_x, 3) - apply_along(imag_part, sin_x, 3)) * (
        1.0 / x_length
    )
    new_velocity = 0.5 * (velocity - smoothed)
    return (new_velocity, warped)


VMEM_BYTES = 24 * 1024 * 1024


def real_basis(length):
    index = np.arange(length)
    half = length // 2
    wave = np.where(index <= half, index, index - half)[:, None]
    angle = 2.0 * np.pi / length * (wave * index[None, :] % length)
    rows = np.where(index[:, None] <= half, np.cos(angle), np.sin(angle)) * np.sqrt(2.0 / length)
    rows[0] /= np.sqrt(2.0)
    rows[half] /= np.sqrt(2.0)
    return rows


def in_two(table):
    high = np.asarray(table, np.float32).astype(jnp.bfloat16)
    low = (np.asarray(table, np.float64) - high.astype(np.float64)).astype(jnp.bfloat16)
    return np.stack([high, low])


def split(values):
    high = values.astype(jnp.bfloat16)
    return high, (values - high.astype(jnp.float32)).astype(jnp.bfloat16)


def times(left, right, dims):
    def one(a, b):
        return lax.dot_general(a, b, (dims, ((), ())), preferred_element_type=jnp.float32)

    return one(left[0], right[0]) + (one(left[0], right[1]) + one(left[1], right[0]))


def wave_sq(index, length):
    wave = jnp.where(index <= length // 2, index, index - length // 2).astype(jnp.float32)
    wave = wave * (2.0 * np.pi / length)
    return wave * wave


def around(value, count):
    return lax.rem(value + 2 * count, count)


def call(kernel, out_shape, *arguments, scratch=(), flops=0, stays=0):
    places = [
        pl.BlockSpec(memory_space=pltpu.HBM if isinstance(a, tuple) else pltpu.SMEM if a.ndim == 1 else pltpu.VMEM)
        for a in arguments
    ]
    arguments = [a[0] if isinstance(a, tuple) else a for a in arguments]
    out_places = [
        pl.BlockSpec(memory_space=pltpu.HBM if k < stays else pltpu.VMEM)
        for k in range(len(jax.tree.leaves(out_shape)))
    ]
    nbytes = sum(a.size * a.dtype.itemsize for a in arguments + jax.tree.leaves(out_shape))
    return pl.pallas_call(
        kernel,
        out_shape=out_shape,
        in_specs=places,
        out_specs=jax.tree.unflatten(jax.tree.structure(out_shape), out_places),
        scratch_shapes=list(scratch),
        compiler_params=pltpu.CompilerParams(vmem_limit_bytes=VMEM_BYTES),
        cost_estimate=pl.CostEstimate(flops=flops, bytes_accessed=nbytes, transcendentals=0),
    )(*arguments)


def by_row(ref, rows):
    cells = jnp.concatenate([ref[z].astype(jnp.float32) for z in range(ref.shape[0])], axis=0)
    cells = jnp.concatenate([cells, jnp.zeros((cells.shape[0], BLOCK - rows), jnp.float32)], axis=1)
    cells = jnp.concatenate([cells, jnp.zeros((BLOCK - cells.shape[0], BLOCK), jnp.float32)], axis=0)
    return cells.T[:rows]


def send_columns_kernel(slabs, place, moving, fetch, *sends):
    planes, rows, _ = moving.shape
    for step, send in enumerate(sends):
        to = around(place[0] + step, slabs)
        block = pl.ds(pl.multiple_of(to * BLOCK, BLOCK), BLOCK)
        for z in range(planes):
            send[z * rows : (z + 1) * rows] = moving[z, :, block]
        asked = jnp.concatenate([fetch[z, pl.ds(to, 1), :] for z in range(planes)] * 2, axis=0).astype(jnp.float32)
        asked = jnp.concatenate([asked, jnp.zeros((2 * planes, BLOCK - rows), jnp.float32)], axis=1)
        send[planes * rows :] = asked.astype(jnp.bfloat16)


def pick_kernel(slabs, place, *refs):
    received, sends = refs[:slabs], refs[slabs:]
    planes, rows = sends[0].shape[0] - 2, sends[0].shape[1]
    me = place[0]
    group = 4

    def name(other, plane):
        number = (around(me - other, slabs) * planes).astype(jnp.float32) + float(plane)
        return jnp.full((rows, BLOCK), number, jnp.float32).astype(jnp.bfloat16)

    for step in range(slabs):
        names = received[step][planes * rows :].astype(jnp.float32)[:planes]
        names = jnp.concatenate([names, jnp.zeros((BLOCK - planes, BLOCK), jnp.float32)], axis=0).T[:rows]
        for start in range(0, planes, group):
            wanted = [
                jnp.broadcast_to(names[:, z : z + 1], (rows, BLOCK)).astype(jnp.bfloat16)
                for z in range(start, start + group)
            ]
            found = [jnp.zeros((rows, BLOCK), jnp.bfloat16) for _ in range(group)]
            for other in range(slabs):
                for plane in range(planes):
                    values = received[other][plane * rows : (plane + 1) * rows]
                    own = name(other, plane)
                    found = [jnp.where(w == own, values, f) for w, f in zip(wanted, found)]
            back = (slabs - step) % slabs
            for z in range(group):
                own = start + z
                sends[back][own + 1] = found[z]
                if own == 0:
                    sends[(back - 1) % slabs][planes + 1] = found[z]
                if own == planes - 1:
                    sends[(back + 1) % slabs][0] = found[z]


def coefficient_kernel(stiffness, tissue, out):
    planes, rows, x_length = stiffness.shape
    blocks = x_length // BLOCK
    marks = by_row(tissue, rows)
    for z in range(planes):
        marked = jnp.concatenate(
            [
                jnp.broadcast_to(marks[:, z * blocks + b : z * blocks + b + 1], (rows, BLOCK))
                for b in range(blocks)
            ],
            axis=1,
        )
        out[z] = 4.0 * marked * stiffness[z]


def force_zx_kernel(slabs, subs, place, *refs):
    received, refs = refs[:slabs], refs[slabs:]
    template, coefficient, basis, first, image, weight, spectra, kept, planes_of, wide = refs
    planes, rows, x_length = template.shape
    for step in range(slabs):
        block = pl.ds(pl.multiple_of(around(place[0] - step, slabs) * BLOCK, BLOCK), BLOCK)
        planes_of[:, :, block] = received[step][...].astype(jnp.float32)
    forces = [[], []]
    for z in range(planes):
        here = planes_of[z + 1]
        own = coefficient[z] * (here - template[z].astype(jnp.float32))
        image[z] = here
        weight[z] = own
        first[z : z + 1] = here[0:1]
        first[planes + z : planes + z + 1] = here[1:2]
        first[2 * planes + z : 2 * planes + z + 1] = own[0:1]
        forces[0].append(own * (planes_of[z + 2] - planes_of[z]))
        forces[1].append(own * (pltpu.roll(here, x_length - 1, 1) - pltpu.roll(here, 1, 1)))
    for a in range(2):
        force = split(jnp.concatenate(forces[a], axis=0))
        wide[a] = times((basis[0], basis[1]), force, ((1,), (1,)))
    part = x_length // (slabs * subs)
    cut = kept.shape[1]
    for d in range(slabs):
        for e in range(subs):
            start = (around(place[0] + d, slabs) * subs + around(place[1] + e, subs)) * part
            spectra[d, e, :part] = wide[0, pl.ds(pl.multiple_of(start, part), part), :]
            spectra[d, e, part:] = wide[1, pl.ds(pl.multiple_of(start + cut, 8), part - cut), :]
    for k in range(slabs * subs):
        kept[k] = wide[1, k * part : k * part + cut, :]


def force_y_kernel(beyond, image, weight, basis, kept, spectra):
    planes, rows, x_length = image.shape
    row = lax.broadcasted_iota(jnp.int32, (rows, x_length), 0)
    force = []
    for z in range(planes):
        here = image[z]
        after = jnp.where(row == rows - 2, beyond[z : z + 1, :], pltpu.roll(here, rows - 2, 0))
        after = jnp.where(row == rows - 1, beyond[planes + z : planes + z + 1, :], after)
        own = pltpu.roll(weight[z], rows - 1, 0)
        own = jnp.where(row == rows - 1, beyond[2 * planes + z : 2 * planes + z + 1, :], own)
        force.append(own * (after - here))
    devices = spectra.shape[0]
    part = x_length // devices
    spectrum = times((basis[0], basis[1]), split(jnp.concatenate(force, axis=0)), ((1,), (1,)))
    spectra[:, :part, :] = spectrum.reshape(devices, part, planes * rows)
    spectra[:, part:, :] = kept[...]


def swap_blocks(values):
    width = values[0].shape[1]
    lane = lax.broadcasted_iota(jnp.int32, values[0].shape, 1)
    lower, even = lane < width // 2, lax.rem(lane // (width // 4), 2) == 0

    def turn(own, count):
        return pltpu.roll(own, count * (width // 4), 1)

    a, b, c, d = values
    a, c = jnp.where(lower, a, turn(c, 2)), jnp.where(lower, turn(a, 2), c)
    b, d = jnp.where(lower, b, turn(d, 2)), jnp.where(lower, turn(b, 2), d)
    return [
        jnp.where(even, a, turn(b, 1)),
        jnp.where(even, turn(a, 3), b),
        jnp.where(even, c, turn(d, 1)),
        jnp.where(even, turn(c, 3), d),
    ]


def solve(first, x_length, offsets, shifted, subs, spectra, basis_z, basis_y, out, cells):
    devices, used, area = spectra.shape
    total_z, _, total_y = cells.shape
    slabs = devices // subs
    planes, rows = total_z // slabs, total_y // subs
    fold = total_y // rows
    tile = 8

    def along_y(k, values):
        high, low = basis_y[2 * k], basis_y[2 * k + 1]
        four = jnp.concatenate(
            [jnp.concatenate([high, low], axis=1), jnp.concatenate([high, jnp.zeros_like(low)], axis=1)], axis=0
        )
        sums = jnp.dot(jnp.concatenate(split(values), axis=1), four, preferred_element_type=jnp.float32)
        return sums[:, :total_y] + sums[:, total_y:]

    def along_z(k, values):
        high, low = basis_z[2 * k], basis_z[2 * k + 1]
        parts = split(values)
        return jnp.dot(
            jnp.concatenate([high, high, low], axis=1),
            jnp.concatenate([parts[0], parts[1], parts[0]], axis=0),
            preferred_element_type=jnp.float32,
        )

    for s in range(slabs):
        own = []
        for f in range(0, planes // fold):
            lanes = slice(f * total_y, (f + 1) * total_y)
            own += swap_blocks([spectra[s * subs + q][:, lanes] for q in range(subs)])
        for low, high, table in ((0, shifted, 2), (shifted, used, 0)):
            if low < high:
                some = along_y(table, jnp.concatenate([o[low:high] for o in own], axis=0))
                cells[s * planes : (s + 1) * planes, low:high] = some.reshape(planes, high - low, total_y)
    index = lax.broadcasted_iota(jnp.int32, (total_z * tile, 1), 0)
    z_sq = wave_sq(index // tile, total_z)
    y_sq = wave_sq(lax.broadcasted_iota(jnp.int32, (1, total_y), 1), total_y)
    own, scale = [], []
    for start in range(0, used, tile):
        own.append(cells[:, start : start + tile, :].reshape(total_z * tile, total_y))
        x_sq = wave_sq(first + offsets[start // tile] + lax.rem(index, tile), x_length)
        scale.append((z_sq + y_sq) * (256.0 / (x_sq * 256.0 + 1.0)) + 1.0)
    own = along_z(0, jnp.concatenate(own, axis=1))
    own = along_z(1, own / jnp.concatenate(scale, axis=1))
    for k, start in enumerate(range(0, used, tile)):
        part = own[:, k * total_y : (k + 1) * total_y]
        cells[:, start : start + tile, :] = part.reshape(total_z, tile, total_y)
    for s in range(slabs):
        own = along_y(1, cells[s * planes : (s + 1) * planes].reshape(planes * used, total_y))
        for f in range(0, planes // fold):
            blocks = swap_blocks([own[z * used : (z + 1) * used] for z in range(f * fold, (f + 1) * fold)])
            for q in range(subs):
                out[s * subs + q, :, f * total_y : (f + 1) * total_y] = blocks[q]


def solve_yx_kernel(subs, x_length, place, spectra, basis_z, basis_y, out, cells):
    devices = out.shape[0]
    part = x_length // devices
    offsets = list(range(0, part, 8)) + list(range(0, out.shape[1] - part, 8))
    solve((place[0] * subs + place[1]) * part, x_length, offsets, part, subs, spectra, basis_z, basis_y, out, cells)


def solve_zx_kernel(slabs, subs, x_length, place, *refs):
    received, refs = refs[:subs], refs[subs:]
    basis_z, basis_y, sends, (spectra, cells) = refs[0], refs[1], refs[2 : 2 + slabs], refs[2 + slabs :]
    part = x_length // (slabs * subs)
    offsets = list(range(0, part, 8)) + list(range(2 * part - received[0].shape[1], part, 8))
    for e in range(subs):
        for d in range(slabs):
            spectra[around(place[0] - d, slabs) * subs + around(place[1] - e, subs)] = received[e][d]
    solve((place[0] * subs + place[1]) * part, x_length, offsets, 0, subs, spectra, basis_z, basis_y, spectra, cells)
    for d in range(slabs):
        for e in range(subs):
            sends[d][e] = spectra[around(place[0] + d, slabs) * subs + around(place[1] + e, subs)]


def moved(spectra, velocity, basis):
    smoothed = times(split(spectra.T), (basis[0], basis[1]), ((1,), (0,)))
    return 0.5 * (velocity - 32.0 * smoothed.reshape(velocity.shape))


def update_z_kernel(slabs, subs, place, basis, velocity, *refs):
    received, (out, kept, gathered) = refs[:subs], refs[subs:]
    part = received[0].shape[1] - kept.shape[1]
    for e in range(subs):
        for d in range(slabs):
            index = around(place[0] - d, slabs) * subs + around(place[1] - e, subs)
            gathered[pl.ds(pl.multiple_of(index * part, part), part), :] = received[e][d, :part]
            kept[index] = received[e][d, part:]
    out[...] = moved(gathered[...], velocity[0], basis)


def update_kernel(spectra, basis, velocity, updated, kept, out, result, done):
    devices, _, area = kept.shape
    part = (spectra.shape[1] + kept.shape[1]) // 2
    leaving = [pltpu.make_async_copy(updated, out.at[0], done.at[0])]
    leaving[0].start()
    for a in range(2):
        if a:
            own = jnp.concatenate([spectra[:, part:, :], kept[...]], axis=1)
        else:
            own = spectra[:, :part, :]
        result[a] = moved(own.reshape(devices * part, area), velocity[a + 1], basis)
        leaving.append(pltpu.make_async_copy(result.at[a], out.at[a + 1], done.at[a + 1]))
        leaving[-1].start()
    for copy in leaving:
        copy.wait()


def place_kernel(slabs, place, *refs):
    received, warped = refs[:slabs], refs[slabs]
    for step in range(slabs):
        block = pl.ds(pl.multiple_of(around(place[0] - step, slabs) * BLOCK, BLOCK), BLOCK)
        warped[:, :, block] = received[step][1:-1]


def local_blocks(velocity, template, moving, stiffness, fetch_plane, tissue):
    planes, rows, x_length = moving.shape
    slabs, subs = lax.axis_size("slab"), lax.axis_size("sub")
    total_z, total_y = planes * slabs, rows * subs
    devices = slabs * subs
    part = x_length // devices
    area = planes * rows
    place = jnp.stack([lax.axis_index("slab"), lax.axis_index("sub")])
    bf16, f16, f32 = jnp.bfloat16, jnp.float16, jnp.float32

    def shape(dims, kind=f32):
        return jax.ShapeDtypeStruct(dims, kind)

    def scatter(sends, axis):
        count = lax.axis_size(axis)
        return [sends[0]] + [
            lax.ppermute(sends[d], axis, [(i, (i + d) % count) for i in range(count)]) for d in range(1, count)
        ]

    def exchange(values):
        return lax.all_to_all(values, ("slab", "sub"), split_axis=0, concat_axis=0, tiled=True)

    fetch, marks = fetch_plane.swapaxes(1, 2), tissue.swapaxes(1, 2)
    coefficient = call(coefficient_kernel, shape(moving.shape), stiffness, marks, flops=1 << 30)
    sends = call(
        functools.partial(send_columns_kernel, slabs),
        [shape(((rows + 2) * planes, BLOCK), bf16)] * slabs,
        place,
        moving,
        fetch,
    )
    sends = call(
        functools.partial(pick_kernel, slabs),
        [shape((planes + 2, rows, BLOCK), bf16)] * slabs,
        place,
        *scatter(sends, "slab"),
        flops=1 << 30,
    )
    received = scatter(sends, "slab")
    basis_x = in_two(real_basis(x_length))
    basis_z = np.kron(real_basis(total_z), np.eye(8))
    basis_z = np.concatenate([in_two(basis_z), in_two(basis_z.T)])
    basis_y = real_basis(total_y)
    basis_y = np.concatenate([in_two(b) for b in (basis_y.T, basis_y, np.roll(basis_y.T, -1, 0))])
    cut = part // 2
    with_z, with_y = 2 * part - cut, part + cut
    first, image, weight, chain, kept = call(
        functools.partial(force_zx_kernel, slabs, subs),
        [
            shape((3 * planes, x_length)),
            shape(moving.shape),
            shape(moving.shape),
            shape((slabs, subs, with_z, area)),
            shape((devices, cut, area)),
        ],
        place,
        *received,
        template,
        coefficient,
        basis_x,
        scratch=[pltpu.VMEM((planes + 2, rows, x_length), f32), pltpu.VMEM((2, x_length, area), f32)],
        flops=3 << 30,
    )
    beyond = lax.ppermute(first, "sub", [((i + 1) % subs, i) for i in range(subs)])
    chain = chain.astype(f16)
    chain = scatter([chain[d] for d in range(slabs)], "slab")
    later, *chain = lax.optimization_barrier((place, *chain))
    warped = call(functools.partial(place_kernel, slabs), shape(moving.shape, bf16), later, *received)
    chain = scatter([jnp.stack([r[e] for r in chain]) for e in range(subs)], "sub")
    spectra = call(
        force_y_kernel,
        shape((devices, with_y, area)),
        beyond,
        image,
        weight,
        basis_x,
        kept,
        flops=2 << 30,
    )
    spectra = exchange(spectra.astype(f16))
    chain = call(
        functools.partial(solve_zx_kernel, slabs, subs, x_length),
        [shape((subs, with_z, area))] * slabs,
        place,
        *[r.astype(f32) for r in chain],
        basis_z,
        basis_y,
        scratch=[pltpu.VMEM((devices, with_z, area), f32), pltpu.VMEM((total_z, with_z, total_y), f32)],
        flops=2 << 30,
    )
    chain, spectra, warped = lax.optimization_barrier((chain, spectra, warped))
    chain = scatter([r.astype(f16) for r in chain], "slab")
    chain = scatter([jnp.stack([r[e] for r in chain]) for e in range(subs)], "sub")
    spectra = call(
        functools.partial(solve_yx_kernel, subs, x_length),
        shape((devices, with_y, area)),
        place,
        spectra.astype(f32),
        basis_z,
        basis_y,
        scratch=[pltpu.VMEM((total_z, with_y, total_y), f32)],
        flops=2 << 30,
    )
    spectra = exchange(spectra.astype(f16))
    x_wave = np.arange(x_length)
    x_wave = 2.0 * np.pi / x_length * np.where(x_wave <= x_length // 2, x_wave, x_wave - x_length // 2)
    basis_back = in_two(real_basis(x_length) / (256.0 * x_wave**2 + 1.0)[:, None])
    updated, kept = call(
        functools.partial(update_z_kernel, slabs, subs),
        [shape(moving.shape), shape((devices, part - cut, area))],
        place,
        basis_back,
        velocity,
        *[r.astype(f32) for r in chain],
        scratch=[pltpu.VMEM((x_length, area), f32)],
        flops=1 << 30,
    )
    new_velocity = call(
        update_kernel,
        shape(velocity.shape),
        spectra.astype(f32),
        basis_back,
        velocity,
        updated,
        kept,
        scratch=[pltpu.VMEM((2,) + moving.shape, f32), pltpu.SemaphoreType.DMA((3,))],
        flops=2 << 30,
        stays=1,
    )
    return (new_velocity, warped)


def local(velocity, template, moving, stiffness, fetch_plane, tissue):
    planes, rows, x_length = moving.shape
    slabs, subs = lax.axis_size("slab"), lax.axis_size("sub")
    fits = (
        x_length == slabs * BLOCK
        and planes == 8
        and planes * slabs * 8 == 256
        and rows % 16 == 0
        and rows * subs == BLOCK
        and subs == 4
        and x_length % (32 * slabs * subs) == 0
    )
    run = local_blocks if fits else local_general
    return run(velocity, template, moving, stiffness, fetch_plane, tissue)


def solution(mesh):
    placed = (
        P(None, ("groups", "slab"), "sub", None),
        P(("groups", "slab"), "sub", None),
        P(("groups", "slab"), "sub", None),
        P(("groups", "slab"), "sub", None),
        P(("groups", "slab"), "sub", None),
        P(("groups", "slab"), "sub", None),
    )
    return jax.shard_map(
        local,
        mesh=mesh,
        in_specs=placed,
        out_specs=(P(None, ("groups", "slab"), "sub", None), P(("groups", "slab"), "sub", None)),
        check_vma=False,
    )
```

```python
import functools

import jax
import jax.numpy as jnp
import numpy as np
from jax import lax
from jax.experimental import pallas as pl
from jax.experimental.pallas import tpu as pltpu
from jax.sharding import PartitionSpec as P

BLOCK = 128


def extended(cells, sides, width):
    for axis, dim in sides:
        count = lax.axis_size(axis)
        head = lax.slice_in_dim(cells, 0, width, axis=dim)
        tail = lax.slice_in_dim(cells, cells.shape[dim] - width, cells.shape[dim], axis=dim)
        cells = jnp.concatenate(
            [
                lax.ppermute(tail, axis, [(i, (i + 1) % count) for i in range(count)]),
                cells,
                lax.ppermute(head, axis, [((i + 1) % count, i) for i in range(count)]),
            ],
            axis=dim,
        )
    return cells


def tables(length):
    wave_ids = jnp.arange(length, dtype=jnp.int32)
    phase = wave_ids[:, None] * wave_ids[None, :] % length
    angle = 2.0 * jnp.pi / length * phase.astype(jnp.float32)
    return (jnp.cos(angle), jnp.sin(angle))


def apply_along(values, matrix, axis_id):
    result = lax.dot_general(
        values,
        matrix,
        (((axis_id,), (0,)), ((), ())),
        precision=lax.Precision.HIGHEST,
        preferred_element_type=jnp.float32,
    )
    return jnp.moveaxis(result, -1, axis_id)


def forward_along(values_pair, axis_id):
    real_part, imag_part = values_pair
    cosine, sine = tables(real_part.shape[axis_id])
    return (
        apply_along(real_part, cosine, axis_id) + apply_along(imag_part, sine, axis_id),
        apply_along(imag_part, cosine, axis_id) - apply_along(real_part, sine, axis_id),
    )


def inverse_along(values_pair, axis_id):
    real_part, imag_part = values_pair
    length = real_part.shape[axis_id]
    cosine, sine = tables(length)
    scale = 1.0 / length
    return (
        (apply_along(real_part, cosine, axis_id) - apply_along(imag_part, sine, axis_id)) * scale,
        (apply_along(imag_part, cosine, axis_id) + apply_along(real_part, sine, axis_id)) * scale,
    )


def symbol_sq(length, first_id, span):
    wave_ids = first_id + jnp.arange(span, dtype=jnp.int32)
    signed = jnp.where(wave_ids < length // 2, wave_ids, wave_ids - length).astype(jnp.float32)
    wave = 2.0 * jnp.pi / length * signed
    return wave * wave


def local_general(velocity, template, moving, stiffness, fetch_plane, tissue):
    planes_dev, rows_dev, x_length = moving.shape
    blocks_x = x_length // BLOCK
    slabs = lax.axis_size("slab")
    subs = lax.axis_size("sub")
    my_slab = lax.axis_index("slab")
    my_sub = lax.axis_index("sub")
    per_dev = planes_dev * rows_dev * blocks_x
    capacity = 2 * per_dev // slabs
    source_plane = fetch_plane.reshape(-1)
    block_ids = jnp.arange(per_dev, dtype=jnp.int32)
    row_of = block_ids // blocks_x % rows_dev
    column_of = block_ids % blocks_x
    moving_rows = moving.reshape(per_dev, BLOCK)
    holder = source_plane // planes_dev
    within = (source_plane % planes_dev * rows_dev + row_of) * blocks_x + column_of
    matches = (holder[:, None] == jnp.arange(slabs, dtype=jnp.int32)[None, :]).astype(jnp.int32)
    earlier = jnp.sum((jnp.cumsum(matches, axis=0) - matches) * matches, axis=1)
    target = holder * capacity + earlier
    wanted = (
        jnp.zeros((slabs * capacity,), jnp.int32).at[target].set(within).reshape(slabs, capacity)
    )
    asked = lax.all_to_all(wanted, "slab", split_axis=0, concat_axis=0, tiled=True)
    fetched = moving_rows[asked.reshape(-1)].reshape(asked.shape + (BLOCK,))
    replies = lax.all_to_all(fetched, "slab", split_axis=0, concat_axis=0, tiled=True)
    warped_rows = replies.reshape(slabs * capacity, BLOCK)[target]
    warped = warped_rows.reshape(planes_dev, rows_dev, x_length)
    padded = extended(warped, (("slab", 0), ("sub", 1)), 1).astype(jnp.float32)
    image = padded[1:-1, 1:-1]
    grad_z = 0.5 * (padded[2:, 1:-1] - padded[:-2, 1:-1])
    grad_y = 0.5 * (padded[1:-1, 2:] - padded[1:-1, :-2])
    grad_x = 0.5 * (jnp.roll(image, -1, 2) - jnp.roll(image, 1, 2))
    residual = image - template.astype(jnp.float32)
    tissue_vox = jnp.repeat(tissue.astype(jnp.float32), BLOCK, axis=2)
    weight_field = tissue_vox * stiffness * residual
    force = jnp.stack([weight_field * grad_z, weight_field * grad_y, weight_field * grad_x])
    cos_x, sin_x = tables(x_length)
    real_part = apply_along(force, cos_x, 3)
    imag_part = -apply_along(force, sin_x, 3)
    moved = (
        lax.all_to_all(real_part, "sub", split_axis=3, concat_axis=2, tiled=True),
        lax.all_to_all(imag_part, "sub", split_axis=3, concat_axis=2, tiled=True),
    )
    moved = forward_along(moved, 2)
    moved = (
        lax.all_to_all(moved[0], "slab", split_axis=2, concat_axis=1, tiled=True),
        lax.all_to_all(moved[1], "slab", split_axis=2, concat_axis=1, tiled=True),
    )
    moved = forward_along(moved, 1)
    total_z = moved[0].shape[1]
    y_span = moved[0].shape[2]
    x_span = moved[0].shape[3]
    factor = 1.0 / (
        symbol_sq(total_z, 0, total_z)[:, None, None]
        + symbol_sq(y_span * slabs, my_slab * y_span, y_span)[None, :, None]
        + symbol_sq(x_span * subs, my_sub * x_span, x_span)[None, None, :]
        + 1.0 / 256.0
    )
    moved = (moved[0] * factor, moved[1] * factor)
    moved = inverse_along(moved, 1)
    moved = (
        lax.all_to_all(moved[0], "slab", split_axis=1, concat_axis=2, tiled=True),
        lax.all_to_all(moved[1], "slab", split_axis=1, concat_axis=2, tiled=True),
    )
    moved = inverse_along(moved, 2)
    real_part, imag_part = (
        lax.all_to_all(moved[0], "sub", split_axis=2, concat_axis=3, tiled=True),
        lax.all_to_all(moved[1], "sub", split_axis=2, concat_axis=3, tiled=True),
    )
    smoothed = (apply_along(real_part, cos_x, 3) - apply_along(imag_part, sin_x, 3)) * (
        1.0 / x_length
    )
    new_velocity = 0.5 * (velocity - smoothed)
    return (new_velocity, warped)


VMEM_BYTES = 24 * 1024 * 1024


def real_basis(length):
    index = np.arange(length)
    half = length // 2
    wave = np.where(index <= half, index, index - half)[:, None]
    angle = 2.0 * np.pi / length * (wave * index[None, :] % length)
    rows = np.where(index[:, None] <= half, np.cos(angle), np.sin(angle)) * np.sqrt(2.0 / length)
    rows[0] /= np.sqrt(2.0)
    rows[half] /= np.sqrt(2.0)
    return rows


def in_two(table):
    high = np.asarray(table, np.float32).astype(jnp.bfloat16)
    low = (np.asarray(table, np.float64) - high.astype(np.float64)).astype(jnp.bfloat16)
    return np.stack([high, low])


def split(values):
    high = values.astype(jnp.bfloat16)
    return high, (values - high.astype(jnp.float32)).astype(jnp.bfloat16)


def times(left, right, dims):
    def one(a, b):
        return lax.dot_general(a, b, (dims, ((), ())), preferred_element_type=jnp.float32)

    return one(left[0], right[0]) + (one(left[0], right[1]) + one(left[1], right[0]))


def wave_sq(index, length):
    wave = jnp.where(index <= length // 2, index, index - length // 2).astype(jnp.float32)
    wave = wave * (2.0 * np.pi / length)
    return wave * wave


HOPS = (0, 2, 1, 3)


def around(value, count):
    return lax.rem(value + 2 * count, count)


def call(kernel, out_shape, *arguments, scratch=(), flops=0, stays=0):
    places = [
        pl.BlockSpec(memory_space=pltpu.HBM if isinstance(a, tuple) else pltpu.SMEM if a.ndim == 1 else pltpu.VMEM)
        for a in arguments
    ]
    arguments = [a[0] if isinstance(a, tuple) else a for a in arguments]
    out_places = [
        pl.BlockSpec(memory_space=pltpu.HBM if k < stays else pltpu.VMEM)
        for k in range(len(jax.tree.leaves(out_shape)))
    ]
    nbytes = sum(a.size * a.dtype.itemsize for a in arguments + jax.tree.leaves(out_shape))
    return pl.pallas_call(
        kernel,
        out_shape=out_shape,
        in_specs=places,
        out_specs=jax.tree.unflatten(jax.tree.structure(out_shape), out_places),
        scratch_shapes=list(scratch),
        compiler_params=pltpu.CompilerParams(vmem_limit_bytes=VMEM_BYTES),
        cost_estimate=pl.CostEstimate(flops=flops, bytes_accessed=nbytes, transcendentals=0),
    )(*arguments)


def by_row(ref, rows):
    cells = jnp.concatenate([ref[z].astype(jnp.float32) for z in range(ref.shape[0])], axis=0)
    cells = jnp.concatenate([cells, jnp.zeros((cells.shape[0], BLOCK - rows), jnp.float32)], axis=1)
    cells = jnp.concatenate([cells, jnp.zeros((BLOCK - cells.shape[0], BLOCK), jnp.float32)], axis=0)
    return cells.T[:rows]


def send_columns_kernel(slabs, place, moving, fetch, *sends):
    planes, rows, _ = moving.shape
    for step, send in enumerate(sends):
        to = around(place[0] + HOPS[step], slabs)
        block = pl.ds(pl.multiple_of(to * BLOCK, BLOCK), BLOCK)
        for z in range(planes):
            send[z * rows : (z + 1) * rows] = moving[z, :, block]
        asked = jnp.concatenate([fetch[z, pl.ds(to, 1), :] for z in range(planes)] * 2, axis=0).astype(jnp.float32)
        asked = jnp.concatenate([asked, jnp.zeros((2 * planes, BLOCK - rows), jnp.float32)], axis=1)
        send[planes * rows :] = asked.astype(jnp.bfloat16)


def pick_kernel(slabs, place, *refs):
    received, sends = refs[:slabs], refs[slabs:]
    planes, rows = sends[0].shape[0] - 2, sends[0].shape[1]
    me = place[0]
    group = 4

    def name(other, plane):
        number = (around(me - HOPS[other], slabs) * planes).astype(jnp.float32) + float(plane)
        return jnp.full((rows, BLOCK), number, jnp.float32).astype(jnp.bfloat16)

    for step in range(slabs):
        names = received[step][planes * rows :].astype(jnp.float32)[:planes]
        names = jnp.concatenate([names, jnp.zeros((BLOCK - planes, BLOCK), jnp.float32)], axis=0).T[:rows]
        for start in range(0, planes, group):
            wanted = [
                jnp.broadcast_to(names[:, z : z + 1], (rows, BLOCK)).astype(jnp.bfloat16)
                for z in range(start, start + group)
            ]
            found = [jnp.zeros((rows, BLOCK), jnp.bfloat16) for _ in range(group)]
            for other in range(slabs):
                for plane in range(planes):
                    values = received[other][plane * rows : (plane + 1) * rows]
                    own = name(other, plane)
                    found = [jnp.where(w == own, values, f) for w, f in zip(wanted, found)]
            back = (slabs - HOPS[step]) % slabs
            for z in range(group):
                own = start + z
                sends[HOPS.index(back)][own + 1] = found[z]
                if own == 0:
                    sends[HOPS.index((back - 1) % slabs)][planes + 1] = found[z]
                if own == planes - 1:
                    sends[HOPS.index((back + 1) % slabs)][0] = found[z]


def coefficient_kernel(stiffness, tissue, out):
    planes, rows, x_length = stiffness.shape
    blocks = x_length // BLOCK
    marks = by_row(tissue, rows)
    for z in range(planes):
        marked = jnp.concatenate(
            [
                jnp.broadcast_to(marks[:, z * blocks + b : z * blocks + b + 1], (rows, BLOCK))
                for b in range(blocks)
            ],
            axis=1,
        )
        out[z] = 4.0 * marked * stiffness[z]


def force_zx_kernel(slabs, subs, place, *refs):
    received, refs = refs[:slabs], refs[slabs:]
    template, coefficient, basis, first, image, weight, spectra, kept, planes_of, wide = refs
    planes, rows, x_length = template.shape
    for step in range(slabs):
        block = pl.ds(pl.multiple_of(around(place[0] - HOPS[step], slabs) * BLOCK, BLOCK), BLOCK)
        planes_of[:, :, block] = received[step][...].astype(jnp.float32)
    forces = [[], []]
    for z in range(planes):
        here = planes_of[z + 1]
        own = coefficient[z] * (here - template[z].astype(jnp.float32))
        image[z] = here
        weight[z] = own
        first[z : z + 1] = here[0:1]
        first[planes + z : planes + z + 1] = here[1:2]
        first[2 * planes + z : 2 * planes + z + 1] = own[0:1]
        forces[0].append(own * (planes_of[z + 2] - planes_of[z]))
        forces[1].append(own * (pltpu.roll(here, x_length - 1, 1) - pltpu.roll(here, 1, 1)))
    for a in range(2):
        force = split(jnp.concatenate(forces[a], axis=0))
        wide[a] = times((basis[0], basis[1]), force, ((1,), (1,)))
    part = x_length // (slabs * subs)
    cut = kept.shape[1]
    for d in range(slabs):
        for e in range(subs):
            start = (around(place[0] + d, slabs) * subs + around(place[1] + e, subs)) * part
            spectra[d, e, :part] = wide[0, pl.ds(pl.multiple_of(start, part), part), :]
            spectra[d, e, part:] = wide[1, pl.ds(pl.multiple_of(start + cut, 8), part - cut), :]
    for k in range(slabs * subs):
        kept[k] = wide[1, k * part : k * part + cut, :]


def force_y_kernel(beyond, image, weight, basis, kept, spectra):
    planes, rows, x_length = image.shape
    row = lax.broadcasted_iota(jnp.int32, (rows, x_length), 0)
    force = []
    for z in range(planes):
        here = image[z]
        after = jnp.where(row == rows - 2, beyond[z : z + 1, :], pltpu.roll(here, rows - 2, 0))
        after = jnp.where(row == rows - 1, beyond[planes + z : planes + z + 1, :], after)
        own = pltpu.roll(weight[z], rows - 1, 0)
        own = jnp.where(row == rows - 1, beyond[2 * planes + z : 2 * planes + z + 1, :], own)
        force.append(own * (after - here))
    devices = spectra.shape[0]
    part = x_length // devices
    spectrum = times((basis[0], basis[1]), split(jnp.concatenate(force, axis=0)), ((1,), (1,)))
    spectra[:, :part, :] = spectrum.reshape(devices, part, planes * rows)
    spectra[:, part:, :] = kept[...]


def swap_blocks(values):
    width = values[0].shape[1]
    lane = lax.broadcasted_iota(jnp.int32, values[0].shape, 1)
    lower, even = lane < width // 2, lax.rem(lane // (width // 4), 2) == 0

    def turn(own, count):
        return pltpu.roll(own, count * (width // 4), 1)

    a, b, c, d = values
    a, c = jnp.where(lower, a, turn(c, 2)), jnp.where(lower, turn(a, 2), c)
    b, d = jnp.where(lower, b, turn(d, 2)), jnp.where(lower, turn(b, 2), d)
    return [
        jnp.where(even, a, turn(b, 1)),
        jnp.where(even, turn(a, 3), b),
        jnp.where(even, c, turn(d, 1)),
        jnp.where(even, turn(c, 3), d),
    ]


def solve(first, x_length, offsets, shifted, subs, spectra, basis_z, basis_y, out, cells):
    devices, used, area = spectra.shape
    total_z, _, total_y = cells.shape
    slabs = devices // subs
    planes, rows = total_z // slabs, total_y // subs
    fold = total_y // rows
    tile = 8

    def along_y(k, values):
        high, low = basis_y[2 * k], basis_y[2 * k + 1]
        four = jnp.concatenate(
            [jnp.concatenate([high, low], axis=1), jnp.concatenate([high, jnp.zeros_like(low)], axis=1)], axis=0
        )
        sums = jnp.dot(jnp.concatenate(split(values), axis=1), four, preferred_element_type=jnp.float32)
        return sums[:, :total_y] + sums[:, total_y:]

    def along_z(k, values):
        high, low = basis_z[2 * k], basis_z[2 * k + 1]
        parts = split(values)
        return jnp.dot(
            jnp.concatenate([high, high, low], axis=1),
            jnp.concatenate([parts[0], parts[1], parts[0]], axis=0),
            preferred_element_type=jnp.float32,
        )

    for s in range(slabs):
        own = []
        for f in range(0, planes // fold):
            lanes = slice(f * total_y, (f + 1) * total_y)
            own += swap_blocks([spectra[s * subs + q][:, lanes] for q in range(subs)])
        for low, high, table in ((0, shifted, 2), (shifted, used, 0)):
            if low < high:
                some = along_y(table, jnp.concatenate([o[low:high] for o in own], axis=0))
                cells[s * planes : (s + 1) * planes, low:high] = some.reshape(planes, high - low, total_y)
    index = lax.broadcasted_iota(jnp.int32, (total_z * tile, 1), 0)
    z_sq = wave_sq(index // tile, total_z)
    y_sq = wave_sq(lax.broadcasted_iota(jnp.int32, (1, total_y), 1), total_y)
    own, scale = [], []
    for start in range(0, used, tile):
        own.append(cells[:, start : start + tile, :].reshape(total_z * tile, total_y))
        x_sq = wave_sq(first + offsets[start // tile] + lax.rem(index, tile), x_length)
        scale.append((z_sq + y_sq) * (256.0 / (x_sq * 256.0 + 1.0)) + 1.0)
    own = along_z(0, jnp.concatenate(own, axis=1))
    own = along_z(1, own / jnp.concatenate(scale, axis=1))
    for k, start in enumerate(range(0, used, tile)):
        part = own[:, k * total_y : (k + 1) * total_y]
        cells[:, start : start + tile, :] = part.reshape(total_z, tile, total_y)
    for s in range(slabs):
        own = along_y(1, cells[s * planes : (s + 1) * planes].reshape(planes * used, total_y))
        for f in range(0, planes // fold):
            blocks = swap_blocks([own[z * used : (z + 1) * used] for z in range(f * fold, (f + 1) * fold)])
            for q in range(subs):
                out[s * subs + q, :, f * total_y : (f + 1) * total_y] = blocks[q]


def solve_yx_kernel(subs, x_length, place, spectra, basis_z, basis_y, out, cells):
    devices = out.shape[0]
    part = x_length // devices
    offsets = list(range(0, part, 8)) + list(range(0, out.shape[1] - part, 8))
    solve((place[0] * subs + place[1]) * part, x_length, offsets, part, subs, spectra, basis_z, basis_y, out, cells)


def solve_zx_kernel(slabs, subs, x_length, place, *refs):
    received, refs = refs[:subs], refs[subs:]
    basis_z, basis_y, sends, (spectra, cells) = refs[0], refs[1], refs[2 : 2 + slabs], refs[2 + slabs :]
    part = x_length // (slabs * subs)
    offsets = list(range(0, part, 8)) + list(range(2 * part - received[0].shape[1], part, 8))
    for e in range(subs):
        for d in range(slabs):
            spectra[around(place[0] - d, slabs) * subs + around(place[1] - e, subs)] = received[e][d]
    solve((place[0] * subs + place[1]) * part, x_length, offsets, 0, subs, spectra, basis_z, basis_y, spectra, cells)
    for d in range(slabs):
        for e in range(subs):
            sends[d][e] = spectra[around(place[0] + d, slabs) * subs + around(place[1] + e, subs)]


def moved(spectra, velocity, basis):
    smoothed = times(split(spectra.T), (basis[0], basis[1]), ((1,), (0,)))
    return 0.5 * (velocity - 32.0 * smoothed.reshape(velocity.shape))


def update_z_kernel(slabs, subs, place, basis, velocity, *refs):
    received, (out, kept, gathered) = refs[:subs], refs[subs:]
    part = received[0].shape[1] - kept.shape[1]
    for e in range(subs):
        for d in range(slabs):
            index = around(place[0] - d, slabs) * subs + around(place[1] - e, subs)
            gathered[pl.ds(pl.multiple_of(index * part, part), part), :] = received[e][d, :part]
            kept[index] = received[e][d, part:]
    out[...] = moved(gathered[...], velocity[0], basis)


def update_kernel(spectra, basis, velocity, updated, kept, out, result, done):
    devices, _, area = kept.shape
    part = (spectra.shape[1] + kept.shape[1]) // 2
    leaving = [pltpu.make_async_copy(updated, out.at[0], done.at[0])]
    leaving[0].start()
    for a in range(2):
        if a:
            own = jnp.concatenate([spectra[:, part:, :], kept[...]], axis=1)
        else:
            own = spectra[:, :part, :]
        high, low = split(own.reshape(devices * part, area).T)
        planes, rows, x_length = velocity.shape[1:]
        some = planes // 2
        for k in range(2):
            cells = slice(k * some * rows, (k + 1) * some * rows)
            smoothed = times((high[cells], low[cells]), (basis[0], basis[1]), ((1,), (0,)))
            own_planes = slice(k * some, (k + 1) * some)
            step = velocity[a + 1, own_planes] - 32.0 * smoothed.reshape(some, rows, x_length)
            result[a, own_planes] = 0.5 * step
            there = out.at[a + 1, pl.ds(k * some, some)]
            own_copy = pltpu.make_async_copy(result.at[a, pl.ds(k * some, some)], there, done.at[1 + 2 * a + k])
            own_copy.start()
            leaving.append(own_copy)
    for copy in leaving:
        copy.wait()


def place_kernel(slabs, place, *refs):
    received, warped = refs[:slabs], refs[slabs]
    for step in range(slabs):
        block = pl.ds(pl.multiple_of(around(place[0] - HOPS[step], slabs) * BLOCK, BLOCK), BLOCK)
        warped[:, :, block] = received[step][1:-1]


def local_blocks(velocity, template, moving, stiffness, fetch_plane, tissue):
    planes, rows, x_length = moving.shape
    slabs, subs = lax.axis_size("slab"), lax.axis_size("sub")
    total_z, total_y = planes * slabs, rows * subs
    devices = slabs * subs
    part = x_length // devices
    area = planes * rows
    place = jnp.stack([lax.axis_index("slab"), lax.axis_index("sub")])
    bf16, f16, f32 = jnp.bfloat16, jnp.float16, jnp.float32

    def shape(dims, kind=f32):
        return jax.ShapeDtypeStruct(dims, kind)

    def scatter(sends, axis, hops=(0, 1, 2, 3)):
        count = lax.axis_size(axis)
        return [sends[0]] + [
            lax.ppermute(sends[d], axis, [(i, (i + hops[d]) % count) for i in range(count)]) for d in range(1, count)
        ]

    def exchange(values):
        return lax.all_to_all(values, ("slab", "sub"), split_axis=0, concat_axis=0, tiled=True)

    fetch, marks = fetch_plane.swapaxes(1, 2), tissue.swapaxes(1, 2)
    coefficient = call(coefficient_kernel, shape(moving.shape), stiffness, marks, flops=1 << 30)
    sends = call(
        functools.partial(send_columns_kernel, slabs),
        [shape(((rows + 2) * planes, BLOCK), bf16)] * slabs,
        place,
        moving,
        fetch,
    )
    sends = call(
        functools.partial(pick_kernel, slabs),
        [shape((planes + 2, rows, BLOCK), bf16)] * slabs,
        place,
        *scatter(sends, "slab", HOPS),
        flops=1 << 30,
    )
    received = scatter(sends, "slab", HOPS)
    basis_x = in_two(real_basis(x_length))
    basis_z = np.kron(real_basis(total_z), np.eye(8))
    basis_z = np.concatenate([in_two(basis_z), in_two(basis_z.T)])
    basis_y = real_basis(total_y)
    basis_y = np.concatenate([in_two(b) for b in (basis_y.T, basis_y, np.roll(basis_y.T, -1, 0))])
    cut = part // 2
    with_z, with_y = 2 * part - cut, part + cut
    first, image, weight, chain, kept = call(
        functools.partial(force_zx_kernel, slabs, subs),
        [
            shape((3 * planes, x_length)),
            shape(moving.shape),
            shape(moving.shape),
            shape((slabs, subs, with_z, area)),
            shape((devices, cut, area)),
        ],
        place,
        *received,
        template,
        coefficient,
        basis_x,
        scratch=[pltpu.VMEM((planes + 2, rows, x_length), f32), pltpu.VMEM((2, x_length, area), f32)],
        flops=3 << 30,
    )
    beyond = lax.ppermute(first, "sub", [((i + 1) % subs, i) for i in range(subs)])
    chain = chain.astype(f16)
    chain = scatter([chain[d] for d in range(slabs)], "slab")
    later, *chain = lax.optimization_barrier((place, *chain))
    warped = call(functools.partial(place_kernel, slabs), shape(moving.shape, bf16), later, *received)
    chain = scatter([jnp.stack([r[e] for r in chain]) for e in range(subs)], "sub")
    spectra = call(
        force_y_kernel,
        shape((devices, with_y, area)),
        beyond,
        image,
        weight,
        basis_x,
        kept,
        flops=2 << 30,
    )
    spectra = exchange(spectra.astype(f16))
    chain = call(
        functools.partial(solve_zx_kernel, slabs, subs, x_length),
        [shape((subs, with_z, area))] * slabs,
        place,
        *[r.astype(f32) for r in chain],
        basis_z,
        basis_y,
        scratch=[pltpu.VMEM((devices, with_z, area), f32), pltpu.VMEM((total_z, with_z, total_y), f32)],
        flops=2 << 30,
    )
    chain, spectra, warped = lax.optimization_barrier((chain, spectra, warped))
    chain = scatter([r.astype(f16) for r in chain], "slab")
    chain = scatter([jnp.stack([r[e] for r in chain]) for e in range(subs)], "sub")
    spectra = call(
        functools.partial(solve_yx_kernel, subs, x_length),
        shape((devices, with_y, area)),
        place,
        spectra.astype(f32),
        basis_z,
        basis_y,
        scratch=[pltpu.VMEM((total_z, with_y, total_y), f32)],
        flops=2 << 30,
    )
    spectra = exchange(spectra.astype(f16))
    x_wave = np.arange(x_length)
    x_wave = 2.0 * np.pi / x_length * np.where(x_wave <= x_length // 2, x_wave, x_wave - x_length // 2)
    basis_back = in_two(real_basis(x_length) / (256.0 * x_wave**2 + 1.0)[:, None])
    updated, kept = call(
        functools.partial(update_z_kernel, slabs, subs),
        [shape(moving.shape), shape((devices, part - cut, area))],
        place,
        basis_back,
        velocity,
        *[r.astype(f32) for r in chain],
        scratch=[pltpu.VMEM((x_length, area), f32)],
        flops=1 << 30,
    )
    new_velocity = call(
        update_kernel,
        shape(velocity.shape),
        spectra.astype(f32),
        basis_back,
        velocity,
        updated,
        kept,
        scratch=[pltpu.VMEM((2,) + moving.shape, f32), pltpu.SemaphoreType.DMA((5,))],
        flops=2 << 30,
        stays=1,
    )
    return (new_velocity, warped)


def local(velocity, template, moving, stiffness, fetch_plane, tissue):
    planes, rows, x_length = moving.shape
    slabs, subs = lax.axis_size("slab"), lax.axis_size("sub")
    fits = (
        x_length == slabs * BLOCK
        and planes == 8
        and planes * slabs * 8 == 256
        and rows % 16 == 0
        and rows * subs == BLOCK
        and slabs == subs == len(HOPS)
        and x_length % (32 * slabs * subs) == 0
    )
    run = local_blocks if fits else local_general
    return run(velocity, template, moving, stiffness, fetch_plane, tissue)


def solution(mesh):
    placed = (
        P(None, ("groups", "slab"), "sub", None),
        P(("groups", "slab"), "sub", None),
        P(("groups", "slab"), "sub", None),
        P(("groups", "slab"), "sub", None),
        P(("groups", "slab"), "sub", None),
        P(("groups", "slab"), "sub", None),
    )
    return jax.shard_map(
        local,
        mesh=mesh,
        in_specs=placed,
        out_specs=(P(None, ("groups", "slab"), "sub", None), P(("groups", "slab"), "sub", None)),
        check_vma=False,
    )
```

```python
import functools

import jax
import jax.numpy as jnp
import numpy as np
from jax import lax
from jax.experimental import pallas as pl
from jax.experimental.pallas import tpu as pltpu
from jax.sharding import PartitionSpec as P

BLOCK = 128


def extended(cells, sides, width):
    for axis, dim in sides:
        count = lax.axis_size(axis)
        head = lax.slice_in_dim(cells, 0, width, axis=dim)
        tail = lax.slice_in_dim(cells, cells.shape[dim] - width, cells.shape[dim], axis=dim)
        cells = jnp.concatenate(
            [
                lax.ppermute(tail, axis, [(i, (i + 1) % count) for i in range(count)]),
                cells,
                lax.ppermute(head, axis, [((i + 1) % count, i) for i in range(count)]),
            ],
            axis=dim,
        )
    return cells


def tables(length):
    wave_ids = jnp.arange(length, dtype=jnp.int32)
    phase = wave_ids[:, None] * wave_ids[None, :] % length
    angle = 2.0 * jnp.pi / length * phase.astype(jnp.float32)
    return (jnp.cos(angle), jnp.sin(angle))


def apply_along(values, matrix, axis_id):
    result = lax.dot_general(
        values,
        matrix,
        (((axis_id,), (0,)), ((), ())),
        precision=lax.Precision.HIGHEST,
        preferred_element_type=jnp.float32,
    )
    return jnp.moveaxis(result, -1, axis_id)


def forward_along(values_pair, axis_id):
    real_part, imag_part = values_pair
    cosine, sine = tables(real_part.shape[axis_id])
    return (
        apply_along(real_part, cosine, axis_id) + apply_along(imag_part, sine, axis_id),
        apply_along(imag_part, cosine, axis_id) - apply_along(real_part, sine, axis_id),
    )


def inverse_along(values_pair, axis_id):
    real_part, imag_part = values_pair
    length = real_part.shape[axis_id]
    cosine, sine = tables(length)
    scale = 1.0 / length
    return (
        (apply_along(real_part, cosine, axis_id) - apply_along(imag_part, sine, axis_id)) * scale,
        (apply_along(imag_part, cosine, axis_id) + apply_along(real_part, sine, axis_id)) * scale,
    )


def symbol_sq(length, first_id, span):
    wave_ids = first_id + jnp.arange(span, dtype=jnp.int32)
    signed = jnp.where(wave_ids < length // 2, wave_ids, wave_ids - length).astype(jnp.float32)
    wave = 2.0 * jnp.pi / length * signed
    return wave * wave


def local_general(velocity, template, moving, stiffness, fetch_plane, tissue):
    planes_dev, rows_dev, x_length = moving.shape
    blocks_x = x_length // BLOCK
    slabs = lax.axis_size("slab")
    subs = lax.axis_size("sub")
    my_slab = lax.axis_index("slab")
    my_sub = lax.axis_index("sub")
    per_dev = planes_dev * rows_dev * blocks_x
    capacity = 2 * per_dev // slabs
    source_plane = fetch_plane.reshape(-1)
    block_ids = jnp.arange(per_dev, dtype=jnp.int32)
    row_of = block_ids // blocks_x % rows_dev
    column_of = block_ids % blocks_x
    moving_rows = moving.reshape(per_dev, BLOCK)
    holder = source_plane // planes_dev
    within = (source_plane % planes_dev * rows_dev + row_of) * blocks_x + column_of
    matches = (holder[:, None] == jnp.arange(slabs, dtype=jnp.int32)[None, :]).astype(jnp.int32)
    earlier = jnp.sum((jnp.cumsum(matches, axis=0) - matches) * matches, axis=1)
    target = holder * capacity + earlier
    wanted = (
        jnp.zeros((slabs * capacity,), jnp.int32).at[target].set(within).reshape(slabs, capacity)
    )
    asked = lax.all_to_all(wanted, "slab", split_axis=0, concat_axis=0, tiled=True)
    fetched = moving_rows[asked.reshape(-1)].reshape(asked.shape + (BLOCK,))
    replies = lax.all_to_all(fetched, "slab", split_axis=0, concat_axis=0, tiled=True)
    warped_rows = replies.reshape(slabs * capacity, BLOCK)[target]
    warped = warped_rows.reshape(planes_dev, rows_dev, x_length)
    padded = extended(warped, (("slab", 0), ("sub", 1)), 1).astype(jnp.float32)
    image = padded[1:-1, 1:-1]
    grad_z = 0.5 * (padded[2:, 1:-1] - padded[:-2, 1:-1])
    grad_y = 0.5 * (padded[1:-1, 2:] - padded[1:-1, :-2])
    grad_x = 0.5 * (jnp.roll(image, -1, 2) - jnp.roll(image, 1, 2))
    residual = image - template.astype(jnp.float32)
    tissue_vox = jnp.repeat(tissue.astype(jnp.float32), BLOCK, axis=2)
    weight_field = tissue_vox * stiffness * residual
    force = jnp.stack([weight_field * grad_z, weight_field * grad_y, weight_field * grad_x])
    cos_x, sin_x = tables(x_length)
    real_part = apply_along(force, cos_x, 3)
    imag_part = -apply_along(force, sin_x, 3)
    moved = (
        lax.all_to_all(real_part, "sub", split_axis=3, concat_axis=2, tiled=True),
        lax.all_to_all(imag_part, "sub", split_axis=3, concat_axis=2, tiled=True),
    )
    moved = forward_along(moved, 2)
    moved = (
        lax.all_to_all(moved[0], "slab", split_axis=2, concat_axis=1, tiled=True),
        lax.all_to_all(moved[1], "slab", split_axis=2, concat_axis=1, tiled=True),
    )
    moved = forward_along(moved, 1)
    total_z = moved[0].shape[1]
    y_span = moved[0].shape[2]
    x_span = moved[0].shape[3]
    factor = 1.0 / (
        symbol_sq(total_z, 0, total_z)[:, None, None]
        + symbol_sq(y_span * slabs, my_slab * y_span, y_span)[None, :, None]
        + symbol_sq(x_span * subs, my_sub * x_span, x_span)[None, None, :]
        + 1.0 / 256.0
    )
    moved = (moved[0] * factor, moved[1] * factor)
    moved = inverse_along(moved, 1)
    moved = (
        lax.all_to_all(moved[0], "slab", split_axis=1, concat_axis=2, tiled=True),
        lax.all_to_all(moved[1], "slab", split_axis=1, concat_axis=2, tiled=True),
    )
    moved = inverse_along(moved, 2)
    real_part, imag_part = (
        lax.all_to_all(moved[0], "sub", split_axis=2, concat_axis=3, tiled=True),
        lax.all_to_all(moved[1], "sub", split_axis=2, concat_axis=3, tiled=True),
    )
    smoothed = (apply_along(real_part, cos_x, 3) - apply_along(imag_part, sin_x, 3)) * (
        1.0 / x_length
    )
    new_velocity = 0.5 * (velocity - smoothed)
    return (new_velocity, warped)


VMEM_BYTES = 24 * 1024 * 1024


def real_basis(length):
    index = np.arange(length)
    half = length // 2
    wave = np.where(index <= half, index, index - half)[:, None]
    angle = 2.0 * np.pi / length * (wave * index[None, :] % length)
    rows = np.where(index[:, None] <= half, np.cos(angle), np.sin(angle)) * np.sqrt(2.0 / length)
    rows[0] /= np.sqrt(2.0)
    rows[half] /= np.sqrt(2.0)
    return rows


def in_two(table):
    high = np.asarray(table, np.float32).astype(jnp.bfloat16)
    low = (np.asarray(table, np.float64) - high.astype(np.float64)).astype(jnp.bfloat16)
    return np.stack([high, low])


def split(values):
    high = values.astype(jnp.bfloat16)
    return high, (values - high.astype(jnp.float32)).astype(jnp.bfloat16)


def times(left, right, dims):
    def one(a, b):
        return lax.dot_general(a, b, (dims, ((), ())), preferred_element_type=jnp.float32)

    return one(left[0], right[0]) + (one(left[0], right[1]) + one(left[1], right[0]))


def wave_sq(index, length):
    wave = jnp.where(index <= length // 2, index, index - length // 2).astype(jnp.float32)
    wave = wave * (2.0 * np.pi / length)
    return wave * wave


HOPS = (0, 2, 1, 3)


def around(value, count):
    return lax.rem(value + 2 * count, count)


def call(kernel, out_shape, *arguments, scratch=(), flops=0, stays=0):
    places = [
        pl.BlockSpec(memory_space=pltpu.HBM if isinstance(a, tuple) else pltpu.SMEM if a.ndim == 1 else pltpu.VMEM)
        for a in arguments
    ]
    arguments = [a[0] if isinstance(a, tuple) else a for a in arguments]
    out_places = [
        pl.BlockSpec(memory_space=pltpu.HBM if k < stays else pltpu.VMEM)
        for k in range(len(jax.tree.leaves(out_shape)))
    ]
    nbytes = sum(a.size * a.dtype.itemsize for a in arguments + jax.tree.leaves(out_shape))
    return pl.pallas_call(
        kernel,
        out_shape=out_shape,
        in_specs=places,
        out_specs=jax.tree.unflatten(jax.tree.structure(out_shape), out_places),
        scratch_shapes=list(scratch),
        compiler_params=pltpu.CompilerParams(vmem_limit_bytes=VMEM_BYTES),
        cost_estimate=pl.CostEstimate(flops=flops, bytes_accessed=nbytes, transcendentals=0),
    )(*arguments)


def by_row(ref, rows):
    cells = jnp.concatenate([ref[z].astype(jnp.float32) for z in range(ref.shape[0])], axis=0)
    cells = jnp.concatenate([cells, jnp.zeros((cells.shape[0], BLOCK - rows), jnp.float32)], axis=1)
    cells = jnp.concatenate([cells, jnp.zeros((BLOCK - cells.shape[0], BLOCK), jnp.float32)], axis=0)
    return cells.T[:rows]


def send_columns_kernel(slabs, place, moving, fetch, *sends):
    planes, rows, _ = moving.shape
    for step, send in enumerate(sends):
        to = around(place[0] + HOPS[step], slabs)
        block = pl.ds(pl.multiple_of(to * BLOCK, BLOCK), BLOCK)
        for z in range(planes):
            send[z * rows : (z + 1) * rows] = moving[z, :, block]
        asked = jnp.concatenate([fetch[z, pl.ds(to, 1), :] for z in range(planes)] * 2, axis=0).astype(jnp.float32)
        asked = jnp.concatenate([asked, jnp.zeros((2 * planes, BLOCK - rows), jnp.float32)], axis=1)
        send[planes * rows :] = asked.astype(jnp.bfloat16)


def pick_kernel(slabs, place, *refs):
    received, sends = refs[:slabs], refs[slabs:]
    planes, rows = sends[0].shape[0] - 2, sends[0].shape[1]
    me = place[0]
    group = 4

    def name(other, plane):
        number = (around(me - HOPS[other], slabs) * planes).astype(jnp.float32) + float(plane)
        return jnp.full((rows, BLOCK), number, jnp.float32).astype(jnp.bfloat16)

    for step in range(slabs):
        names = received[step][planes * rows :].astype(jnp.float32)[:planes]
        names = jnp.concatenate([names, jnp.zeros((BLOCK - planes, BLOCK), jnp.float32)], axis=0).T[:rows]
        for start in range(0, planes, group):
            wanted = [
                jnp.broadcast_to(names[:, z : z + 1], (rows, BLOCK)).astype(jnp.bfloat16)
                for z in range(start, start + group)
            ]
            found = [jnp.zeros((rows, BLOCK), jnp.bfloat16) for _ in range(group)]
            for other in range(slabs):
                for plane in range(planes):
                    values = received[other][plane * rows : (plane + 1) * rows]
                    own = name(other, plane)
                    found = [jnp.where(w == own, values, f) for w, f in zip(wanted, found)]
            back = (slabs - HOPS[step]) % slabs
            for z in range(group):
                own = start + z
                sends[HOPS.index(back)][own + 1] = found[z]
                if own == 0:
                    sends[HOPS.index((back - 1) % slabs)][planes + 1] = found[z]
                if own == planes - 1:
                    sends[HOPS.index((back + 1) % slabs)][0] = found[z]


def coefficient_kernel(stiffness, tissue, out):
    planes, rows, x_length = stiffness.shape
    blocks = x_length // BLOCK
    marks = by_row(tissue, rows)
    for z in range(planes):
        marked = jnp.concatenate(
            [
                jnp.broadcast_to(marks[:, z * blocks + b : z * blocks + b + 1], (rows, BLOCK))
                for b in range(blocks)
            ],
            axis=1,
        )
        out[z] = 4.0 * marked * stiffness[z]


def force_zx_kernel(slabs, subs, place, *refs):
    received, refs = refs[:slabs], refs[slabs:]
    template, coefficient, basis, upper, first, image, weight, spectra, planes_of, wide, wide_x = refs
    planes, rows, x_length = template.shape
    for step in range(slabs):
        block = pl.ds(pl.multiple_of(around(place[0] - HOPS[step], slabs) * BLOCK, BLOCK), BLOCK)
        planes_of[:, :, block] = received[step][...].astype(jnp.float32)
    forces = [[], []]
    for z in range(planes):
        here = planes_of[z + 1]
        own = coefficient[z] * (here - template[z].astype(jnp.float32))
        image[z] = here
        weight[z] = own
        first[z : z + 1] = here[0:1]
        first[planes + z : planes + z + 1] = here[1:2]
        first[2 * planes + z : 2 * planes + z + 1] = own[0:1]
        forces[0].append(own * (planes_of[z + 2] - planes_of[z]))
        forces[1].append(own * (pltpu.roll(here, x_length - 1, 1) - pltpu.roll(here, 1, 1)))
    wide[...] = times((basis[0], basis[1]), split(jnp.concatenate(forces[0], axis=0)), ((1,), (1,)))
    wide_x[...] = times((upper[0], upper[1]), split(jnp.concatenate(forces[1], axis=0)), ((1,), (1,)))
    part = x_length // (slabs * subs)
    rest = spectra.shape[2] - part
    for d in range(slabs):
        for e in range(subs):
            index = around(place[0] + d, slabs) * subs + around(place[1] + e, subs)
            spectra[d, e, :part] = wide[pl.ds(pl.multiple_of(index * part, part), part), :]
            spectra[d, e, part:] = wide_x[pl.ds(pl.multiple_of(index * rest, rest), rest), :]


def force_y_kernel(beyond, image, weight, basis, lower, spectra):
    planes, rows, x_length = image.shape
    row = lax.broadcasted_iota(jnp.int32, (rows, x_length), 0)
    force, along_x = [], []
    for z in range(planes):
        here = image[z]
        after = jnp.where(row == rows - 2, beyond[z : z + 1, :], pltpu.roll(here, rows - 2, 0))
        after = jnp.where(row == rows - 1, beyond[planes + z : planes + z + 1, :], after)
        own = pltpu.roll(weight[z], rows - 1, 0)
        own = jnp.where(row == rows - 1, beyond[2 * planes + z : 2 * planes + z + 1, :], own)
        force.append(own * (after - here))
        along_x.append(weight[z] * (pltpu.roll(here, x_length - 1, 1) - pltpu.roll(here, 1, 1)))
    devices = spectra.shape[0]
    part = x_length // devices
    spectrum = times((basis[0], basis[1]), split(jnp.concatenate(force, axis=0)), ((1,), (1,)))
    spectra[:, :part, :] = spectrum.reshape(devices, part, planes * rows)
    spectrum = times((lower[0], lower[1]), split(jnp.concatenate(along_x, axis=0)), ((1,), (1,)))
    spectra[:, part:, :] = spectrum.reshape(devices, -1, planes * rows)


def swap_blocks(values):
    width = values[0].shape[1]
    lane = lax.broadcasted_iota(jnp.int32, values[0].shape, 1)
    lower, even = lane < width // 2, lax.rem(lane // (width // 4), 2) == 0

    def turn(own, count):
        return pltpu.roll(own, count * (width // 4), 1)

    a, b, c, d = values
    a, c = jnp.where(lower, a, turn(c, 2)), jnp.where(lower, turn(a, 2), c)
    b, d = jnp.where(lower, b, turn(d, 2)), jnp.where(lower, turn(b, 2), d)
    return [
        jnp.where(even, a, turn(b, 1)),
        jnp.where(even, turn(a, 3), b),
        jnp.where(even, c, turn(d, 1)),
        jnp.where(even, turn(c, 3), d),
    ]


def solve(first, x_length, offsets, shifted, subs, spectra, basis_z, basis_y, out, cells):
    devices, used, area = spectra.shape
    total_z, _, total_y = cells.shape
    slabs = devices // subs
    planes, rows = total_z // slabs, total_y // subs
    fold = total_y // rows
    tile = 8

    def along_y(k, values):
        high, low = basis_y[2 * k], basis_y[2 * k + 1]
        four = jnp.concatenate(
            [jnp.concatenate([high, low], axis=1), jnp.concatenate([high, jnp.zeros_like(low)], axis=1)], axis=0
        )
        sums = jnp.dot(jnp.concatenate(split(values), axis=1), four, preferred_element_type=jnp.float32)
        return sums[:, :total_y] + sums[:, total_y:]

    def along_z(k, values):
        high, low = basis_z[2 * k], basis_z[2 * k + 1]
        parts = split(values)
        return jnp.dot(
            jnp.concatenate([high, high, low], axis=1),
            jnp.concatenate([parts[0], parts[1], parts[0]], axis=0),
            preferred_element_type=jnp.float32,
        )

    for s in range(slabs):
        own = []
        for f in range(0, planes // fold):
            lanes = slice(f * total_y, (f + 1) * total_y)
            own += swap_blocks([spectra[s * subs + q][:, lanes] for q in range(subs)])
        for low, high, table in ((0, shifted, 2), (shifted, used, 0)):
            if low < high:
                some = along_y(table, jnp.concatenate([o[low:high] for o in own], axis=0))
                cells[s * planes : (s + 1) * planes, low:high] = some.reshape(planes, high - low, total_y)
    index = lax.broadcasted_iota(jnp.int32, (total_z * tile, 1), 0)
    z_sq = wave_sq(index // tile, total_z)
    y_sq = wave_sq(lax.broadcasted_iota(jnp.int32, (1, total_y), 1), total_y)
    own, scale = [], []
    for start in range(0, used, tile):
        own.append(cells[:, start : start + tile, :].reshape(total_z * tile, total_y))
        x_sq = wave_sq(first + offsets[start // tile] + lax.rem(index, tile), x_length)
        scale.append((z_sq + y_sq) * (256.0 / (x_sq * 256.0 + 1.0)) + 1.0)
    own = along_z(0, jnp.concatenate(own, axis=1))
    own = along_z(1, own / jnp.concatenate(scale, axis=1))
    for k, start in enumerate(range(0, used, tile)):
        part = own[:, k * total_y : (k + 1) * total_y]
        cells[:, start : start + tile, :] = part.reshape(total_z, tile, total_y)
    for s in range(slabs):
        own = along_y(1, cells[s * planes : (s + 1) * planes].reshape(planes * used, total_y))
        for f in range(0, planes // fold):
            blocks = swap_blocks([own[z * used : (z + 1) * used] for z in range(f * fold, (f + 1) * fold)])
            for q in range(subs):
                out[s * subs + q, :, f * total_y : (f + 1) * total_y] = blocks[q]


def solve_yx_kernel(subs, x_length, place, spectra, basis_z, basis_y, out, cells):
    devices = out.shape[0]
    part = x_length // devices
    offsets = list(range(0, part, 8)) + list(range(0, out.shape[1] - part, 8))
    solve((place[0] * subs + place[1]) * part, x_length, offsets, part, subs, spectra, basis_z, basis_y, out, cells)


def solve_zx_kernel(slabs, subs, x_length, place, *refs):
    received, refs = refs[:subs], refs[subs:]
    basis_z, basis_y, sends, (spectra, cells) = refs[0], refs[1], refs[2 : 2 + slabs], refs[2 + slabs :]
    part = x_length // (slabs * subs)
    offsets = list(range(0, part, 8)) + list(range(2 * part - received[0].shape[1], part, 8))
    for e in range(subs):
        for d in range(slabs):
            spectra[around(place[0] - d, slabs) * subs + around(place[1] - e, subs)] = received[e][d]
    solve((place[0] * subs + place[1]) * part, x_length, offsets, 0, subs, spectra, basis_z, basis_y, spectra, cells)
    for d in range(slabs):
        for e in range(subs):
            sends[d][e] = spectra[around(place[0] + d, slabs) * subs + around(place[1] + e, subs)]


def moved(spectra, velocity, basis):
    smoothed = times(split(spectra.T), (basis[0], basis[1]), ((1,), (0,)))
    return 0.5 * (velocity - 32.0 * smoothed.reshape(velocity.shape))


def update_z_kernel(slabs, subs, place, basis, velocity, *refs):
    received, (out, kept, gathered) = refs[:subs], refs[subs:]
    part = received[0].shape[1] - kept.shape[1]
    for e in range(subs):
        for d in range(slabs):
            index = around(place[0] - d, slabs) * subs + around(place[1] - e, subs)
            gathered[pl.ds(pl.multiple_of(index * part, part), part), :] = received[e][d, :part]
            kept[index] = received[e][d, part:]
    out[...] = moved(gathered[...], velocity[0], basis)


def update_kernel(spectra, basis, velocity, updated, kept, out, result, done):
    devices, _, area = kept.shape
    part = (spectra.shape[1] + kept.shape[1]) // 2
    leaving = [pltpu.make_async_copy(updated, out.at[0], done.at[0])]
    leaving[0].start()
    for a in range(2):
        if a:
            own = jnp.concatenate([spectra[:, part:, :], kept[...]], axis=1)
        else:
            own = spectra[:, :part, :]
        high, low = split(own.reshape(devices * part, area).T)
        planes, rows, x_length = velocity.shape[1:]
        some = planes // 2
        for k in range(2):
            cells = slice(k * some * rows, (k + 1) * some * rows)
            smoothed = times((high[cells], low[cells]), (basis[0], basis[1]), ((1,), (0,)))
            own_planes = slice(k * some, (k + 1) * some)
            step = velocity[a + 1, own_planes] - 32.0 * smoothed.reshape(some, rows, x_length)
            result[a, own_planes] = 0.5 * step
            there = out.at[a + 1, pl.ds(k * some, some)]
            own_copy = pltpu.make_async_copy(result.at[a, pl.ds(k * some, some)], there, done.at[1 + 2 * a + k])
            own_copy.start()
            leaving.append(own_copy)
    for copy in leaving:
        copy.wait()


def place_kernel(slabs, place, *refs):
    received, warped = refs[:slabs], refs[slabs]
    for step in range(slabs):
        block = pl.ds(pl.multiple_of(around(place[0] - HOPS[step], slabs) * BLOCK, BLOCK), BLOCK)
        warped[:, :, block] = received[step][1:-1]


def local_blocks(velocity, template, moving, stiffness, fetch_plane, tissue):
    planes, rows, x_length = moving.shape
    slabs, subs = lax.axis_size("slab"), lax.axis_size("sub")
    total_z, total_y = planes * slabs, rows * subs
    devices = slabs * subs
    part = x_length // devices
    area = planes * rows
    place = jnp.stack([lax.axis_index("slab"), lax.axis_index("sub")])
    bf16, f16, f32 = jnp.bfloat16, jnp.float16, jnp.float32

    def shape(dims, kind=f32):
        return jax.ShapeDtypeStruct(dims, kind)

    def scatter(sends, axis, hops=(0, 1, 2, 3)):
        count = lax.axis_size(axis)
        return [sends[0]] + [
            lax.ppermute(sends[d], axis, [(i, (i + hops[d]) % count) for i in range(count)]) for d in range(1, count)
        ]

    def exchange(values):
        return lax.all_to_all(values, ("slab", "sub"), split_axis=0, concat_axis=0, tiled=True)

    fetch, marks = fetch_plane.swapaxes(1, 2), tissue.swapaxes(1, 2)
    coefficient = call(coefficient_kernel, shape(moving.shape), stiffness, marks, flops=1 << 30)
    sends = call(
        functools.partial(send_columns_kernel, slabs),
        [shape(((rows + 2) * planes, BLOCK), bf16)] * slabs,
        place,
        moving,
        fetch,
    )
    sends = call(
        functools.partial(pick_kernel, slabs),
        [shape((planes + 2, rows, BLOCK), bf16)] * slabs,
        place,
        *scatter(sends, "slab", HOPS),
        flops=1 << 30,
    )
    received = scatter(sends, "slab", HOPS)
    basis_x = in_two(real_basis(x_length))
    basis_z = np.kron(real_basis(total_z), np.eye(8))
    basis_z = np.concatenate([in_two(basis_z), in_two(basis_z.T)])
    basis_y = real_basis(total_y)
    basis_y = np.concatenate([in_two(b) for b in (basis_y.T, basis_y, np.roll(basis_y.T, -1, 0))])
    cut = part // 2
    with_z, with_y = 2 * part - cut, part + cut
    by_part = basis_x.reshape(2, devices, part, x_length)
    lower, upper = (h.reshape(2, -1, x_length) for h in (by_part[:, :, :cut], by_part[:, :, cut:]))
    first, image, weight, chain = call(
        functools.partial(force_zx_kernel, slabs, subs),
        [
            shape((3 * planes, x_length)),
            shape(moving.shape),
            shape(moving.shape),
            shape((slabs, subs, with_z, area)),
        ],
        place,
        *received,
        template,
        coefficient,
        basis_x,
        upper,
        scratch=[pltpu.VMEM((planes + 2, rows, x_length), f32), pltpu.VMEM((x_length, area), f32), pltpu.VMEM((devices * (part - cut), area), f32)],
        flops=3 << 30,
    )
    beyond = lax.ppermute(first, "sub", [((i + 1) % subs, i) for i in range(subs)])
    chain = chain.astype(f16)
    chain = scatter([chain[d] for d in range(slabs)], "slab")
    later, *chain = lax.optimization_barrier((place, *chain))
    warped = call(functools.partial(place_kernel, slabs), shape(moving.shape, bf16), later, *received)
    chain = scatter([jnp.stack([r[e] for r in chain]) for e in range(subs)], "sub")
    spectra = call(
        force_y_kernel,
        shape((devices, with_y, area)),
        beyond,
        image,
        weight,
        basis_x,
        lower,
        flops=2 << 30,
    )
    spectra = exchange(spectra.astype(f16))
    chain = call(
        functools.partial(solve_zx_kernel, slabs, subs, x_length),
        [shape((subs, with_z, area))] * slabs,
        place,
        *[r.astype(f32) for r in chain],
        basis_z,
        basis_y,
        scratch=[pltpu.VMEM((devices, with_z, area), f32), pltpu.VMEM((total_z, with_z, total_y), f32)],
        flops=2 << 30,
    )
    chain, spectra, warped = lax.optimization_barrier((chain, spectra, warped))
    chain = scatter([r.astype(f16) for r in chain], "slab")
    chain = scatter([jnp.stack([r[e] for r in chain]) for e in range(subs)], "sub")
    spectra = call(
        functools.partial(solve_yx_kernel, subs, x_length),
        shape((devices, with_y, area)),
        place,
        spectra.astype(f32),
        basis_z,
        basis_y,
        scratch=[pltpu.VMEM((total_z, with_y, total_y), f32)],
        flops=2 << 30,
    )
    spectra = exchange(spectra.astype(f16))
    x_wave = np.arange(x_length)
    x_wave = 2.0 * np.pi / x_length * np.where(x_wave <= x_length // 2, x_wave, x_wave - x_length // 2)
    basis_back = in_two(real_basis(x_length) / (256.0 * x_wave**2 + 1.0)[:, None])
    updated, kept = call(
        functools.partial(update_z_kernel, slabs, subs),
        [shape(moving.shape), shape((devices, part - cut, area))],
        place,
        basis_back,
        velocity,
        *[r.astype(f32) for r in chain],
        scratch=[pltpu.VMEM((x_length, area), f32)],
        flops=1 << 30,
    )
    new_velocity = call(
        update_kernel,
        shape(velocity.shape),
        spectra.astype(f32),
        basis_back,
        velocity,
        updated,
        kept,
        scratch=[pltpu.VMEM((2,) + moving.shape, f32), pltpu.SemaphoreType.DMA((5,))],
        flops=2 << 30,
        stays=1,
    )
    return (new_velocity, warped)


def local(velocity, template, moving, stiffness, fetch_plane, tissue):
    planes, rows, x_length = moving.shape
    slabs, subs = lax.axis_size("slab"), lax.axis_size("sub")
    fits = (
        x_length == slabs * BLOCK
        and planes == 8
        and planes * slabs * 8 == 256
        and rows % 16 == 0
        and rows * subs == BLOCK
        and slabs == subs == len(HOPS)
        and x_length % (32 * slabs * subs) == 0
    )
    run = local_blocks if fits else local_general
    return run(velocity, template, moving, stiffness, fetch_plane, tissue)


def solution(mesh):
    placed = (
        P(None, ("groups", "slab"), "sub", None),
        P(("groups", "slab"), "sub", None),
        P(("groups", "slab"), "sub", None),
        P(("groups", "slab"), "sub", None),
        P(("groups", "slab"), "sub", None),
        P(("groups", "slab"), "sub", None),
    )
    return jax.shard_map(
        local,
        mesh=mesh,
        in_specs=placed,
        out_specs=(P(None, ("groups", "slab"), "sub", None), P(("groups", "slab"), "sub", None)),
        check_vma=False,
    )
```

```python
import functools

import jax
import jax.numpy as jnp
import numpy as np
from jax import lax
from jax.experimental import pallas as pl
from jax.experimental.pallas import tpu as pltpu
from jax.sharding import PartitionSpec as P

BLOCK = 128


def extended(cells, sides, width):
    for axis, dim in sides:
        count = lax.axis_size(axis)
        head = lax.slice_in_dim(cells, 0, width, axis=dim)
        tail = lax.slice_in_dim(cells, cells.shape[dim] - width, cells.shape[dim], axis=dim)
        cells = jnp.concatenate(
            [
                lax.ppermute(tail, axis, [(i, (i + 1) % count) for i in range(count)]),
                cells,
                lax.ppermute(head, axis, [((i + 1) % count, i) for i in range(count)]),
            ],
            axis=dim,
        )
    return cells


def tables(length):
    wave_ids = jnp.arange(length, dtype=jnp.int32)
    phase = wave_ids[:, None] * wave_ids[None, :] % length
    angle = 2.0 * jnp.pi / length * phase.astype(jnp.float32)
    return (jnp.cos(angle), jnp.sin(angle))


def apply_along(values, matrix, axis_id):
    result = lax.dot_general(
        values,
        matrix,
        (((axis_id,), (0,)), ((), ())),
        precision=lax.Precision.HIGHEST,
        preferred_element_type=jnp.float32,
    )
    return jnp.moveaxis(result, -1, axis_id)


def forward_along(values_pair, axis_id):
    real_part, imag_part = values_pair
    cosine, sine = tables(real_part.shape[axis_id])
    return (
        apply_along(real_part, cosine, axis_id) + apply_along(imag_part, sine, axis_id),
        apply_along(imag_part, cosine, axis_id) - apply_along(real_part, sine, axis_id),
    )


def inverse_along(values_pair, axis_id):
    real_part, imag_part = values_pair
    length = real_part.shape[axis_id]
    cosine, sine = tables(length)
    scale = 1.0 / length
    return (
        (apply_along(real_part, cosine, axis_id) - apply_along(imag_part, sine, axis_id)) * scale,
        (apply_along(imag_part, cosine, axis_id) + apply_along(real_part, sine, axis_id)) * scale,
    )


def symbol_sq(length, first_id, span):
    wave_ids = first_id + jnp.arange(span, dtype=jnp.int32)
    signed = jnp.where(wave_ids < length // 2, wave_ids, wave_ids - length).astype(jnp.float32)
    wave = 2.0 * jnp.pi / length * signed
    return wave * wave


def local_general(velocity, template, moving, stiffness, fetch_plane, tissue):
    planes_dev, rows_dev, x_length = moving.shape
    blocks_x = x_length // BLOCK
    slabs = lax.axis_size("slab")
    subs = lax.axis_size("sub")
    my_slab = lax.axis_index("slab")
    my_sub = lax.axis_index("sub")
    per_dev = planes_dev * rows_dev * blocks_x
    capacity = 2 * per_dev // slabs
    source_plane = fetch_plane.reshape(-1)
    block_ids = jnp.arange(per_dev, dtype=jnp.int32)
    row_of = block_ids // blocks_x % rows_dev
    column_of = block_ids % blocks_x
    moving_rows = moving.reshape(per_dev, BLOCK)
    holder = source_plane // planes_dev
    within = (source_plane % planes_dev * rows_dev + row_of) * blocks_x + column_of
    matches = (holder[:, None] == jnp.arange(slabs, dtype=jnp.int32)[None, :]).astype(jnp.int32)
    earlier = jnp.sum((jnp.cumsum(matches, axis=0) - matches) * matches, axis=1)
    target = holder * capacity + earlier
    wanted = (
        jnp.zeros((slabs * capacity,), jnp.int32).at[target].set(within).reshape(slabs, capacity)
    )
    asked = lax.all_to_all(wanted, "slab", split_axis=0, concat_axis=0, tiled=True)
    fetched = moving_rows[asked.reshape(-1)].reshape(asked.shape + (BLOCK,))
    replies = lax.all_to_all(fetched, "slab", split_axis=0, concat_axis=0, tiled=True)
    warped_rows = replies.reshape(slabs * capacity, BLOCK)[target]
    warped = warped_rows.reshape(planes_dev, rows_dev, x_length)
    padded = extended(warped, (("slab", 0), ("sub", 1)), 1).astype(jnp.float32)
    image = padded[1:-1, 1:-1]
    grad_z = 0.5 * (padded[2:, 1:-1] - padded[:-2, 1:-1])
    grad_y = 0.5 * (padded[1:-1, 2:] - padded[1:-1, :-2])
    grad_x = 0.5 * (jnp.roll(image, -1, 2) - jnp.roll(image, 1, 2))
    residual = image - template.astype(jnp.float32)
    tissue_vox = jnp.repeat(tissue.astype(jnp.float32), BLOCK, axis=2)
    weight_field = tissue_vox * stiffness * residual
    force = jnp.stack([weight_field * grad_z, weight_field * grad_y, weight_field * grad_x])
    cos_x, sin_x = tables(x_length)
    real_part = apply_along(force, cos_x, 3)
    imag_part = -apply_along(force, sin_x, 3)
    moved = (
        lax.all_to_all(real_part, "sub", split_axis=3, concat_axis=2, tiled=True),
        lax.all_to_all(imag_part, "sub", split_axis=3, concat_axis=2, tiled=True),
    )
    moved = forward_along(moved, 2)
    moved = (
        lax.all_to_all(moved[0], "slab", split_axis=2, concat_axis=1, tiled=True),
        lax.all_to_all(moved[1], "slab", split_axis=2, concat_axis=1, tiled=True),
    )
    moved = forward_along(moved, 1)
    total_z = moved[0].shape[1]
    y_span = moved[0].shape[2]
    x_span = moved[0].shape[3]
    factor = 1.0 / (
        symbol_sq(total_z, 0, total_z)[:, None, None]
        + symbol_sq(y_span * slabs, my_slab * y_span, y_span)[None, :, None]
        + symbol_sq(x_span * subs, my_sub * x_span, x_span)[None, None, :]
        + 1.0 / 256.0
    )
    moved = (moved[0] * factor, moved[1] * factor)
    moved = inverse_along(moved, 1)
    moved = (
        lax.all_to_all(moved[0], "slab", split_axis=1, concat_axis=2, tiled=True),
        lax.all_to_all(moved[1], "slab", split_axis=1, concat_axis=2, tiled=True),
    )
    moved = inverse_along(moved, 2)
    real_part, imag_part = (
        lax.all_to_all(moved[0], "sub", split_axis=2, concat_axis=3, tiled=True),
        lax.all_to_all(moved[1], "sub", split_axis=2, concat_axis=3, tiled=True),
    )
    smoothed = (apply_along(real_part, cos_x, 3) - apply_along(imag_part, sin_x, 3)) * (
        1.0 / x_length
    )
    new_velocity = 0.5 * (velocity - smoothed)
    return (new_velocity, warped)


VMEM_BYTES = 24 * 1024 * 1024


def real_basis(length):
    index = np.arange(length)
    half = length // 2
    wave = np.where(index <= half, index, index - half)[:, None]
    angle = 2.0 * np.pi / length * (wave * index[None, :] % length)
    rows = np.where(index[:, None] <= half, np.cos(angle), np.sin(angle)) * np.sqrt(2.0 / length)
    rows[0] /= np.sqrt(2.0)
    rows[half] /= np.sqrt(2.0)
    return rows


def in_two(table):
    high = np.asarray(table, np.float32).astype(jnp.bfloat16)
    low = (np.asarray(table, np.float64) - high.astype(np.float64)).astype(jnp.bfloat16)
    return np.stack([high, low])


def split(values):
    high = values.astype(jnp.bfloat16)
    return high, (values - high.astype(jnp.float32)).astype(jnp.bfloat16)


def times(left, right, dims):
    def one(a, b):
        return lax.dot_general(a, b, (dims, ((), ())), preferred_element_type=jnp.float32)

    return one(left[0], right[0]) + (one(left[0], right[1]) + one(left[1], right[0]))


def wave_sq(index, length):
    wave = jnp.where(index <= length // 2, index, index - length // 2).astype(jnp.float32)
    wave = wave * (2.0 * np.pi / length)
    return wave * wave


HOPS = (0, 2, 1, 3)


def around(value, count):
    return lax.rem(value + 2 * count, count)


def call(kernel, out_shape, *arguments, scratch=(), flops=0, stays=0):
    places = [
        pl.BlockSpec(memory_space=pltpu.HBM if isinstance(a, tuple) else pltpu.SMEM if a.ndim == 1 else pltpu.VMEM)
        for a in arguments
    ]
    arguments = [a[0] if isinstance(a, tuple) else a for a in arguments]
    out_places = [
        pl.BlockSpec(memory_space=pltpu.HBM if k < stays else pltpu.VMEM)
        for k in range(len(jax.tree.leaves(out_shape)))
    ]
    nbytes = sum(a.size * a.dtype.itemsize for a in arguments + jax.tree.leaves(out_shape))
    return pl.pallas_call(
        kernel,
        out_shape=out_shape,
        in_specs=places,
        out_specs=jax.tree.unflatten(jax.tree.structure(out_shape), out_places),
        scratch_shapes=list(scratch),
        compiler_params=pltpu.CompilerParams(vmem_limit_bytes=VMEM_BYTES),
        cost_estimate=pl.CostEstimate(flops=flops, bytes_accessed=nbytes, transcendentals=0),
    )(*arguments)


def by_row(ref, rows):
    cells = jnp.concatenate([ref[z].astype(jnp.float32) for z in range(ref.shape[0])], axis=0)
    cells = jnp.concatenate([cells, jnp.zeros((cells.shape[0], BLOCK - rows), jnp.float32)], axis=1)
    cells = jnp.concatenate([cells, jnp.zeros((BLOCK - cells.shape[0], BLOCK), jnp.float32)], axis=0)
    return cells.T[:rows]


def send_columns_kernel(slabs, place, moving, fetch, *sends):
    planes, rows, _ = moving.shape
    for step, send in enumerate(sends):
        to = around(place[0] + HOPS[step], slabs)
        block = pl.ds(pl.multiple_of(to * BLOCK, BLOCK), BLOCK)
        for z in range(planes):
            send[z * rows : (z + 1) * rows] = moving[z, :, block]
        asked = jnp.concatenate([fetch[z, pl.ds(to, 1), :] for z in range(planes)] * 2, axis=0).astype(jnp.float32)
        asked = jnp.concatenate([asked, jnp.zeros((2 * planes, BLOCK - rows), jnp.float32)], axis=1)
        send[planes * rows :] = asked.astype(jnp.bfloat16)


def pick_kernel(slabs, place, *refs):
    received, sends = refs[:slabs], refs[slabs:]
    planes, rows = sends[0].shape[0] - 2, sends[0].shape[1]
    me = place[0]
    group = 4

    def name(other, plane):
        number = (around(me - HOPS[other], slabs) * planes).astype(jnp.float32) + float(plane)
        return jnp.full((rows, BLOCK), number, jnp.float32).astype(jnp.bfloat16)

    for step in range(slabs):
        names = received[step][planes * rows :].astype(jnp.float32)[:planes]
        names = jnp.concatenate([names, jnp.zeros((BLOCK - planes, BLOCK), jnp.float32)], axis=0).T[:rows]
        for start in range(0, planes, group):
            wanted = [
                jnp.broadcast_to(names[:, z : z + 1], (rows, BLOCK)).astype(jnp.bfloat16)
                for z in range(start, start + group)
            ]
            found = [jnp.zeros((rows, BLOCK), jnp.bfloat16) for _ in range(group)]
            for other in range(slabs):
                for plane in range(planes):
                    values = received[other][plane * rows : (plane + 1) * rows]
                    own = name(other, plane)
                    found = [jnp.where(w == own, values, f) for w, f in zip(wanted, found)]
            back = (slabs - HOPS[step]) % slabs
            for z in range(group):
                own = start + z
                sends[HOPS.index(back)][own + 1] = found[z]
                if own == 0:
                    sends[HOPS.index((back - 1) % slabs)][planes + 1] = found[z]
                if own == planes - 1:
                    sends[HOPS.index((back + 1) % slabs)][0] = found[z]


def coefficient_kernel(stiffness, tissue, out):
    planes, rows, x_length = stiffness.shape
    blocks = x_length // BLOCK
    marks = by_row(tissue, rows)
    for z in range(planes):
        marked = jnp.concatenate(
            [
                jnp.broadcast_to(marks[:, z * blocks + b : z * blocks + b + 1], (rows, BLOCK))
                for b in range(blocks)
            ],
            axis=1,
        )
        out[z] = 4.0 * marked * stiffness[z]


def force_zx_kernel(slabs, subs, place, *refs):
    received, refs = refs[:slabs], refs[slabs:]
    template, coefficient, basis, first, image, weight, spectra, kept, planes_of, wide = refs
    planes, rows, x_length = template.shape
    for step in range(slabs):
        block = pl.ds(pl.multiple_of(around(place[0] - HOPS[step], slabs) * BLOCK, BLOCK), BLOCK)
        planes_of[:, :, block] = received[step][...].astype(jnp.float32)
    forces = [[], []]
    for z in range(planes):
        here = planes_of[z + 1]
        own = coefficient[z] * (here - template[z].astype(jnp.float32))
        image[z] = here
        weight[z] = own
        first[z : z + 1] = here[0:1]
        first[planes + z : planes + z + 1] = here[1:2]
        first[2 * planes + z : 2 * planes + z + 1] = own[0:1]
        forces[0].append(own * (planes_of[z + 2] - planes_of[z]))
        forces[1].append(own * (pltpu.roll(here, x_length - 1, 1) - pltpu.roll(here, 1, 1)))
    for a in range(2):
        force = split(jnp.concatenate(forces[a], axis=0))
        wide[a] = times((basis[0], basis[1]), force, ((1,), (1,)))
    part = x_length // (slabs * subs)
    cut = kept.shape[1]
    for d in range(slabs):
        for e in range(subs):
            start = (around(place[0] + d, slabs) * subs + around(place[1] + e, subs)) * part
            spectra[d, e, :part] = wide[0, pl.ds(pl.multiple_of(start, part), part), :]
            spectra[d, e, part:] = wide[1, pl.ds(pl.multiple_of(start + cut, 8), part - cut), :]
    for k in range(slabs * subs):
        kept[k] = wide[1, k * part : k * part + cut, :]


def force_y_kernel(beyond, image, weight, basis, kept, spectra):
    planes, rows, x_length = image.shape
    row = lax.broadcasted_iota(jnp.int32, (rows, x_length), 0)
    force = []
    for z in range(planes):
        here = image[z]
        after = jnp.where(row == rows - 2, beyond[z : z + 1, :], pltpu.roll(here, rows - 2, 0))
        after = jnp.where(row == rows - 1, beyond[planes + z : planes + z + 1, :], after)
        own = pltpu.roll(weight[z], rows - 1, 0)
        own = jnp.where(row == rows - 1, beyond[2 * planes + z : 2 * planes + z + 1, :], own)
        force.append(own * (after - here))
    devices = spectra.shape[0]
    part = x_length // devices
    spectrum = times((basis[0], basis[1]), split(jnp.concatenate(force, axis=0)), ((1,), (1,)))
    spectra[:, :part, :] = spectrum.reshape(devices, part, planes * rows)
    spectra[:, part:, :] = kept[...]


def swap_blocks(values):
    width = values[0].shape[1]
    lane = lax.broadcasted_iota(jnp.int32, values[0].shape, 1)
    lower, even = lane < width // 2, lax.rem(lane // (width // 4), 2) == 0

    def turn(own, count):
        return pltpu.roll(own, count * (width // 4), 1)

    a, b, c, d = values
    a, c = jnp.where(lower, a, turn(c, 2)), jnp.where(lower, turn(a, 2), c)
    b, d = jnp.where(lower, b, turn(d, 2)), jnp.where(lower, turn(b, 2), d)
    return [
        jnp.where(even, a, turn(b, 1)),
        jnp.where(even, turn(a, 3), b),
        jnp.where(even, c, turn(d, 1)),
        jnp.where(even, turn(c, 3), d),
    ]


def solve(first, x_length, offsets, shifted, subs, spectra, basis_z, basis_y, out, cells):
    devices, used, area = spectra.shape
    total_z, _, total_y = cells.shape
    slabs = devices // subs
    planes, rows = total_z // slabs, total_y // subs
    fold = total_y // rows
    tile = 8

    def along_y(k, values):
        high, low = basis_y[2 * k], basis_y[2 * k + 1]
        four = jnp.concatenate(
            [jnp.concatenate([high, low], axis=1), jnp.concatenate([high, jnp.zeros_like(low)], axis=1)], axis=0
        )
        sums = jnp.dot(jnp.concatenate(split(values), axis=1), four, preferred_element_type=jnp.float32)
        return sums[:, :total_y] + sums[:, total_y:]

    def along_z(k, values):
        high, low = basis_z[2 * k], basis_z[2 * k + 1]
        parts = split(values)
        return jnp.dot(
            jnp.concatenate([high, high, low], axis=1),
            jnp.concatenate([parts[0], parts[1], parts[0]], axis=0),
            preferred_element_type=jnp.float32,
        )

    for s in range(slabs):
        own = []
        for f in range(0, planes // fold):
            lanes = slice(f * total_y, (f + 1) * total_y)
            own += swap_blocks([spectra[s * subs + q][:, lanes] for q in range(subs)])
        for low, high, table in ((0, shifted, 2), (shifted, used, 0)):
            if low < high:
                some = along_y(table, jnp.concatenate([o[low:high] for o in own], axis=0))
                cells[s * planes : (s + 1) * planes, low:high] = some.reshape(planes, high - low, total_y)
    index = lax.broadcasted_iota(jnp.int32, (total_z * tile, 1), 0)
    z_sq = wave_sq(index // tile, total_z)
    y_sq = wave_sq(lax.broadcasted_iota(jnp.int32, (1, total_y), 1), total_y)
    own, scale = [], []
    for start in range(0, used, tile):
        own.append(cells[:, start : start + tile, :].reshape(total_z * tile, total_y))
        x_sq = wave_sq(first + offsets[start // tile] + lax.rem(index, tile), x_length)
        scale.append((z_sq + y_sq) * (256.0 / (x_sq * 256.0 + 1.0)) + 1.0)
    own = along_z(0, jnp.concatenate(own, axis=1))
    own = along_z(1, own / jnp.concatenate(scale, axis=1))
    for k, start in enumerate(range(0, used, tile)):
        part = own[:, k * total_y : (k + 1) * total_y]
        cells[:, start : start + tile, :] = part.reshape(total_z, tile, total_y)
    for s in range(slabs):
        own = along_y(1, cells[s * planes : (s + 1) * planes].reshape(planes * used, total_y))
        for f in range(0, planes // fold):
            blocks = swap_blocks([own[z * used : (z + 1) * used] for z in range(f * fold, (f + 1) * fold)])
            for q in range(subs):
                out[s * subs + q, :, f * total_y : (f + 1) * total_y] = blocks[q]


def solve_yx_kernel(subs, x_length, place, spectra, basis_z, basis_y, out, cells):
    devices = out.shape[0]
    part = x_length // devices
    offsets = list(range(0, part, 8)) + list(range(0, out.shape[1] - part, 8))
    solve((place[0] * subs + place[1]) * part, x_length, offsets, part, subs, spectra, basis_z, basis_y, out, cells)


def solve_zx_kernel(slabs, subs, x_length, place, *refs):
    received, refs = refs[:subs], refs[subs:]
    basis_z, basis_y, sends, (spectra, cells) = refs[0], refs[1], refs[2 : 2 + slabs], refs[2 + slabs :]
    part = x_length // (slabs * subs)
    offsets = list(range(0, part, 8)) + list(range(2 * part - received[0].shape[1], part, 8))
    for e in range(subs):
        for d in range(slabs):
            spectra[around(place[0] - d, slabs) * subs + around(place[1] - e, subs)] = received[e][d]
    solve((place[0] * subs + place[1]) * part, x_length, offsets, 0, subs, spectra, basis_z, basis_y, spectra, cells)
    for d in range(slabs):
        for e in range(subs):
            sends[d][e] = spectra[around(place[0] + d, slabs) * subs + around(place[1] + e, subs)]


def moved(spectra, velocity, basis):
    smoothed = times(split(spectra.T), (basis[0], basis[1]), ((1,), (0,)))
    return 0.5 * (velocity - 32.0 * smoothed.reshape(velocity.shape))


def update_z_kernel(slabs, subs, place, basis, velocity, *refs):
    received, (out, kept, gathered) = refs[:subs], refs[subs:]
    part = received[0].shape[1] - kept.shape[1]
    for e in range(subs):
        for d in range(slabs):
            index = around(place[0] - d, slabs) * subs + around(place[1] - e, subs)
            gathered[pl.ds(pl.multiple_of(index * part, part), part), :] = received[e][d, :part]
            kept[index] = received[e][d, part:]
    out[...] = moved(gathered[...], velocity[0], basis)


def update_kernel(spectra, basis, velocity, updated, kept, out, result, done):
    devices, _, area = kept.shape
    part = (spectra.shape[1] + kept.shape[1]) // 2
    leaving = [pltpu.make_async_copy(updated, out.at[0], done.at[0])]
    leaving[0].start()
    for a in range(2):
        if a:
            own = jnp.concatenate([spectra[:, part:, :], kept[...]], axis=1)
        else:
            own = spectra[:, :part, :]
        high, low = split(own.reshape(devices * part, area).T)
        planes, rows, x_length = velocity.shape[1:]
        some = planes // 2
        for k in range(2):
            cells = slice(k * some * rows, (k + 1) * some * rows)
            smoothed = times((high[cells], low[cells]), (basis[0], basis[1]), ((1,), (0,)))
            own_planes = slice(k * some, (k + 1) * some)
            step = velocity[a + 1, own_planes] - 32.0 * smoothed.reshape(some, rows, x_length)
            result[a, own_planes] = 0.5 * step
            there = out.at[a + 1, pl.ds(k * some, some)]
            own_copy = pltpu.make_async_copy(result.at[a, pl.ds(k * some, some)], there, done.at[1 + 2 * a + k])
            own_copy.start()
            leaving.append(own_copy)
    for copy in leaving:
        copy.wait()


def place_kernel(slabs, place, *refs):
    received, warped = refs[:slabs], refs[slabs]
    for step in range(slabs):
        block = pl.ds(pl.multiple_of(around(place[0] - HOPS[step], slabs) * BLOCK, BLOCK), BLOCK)
        warped[:, :, block] = received[step][1:-1]


def local_blocks(velocity, template, moving, stiffness, fetch_plane, tissue):
    planes, rows, x_length = moving.shape
    slabs, subs = lax.axis_size("slab"), lax.axis_size("sub")
    total_z, total_y = planes * slabs, rows * subs
    devices = slabs * subs
    part = x_length // devices
    area = planes * rows
    place = jnp.stack([lax.axis_index("slab"), lax.axis_index("sub")])
    bf16, f16, f32 = jnp.bfloat16, jnp.float16, jnp.float32

    def shape(dims, kind=f32):
        return jax.ShapeDtypeStruct(dims, kind)

    def scatter(sends, axis, hops=(0, 1, 2, 3)):
        count = lax.axis_size(axis)
        return [sends[0]] + [
            lax.ppermute(sends[d], axis, [(i, (i + hops[d]) % count) for i in range(count)]) for d in range(1, count)
        ]

    def exchange(values):
        return lax.all_to_all(values, ("slab", "sub"), split_axis=0, concat_axis=0, tiled=True)

    fetch, marks = fetch_plane.swapaxes(1, 2), tissue.swapaxes(1, 2)
    coefficient = call(coefficient_kernel, shape(moving.shape), stiffness, marks, flops=1 << 30)
    sends = call(
        functools.partial(send_columns_kernel, slabs),
        [shape(((rows + 2) * planes, BLOCK), bf16)] * slabs,
        place,
        moving,
        fetch,
    )
    sends = call(
        functools.partial(pick_kernel, slabs),
        [shape((planes + 2, rows, BLOCK), bf16)] * slabs,
        place,
        *scatter(sends, "slab", HOPS),
        flops=1 << 30,
    )
    received = scatter(sends, "slab", HOPS)
    basis_x = in_two(real_basis(x_length))
    basis_z = np.kron(real_basis(total_z), np.eye(8))
    basis_z = np.concatenate([in_two(basis_z), in_two(basis_z.T)])
    basis_y = real_basis(total_y)
    basis_y = np.concatenate([in_two(b) for b in (basis_y.T, basis_y, np.roll(basis_y.T, -1, 0))])
    cut = part // 2
    with_z, with_y = 2 * part - cut, part + cut
    first, image, weight, chain, kept = call(
        functools.partial(force_zx_kernel, slabs, subs),
        [
            shape((3 * planes, x_length)),
            shape(moving.shape),
            shape(moving.shape),
            shape((slabs, subs, with_z, area)),
            shape((devices, cut, area)),
        ],
        place,
        *received,
        template,
        coefficient,
        basis_x,
        scratch=[pltpu.VMEM((planes + 2, rows, x_length), f32), pltpu.VMEM((2, x_length, area), f32)],
        flops=3 << 30,
    )
    beyond = lax.ppermute(first, "sub", [((i + 1) % subs, i) for i in range(subs)])
    chain = chain.astype(f16)
    chain = scatter([chain[d] for d in HOPS], "slab", HOPS)
    chain = [chain[HOPS.index(d)] for d in range(slabs)]
    later, *chain = lax.optimization_barrier((place, *chain))
    warped = call(functools.partial(place_kernel, slabs), shape(moving.shape, bf16), later, *received)
    chain = scatter([jnp.stack([r[e] for r in chain]) for e in range(subs)], "sub")
    spectra = call(
        force_y_kernel,
        shape((devices, with_y, area)),
        beyond,
        image,
        weight,
        basis_x,
        kept,
        flops=2 << 30,
    )
    spectra = exchange(spectra.astype(f16))
    chain = call(
        functools.partial(solve_zx_kernel, slabs, subs, x_length),
        [shape((subs, with_z, area))] * slabs,
        place,
        *[r.astype(f32) for r in chain],
        basis_z,
        basis_y,
        scratch=[pltpu.VMEM((devices, with_z, area), f32), pltpu.VMEM((total_z, with_z, total_y), f32)],
        flops=2 << 30,
    )
    chain, spectra, warped = lax.optimization_barrier((chain, spectra, warped))
    chain = scatter([chain[d].astype(f16) for d in HOPS], "slab", HOPS)
    chain = [chain[HOPS.index(d)] for d in range(slabs)]
    chain = scatter([jnp.stack([r[e] for r in chain]) for e in range(subs)], "sub")
    spectra = call(
        functools.partial(solve_yx_kernel, subs, x_length),
        shape((devices, with_y, area)),
        place,
        spectra.astype(f32),
        basis_z,
        basis_y,
        scratch=[pltpu.VMEM((total_z, with_y, total_y), f32)],
        flops=2 << 30,
    )
    spectra = exchange(spectra.astype(f16))
    x_wave = np.arange(x_length)
    x_wave = 2.0 * np.pi / x_length * np.where(x_wave <= x_length // 2, x_wave, x_wave - x_length // 2)
    basis_back = in_two(real_basis(x_length) / (256.0 * x_wave**2 + 1.0)[:, None])
    updated, kept = call(
        functools.partial(update_z_kernel, slabs, subs),
        [shape(moving.shape), shape((devices, part - cut, area))],
        place,
        basis_back,
        velocity,
        *[r.astype(f32) for r in chain],
        scratch=[pltpu.VMEM((x_length, area), f32)],
        flops=1 << 30,
    )
    new_velocity = call(
        update_kernel,
        shape(velocity.shape),
        spectra.astype(f32),
        basis_back,
        velocity,
        updated,
        kept,
        scratch=[pltpu.VMEM((2,) + moving.shape, f32), pltpu.SemaphoreType.DMA((5,))],
        flops=2 << 30,
        stays=1,
    )
    return (new_velocity, warped)


def local(velocity, template, moving, stiffness, fetch_plane, tissue):
    planes, rows, x_length = moving.shape
    slabs, subs = lax.axis_size("slab"), lax.axis_size("sub")
    fits = (
        x_length == slabs * BLOCK
        and planes == 8
        and planes * slabs * 8 == 256
        and rows % 16 == 0
        and rows * subs == BLOCK
        and slabs == subs == len(HOPS)
        and x_length % (32 * slabs * subs) == 0
    )
    run = local_blocks if fits else local_general
    return run(velocity, template, moving, stiffness, fetch_plane, tissue)


def solution(mesh):
    placed = (
        P(None, ("groups", "slab"), "sub", None),
        P(("groups", "slab"), "sub", None),
        P(("groups", "slab"), "sub", None),
        P(("groups", "slab"), "sub", None),
        P(("groups", "slab"), "sub", None),
        P(("groups", "slab"), "sub", None),
    )
    return jax.shard_map(
        local,
        mesh=mesh,
        in_specs=placed,
        out_specs=(P(None, ("groups", "slab"), "sub", None), P(("groups", "slab"), "sub", None)),
        check_vma=False,
    )
```

```python
import functools

import jax
import jax.numpy as jnp
import numpy as np
from jax import lax
from jax.experimental import pallas as pl
from jax.experimental.pallas import tpu as pltpu
from jax.sharding import PartitionSpec as P

BLOCK = 128


def extended(cells, sides, width):
    for axis, dim in sides:
        count = lax.axis_size(axis)
        head = lax.slice_in_dim(cells, 0, width, axis=dim)
        tail = lax.slice_in_dim(cells, cells.shape[dim] - width, cells.shape[dim], axis=dim)
        cells = jnp.concatenate(
            [
                lax.ppermute(tail, axis, [(i, (i + 1) % count) for i in range(count)]),
                cells,
                lax.ppermute(head, axis, [((i + 1) % count, i) for i in range(count)]),
            ],
            axis=dim,
        )
    return cells


def tables(length):
    wave_ids = jnp.arange(length, dtype=jnp.int32)
    phase = wave_ids[:, None] * wave_ids[None, :] % length
    angle = 2.0 * jnp.pi / length * phase.astype(jnp.float32)
    return (jnp.cos(angle), jnp.sin(angle))


def apply_along(values, matrix, axis_id):
    result = lax.dot_general(
        values,
        matrix,
        (((axis_id,), (0,)), ((), ())),
        precision=lax.Precision.HIGHEST,
        preferred_element_type=jnp.float32,
    )
    return jnp.moveaxis(result, -1, axis_id)


def forward_along(values_pair, axis_id):
    real_part, imag_part = values_pair
    cosine, sine = tables(real_part.shape[axis_id])
    return (
        apply_along(real_part, cosine, axis_id) + apply_along(imag_part, sine, axis_id),
        apply_along(imag_part, cosine, axis_id) - apply_along(real_part, sine, axis_id),
    )


def inverse_along(values_pair, axis_id):
    real_part, imag_part = values_pair
    length = real_part.shape[axis_id]
    cosine, sine = tables(length)
    scale = 1.0 / length
    return (
        (apply_along(real_part, cosine, axis_id) - apply_along(imag_part, sine, axis_id)) * scale,
        (apply_along(imag_part, cosine, axis_id) + apply_along(real_part, sine, axis_id)) * scale,
    )


def symbol_sq(length, first_id, span):
    wave_ids = first_id + jnp.arange(span, dtype=jnp.int32)
    signed = jnp.where(wave_ids < length // 2, wave_ids, wave_ids - length).astype(jnp.float32)
    wave = 2.0 * jnp.pi / length * signed
    return wave * wave


def local_general(velocity, template, moving, stiffness, fetch_plane, tissue):
    planes_dev, rows_dev, x_length = moving.shape
    blocks_x = x_length // BLOCK
    slabs = lax.axis_size("slab")
    subs = lax.axis_size("sub")
    my_slab = lax.axis_index("slab")
    my_sub = lax.axis_index("sub")
    per_dev = planes_dev * rows_dev * blocks_x
    capacity = 2 * per_dev // slabs
    source_plane = fetch_plane.reshape(-1)
    block_ids = jnp.arange(per_dev, dtype=jnp.int32)
    row_of = block_ids // blocks_x % rows_dev
    column_of = block_ids % blocks_x
    moving_rows = moving.reshape(per_dev, BLOCK)
    holder = source_plane // planes_dev
    within = (source_plane % planes_dev * rows_dev + row_of) * blocks_x + column_of
    matches = (holder[:, None] == jnp.arange(slabs, dtype=jnp.int32)[None, :]).astype(jnp.int32)
    earlier = jnp.sum((jnp.cumsum(matches, axis=0) - matches) * matches, axis=1)
    target = holder * capacity + earlier
    wanted = (
        jnp.zeros((slabs * capacity,), jnp.int32).at[target].set(within).reshape(slabs, capacity)
    )
    asked = lax.all_to_all(wanted, "slab", split_axis=0, concat_axis=0, tiled=True)
    fetched = moving_rows[asked.reshape(-1)].reshape(asked.shape + (BLOCK,))
    replies = lax.all_to_all(fetched, "slab", split_axis=0, concat_axis=0, tiled=True)
    warped_rows = replies.reshape(slabs * capacity, BLOCK)[target]
    warped = warped_rows.reshape(planes_dev, rows_dev, x_length)
    padded = extended(warped, (("slab", 0), ("sub", 1)), 1).astype(jnp.float32)
    image = padded[1:-1, 1:-1]
    grad_z = 0.5 * (padded[2:, 1:-1] - padded[:-2, 1:-1])
    grad_y = 0.5 * (padded[1:-1, 2:] - padded[1:-1, :-2])
    grad_x = 0.5 * (jnp.roll(image, -1, 2) - jnp.roll(image, 1, 2))
    residual = image - template.astype(jnp.float32)
    tissue_vox = jnp.repeat(tissue.astype(jnp.float32), BLOCK, axis=2)
    weight_field = tissue_vox * stiffness * residual
    force = jnp.stack([weight_field * grad_z, weight_field * grad_y, weight_field * grad_x])
    cos_x, sin_x = tables(x_length)
    real_part = apply_along(force, cos_x, 3)
    imag_part = -apply_along(force, sin_x, 3)
    moved = (
        lax.all_to_all(real_part, "sub", split_axis=3, concat_axis=2, tiled=True),
        lax.all_to_all(imag_part, "sub", split_axis=3, concat_axis=2, tiled=True),
    )
    moved = forward_along(moved, 2)
    moved = (
        lax.all_to_all(moved[0], "slab", split_axis=2, concat_axis=1, tiled=True),
        lax.all_to_all(moved[1], "slab", split_axis=2, concat_axis=1, tiled=True),
    )
    moved = forward_along(moved, 1)
    total_z = moved[0].shape[1]
    y_span = moved[0].shape[2]
    x_span = moved[0].shape[3]
    factor = 1.0 / (
        symbol_sq(total_z, 0, total_z)[:, None, None]
        + symbol_sq(y_span * slabs, my_slab * y_span, y_span)[None, :, None]
        + symbol_sq(x_span * subs, my_sub * x_span, x_span)[None, None, :]
        + 1.0 / 256.0
    )
    moved = (moved[0] * factor, moved[1] * factor)
    moved = inverse_along(moved, 1)
    moved = (
        lax.all_to_all(moved[0], "slab", split_axis=1, concat_axis=2, tiled=True),
        lax.all_to_all(moved[1], "slab", split_axis=1, concat_axis=2, tiled=True),
    )
    moved = inverse_along(moved, 2)
    real_part, imag_part = (
        lax.all_to_all(moved[0], "sub", split_axis=2, concat_axis=3, tiled=True),
        lax.all_to_all(moved[1], "sub", split_axis=2, concat_axis=3, tiled=True),
    )
    smoothed = (apply_along(real_part, cos_x, 3) - apply_along(imag_part, sin_x, 3)) * (
        1.0 / x_length
    )
    new_velocity = 0.5 * (velocity - smoothed)
    return (new_velocity, warped)


VMEM_BYTES = 24 * 1024 * 1024


def real_basis(length):
    index = np.arange(length)
    half = length // 2
    wave = np.where(index <= half, index, index - half)[:, None]
    angle = 2.0 * np.pi / length * (wave * index[None, :] % length)
    rows = np.where(index[:, None] <= half, np.cos(angle), np.sin(angle)) * np.sqrt(2.0 / length)
    rows[0] /= np.sqrt(2.0)
    rows[half] /= np.sqrt(2.0)
    return rows


def in_two(table):
    high = np.asarray(table, np.float32).astype(jnp.bfloat16)
    low = (np.asarray(table, np.float64) - high.astype(np.float64)).astype(jnp.bfloat16)
    return np.stack([high, low])


def split(values):
    high = values.astype(jnp.bfloat16)
    return high, (values - high.astype(jnp.float32)).astype(jnp.bfloat16)


def times(left, right, dims):
    def one(a, b):
        return lax.dot_general(a, b, (dims, ((), ())), preferred_element_type=jnp.float32)

    return one(left[0], right[0]) + (one(left[0], right[1]) + one(left[1], right[0]))


def wave_sq(index, length):
    wave = jnp.where(index <= length // 2, index, index - length // 2).astype(jnp.float32)
    wave = wave * (2.0 * np.pi / length)
    return wave * wave


HOPS = (0, 2, 3, 1)


def around(value, count):
    return lax.rem(value + 2 * count, count)


def call(kernel, out_shape, *arguments, scratch=(), flops=0, stays=0):
    places = [
        pl.BlockSpec(memory_space=pltpu.HBM if isinstance(a, tuple) else pltpu.SMEM if a.ndim == 1 else pltpu.VMEM)
        for a in arguments
    ]
    arguments = [a[0] if isinstance(a, tuple) else a for a in arguments]
    out_places = [
        pl.BlockSpec(memory_space=pltpu.HBM if k < stays else pltpu.VMEM)
        for k in range(len(jax.tree.leaves(out_shape)))
    ]
    nbytes = sum(a.size * a.dtype.itemsize for a in arguments + jax.tree.leaves(out_shape))
    return pl.pallas_call(
        kernel,
        out_shape=out_shape,
        in_specs=places,
        out_specs=jax.tree.unflatten(jax.tree.structure(out_shape), out_places),
        scratch_shapes=list(scratch),
        compiler_params=pltpu.CompilerParams(vmem_limit_bytes=VMEM_BYTES),
        cost_estimate=pl.CostEstimate(flops=flops, bytes_accessed=nbytes, transcendentals=0),
    )(*arguments)


def by_row(ref, rows):
    cells = jnp.concatenate([ref[z].astype(jnp.float32) for z in range(ref.shape[0])], axis=0)
    cells = jnp.concatenate([cells, jnp.zeros((cells.shape[0], BLOCK - rows), jnp.float32)], axis=1)
    cells = jnp.concatenate([cells, jnp.zeros((BLOCK - cells.shape[0], BLOCK), jnp.float32)], axis=0)
    return cells.T[:rows]


def send_columns_kernel(slabs, place, moving, fetch, *sends):
    planes, rows, _ = moving.shape
    for step, send in enumerate(sends):
        to = around(place[0] + HOPS[step], slabs)
        block = pl.ds(pl.multiple_of(to * BLOCK, BLOCK), BLOCK)
        for z in range(planes):
            send[z * rows : (z + 1) * rows] = moving[z, :, block]
        asked = jnp.concatenate([fetch[z, pl.ds(to, 1), :] for z in range(planes)] * 2, axis=0).astype(jnp.float32)
        asked = jnp.concatenate([asked, jnp.zeros((2 * planes, BLOCK - rows), jnp.float32)], axis=1)
        send[planes * rows :] = asked.astype(jnp.bfloat16)


def pick_kernel(slabs, place, *refs):
    received, sends = refs[:slabs], refs[slabs:]
    planes, rows = sends[0].shape[0] - 2, sends[0].shape[1]
    me = place[0]
    group = 4

    def name(other, plane):
        number = (around(me - HOPS[other], slabs) * planes).astype(jnp.float32) + float(plane)
        return jnp.full((rows, BLOCK), number, jnp.float32).astype(jnp.bfloat16)

    for step in range(slabs):
        names = received[step][planes * rows :].astype(jnp.float32)[:planes]
        names = jnp.concatenate([names, jnp.zeros((BLOCK - planes, BLOCK), jnp.float32)], axis=0).T[:rows]
        for start in range(0, planes, group):
            wanted = [
                jnp.broadcast_to(names[:, z : z + 1], (rows, BLOCK)).astype(jnp.bfloat16)
                for z in range(start, start + group)
            ]
            found = [jnp.zeros((rows, BLOCK), jnp.bfloat16) for _ in range(group)]
            for other in range(slabs):
                for plane in range(planes):
                    values = received[other][plane * rows : (plane + 1) * rows]
                    own = name(other, plane)
                    found = [jnp.where(w == own, values, f) for w, f in zip(wanted, found)]
            back = (slabs - HOPS[step]) % slabs
            for z in range(group):
                own = start + z
                sends[HOPS.index(back)][own + 1] = found[z]
                if own == 0:
                    sends[HOPS.index((back - 1) % slabs)][planes + 1] = found[z]
                if own == planes - 1:
                    sends[HOPS.index((back + 1) % slabs)][0] = found[z]


def coefficient_kernel(stiffness, tissue, out):
    planes, rows, x_length = stiffness.shape
    blocks = x_length // BLOCK
    marks = by_row(tissue, rows)
    for z in range(planes):
        marked = jnp.concatenate(
            [
                jnp.broadcast_to(marks[:, z * blocks + b : z * blocks + b + 1], (rows, BLOCK))
                for b in range(blocks)
            ],
            axis=1,
        )
        out[z] = 4.0 * marked * stiffness[z]


def force_zx_kernel(slabs, subs, place, *refs):
    received, refs = refs[:slabs], refs[slabs:]
    template, coefficient, basis, first, image, weight, spectra, kept, planes_of, wide = refs
    planes, rows, x_length = template.shape
    for step in range(slabs):
        block = pl.ds(pl.multiple_of(around(place[0] - HOPS[step], slabs) * BLOCK, BLOCK), BLOCK)
        planes_of[:, :, block] = received[step][...].astype(jnp.float32)
    forces = [[], []]
    for z in range(planes):
        here = planes_of[z + 1]
        own = coefficient[z] * (here - template[z].astype(jnp.float32))
        image[z] = here
        weight[z] = own
        first[z : z + 1] = here[0:1]
        first[planes + z : planes + z + 1] = here[1:2]
        first[2 * planes + z : 2 * planes + z + 1] = own[0:1]
        forces[0].append(own * (planes_of[z + 2] - planes_of[z]))
        forces[1].append(own * (pltpu.roll(here, x_length - 1, 1) - pltpu.roll(here, 1, 1)))
    for a in range(2):
        force = split(jnp.concatenate(forces[a], axis=0))
        wide[a] = times((basis[0], basis[1]), force, ((1,), (1,)))
    part = x_length // (slabs * subs)
    cut = kept.shape[1]
    for d in range(slabs):
        for e in range(subs):
            start = (around(place[0] + d, slabs) * subs + around(place[1] + e, subs)) * part
            spectra[d, e, :part] = wide[0, pl.ds(pl.multiple_of(start, part), part), :]
            spectra[d, e, part:] = wide[1, pl.ds(pl.multiple_of(start + cut, 8), part - cut), :]
    for k in range(slabs * subs):
        kept[k] = wide[1, k * part : k * part + cut, :]


def force_y_kernel(beyond, image, weight, basis, kept, spectra):
    planes, rows, x_length = image.shape
    row = lax.broadcasted_iota(jnp.int32, (rows, x_length), 0)
    force = []
    for z in range(planes):
        here = image[z]
        after = jnp.where(row == rows - 2, beyond[z : z + 1, :], pltpu.roll(here, rows - 2, 0))
        after = jnp.where(row == rows - 1, beyond[planes + z : planes + z + 1, :], after)
        own = pltpu.roll(weight[z], rows - 1, 0)
        own = jnp.where(row == rows - 1, beyond[2 * planes + z : 2 * planes + z + 1, :], own)
        force.append(own * (after - here))
    devices = spectra.shape[0]
    part = x_length // devices
    spectrum = times((basis[0], basis[1]), split(jnp.concatenate(force, axis=0)), ((1,), (1,)))
    spectra[:, :part, :] = spectrum.reshape(devices, part, planes * rows)
    spectra[:, part:, :] = kept[...]


def swap_blocks(values):
    width = values[0].shape[1]
    lane = lax.broadcasted_iota(jnp.int32, values[0].shape, 1)
    lower, even = lane < width // 2, lax.rem(lane // (width // 4), 2) == 0

    def turn(own, count):
        return pltpu.roll(own, count * (width // 4), 1)

    a, b, c, d = values
    a, c = jnp.where(lower, a, turn(c, 2)), jnp.where(lower, turn(a, 2), c)
    b, d = jnp.where(lower, b, turn(d, 2)), jnp.where(lower, turn(b, 2), d)
    return [
        jnp.where(even, a, turn(b, 1)),
        jnp.where(even, turn(a, 3), b),
        jnp.where(even, c, turn(d, 1)),
        jnp.where(even, turn(c, 3), d),
    ]


def solve(first, x_length, offsets, shifted, subs, spectra, basis_z, basis_y, out, cells):
    devices, used, area = spectra.shape
    total_z, _, total_y = cells.shape
    slabs = devices // subs
    planes, rows = total_z // slabs, total_y // subs
    fold = total_y // rows
    tile = 8

    def along_y(k, values):
        high, low = basis_y[2 * k], basis_y[2 * k + 1]
        four = jnp.concatenate(
            [jnp.concatenate([high, low], axis=1), jnp.concatenate([high, jnp.zeros_like(low)], axis=1)], axis=0
        )
        sums = jnp.dot(jnp.concatenate(split(values), axis=1), four, preferred_element_type=jnp.float32)
        return sums[:, :total_y] + sums[:, total_y:]

    def along_z(k, values):
        high, low = basis_z[2 * k], basis_z[2 * k + 1]
        parts = split(values)
        return jnp.dot(
            jnp.concatenate([high, high, low], axis=1),
            jnp.concatenate([parts[0], parts[1], parts[0]], axis=0),
            preferred_element_type=jnp.float32,
        )

    for s in range(slabs):
        own = []
        for f in range(0, planes // fold):
            lanes = slice(f * total_y, (f + 1) * total_y)
            own += swap_blocks([spectra[s * subs + q][:, lanes] for q in range(subs)])
        for low, high, table in ((0, shifted, 2), (shifted, used, 0)):
            if low < high:
                some = along_y(table, jnp.concatenate([o[low:high] for o in own], axis=0))
                cells[s * planes : (s + 1) * planes, low:high] = some.reshape(planes, high - low, total_y)
    index = lax.broadcasted_iota(jnp.int32, (total_z * tile, 1), 0)
    z_sq = wave_sq(index // tile, total_z)
    y_sq = wave_sq(lax.broadcasted_iota(jnp.int32, (1, total_y), 1), total_y)
    own, scale = [], []
    for start in range(0, used, tile):
        own.append(cells[:, start : start + tile, :].reshape(total_z * tile, total_y))
        x_sq = wave_sq(first + offsets[start // tile] + lax.rem(index, tile), x_length)
        scale.append((z_sq + y_sq) * (256.0 / (x_sq * 256.0 + 1.0)) + 1.0)
    own = along_z(0, jnp.concatenate(own, axis=1))
    own = along_z(1, own / jnp.concatenate(scale, axis=1))
    for k, start in enumerate(range(0, used, tile)):
        part = own[:, k * total_y : (k + 1) * total_y]
        cells[:, start : start + tile, :] = part.reshape(total_z, tile, total_y)
    for s in range(slabs):
        own = along_y(1, cells[s * planes : (s + 1) * planes].reshape(planes * used, total_y))
        for f in range(0, planes // fold):
            blocks = swap_blocks([own[z * used : (z + 1) * used] for z in range(f * fold, (f + 1) * fold)])
            for q in range(subs):
                out[s * subs + q, :, f * total_y : (f + 1) * total_y] = blocks[q]


def solve_yx_kernel(subs, x_length, place, spectra, basis_z, basis_y, out, cells):
    devices = out.shape[0]
    part = x_length // devices
    offsets = list(range(0, part, 8)) + list(range(0, out.shape[1] - part, 8))
    solve((place[0] * subs + place[1]) * part, x_length, offsets, part, subs, spectra, basis_z, basis_y, out, cells)


def solve_zx_kernel(slabs, subs, x_length, place, *refs):
    received, refs = refs[:subs], refs[subs:]
    basis_z, basis_y, sends, (spectra, cells) = refs[0], refs[1], refs[2 : 2 + slabs], refs[2 + slabs :]
    part = x_length // (slabs * subs)
    offsets = list(range(0, part, 8)) + list(range(2 * part - received[0].shape[1], part, 8))
    for e in range(subs):
        for d in range(slabs):
            spectra[around(place[0] - d, slabs) * subs + around(place[1] - e, subs)] = received[e][d]
    solve((place[0] * subs + place[1]) * part, x_length, offsets, 0, subs, spectra, basis_z, basis_y, spectra, cells)
    for d in range(slabs):
        for e in range(subs):
            sends[d][e] = spectra[around(place[0] + d, slabs) * subs + around(place[1] + e, subs)]


def moved(spectra, velocity, basis):
    smoothed = times(split(spectra.T), (basis[0], basis[1]), ((1,), (0,)))
    return 0.5 * (velocity - 32.0 * smoothed.reshape(velocity.shape))


def update_z_kernel(slabs, subs, place, basis, velocity, *refs):
    received, (out, kept, gathered) = refs[:subs], refs[subs:]
    part = received[0].shape[1] - kept.shape[1]
    for e in range(subs):
        for d in range(slabs):
            index = around(place[0] - d, slabs) * subs + around(place[1] - e, subs)
            gathered[pl.ds(pl.multiple_of(index * part, part), part), :] = received[e][d, :part]
            kept[index] = received[e][d, part:]
    out[...] = moved(gathered[...], velocity[0], basis)


def update_kernel(spectra, basis, velocity, updated, kept, out, result, done):
    devices, _, area = kept.shape
    part = (spectra.shape[1] + kept.shape[1]) // 2
    leaving = [pltpu.make_async_copy(updated, out.at[0], done.at[0])]
    leaving[0].start()
    for a in range(2):
        if a:
            own = jnp.concatenate([spectra[:, part:, :], kept[...]], axis=1)
        else:
            own = spectra[:, :part, :]
        high, low = split(own.reshape(devices * part, area).T)
        planes, rows, x_length = velocity.shape[1:]
        some = planes // 2
        for k in range(2):
            cells = slice(k * some * rows, (k + 1) * some * rows)
            smoothed = times((high[cells], low[cells]), (basis[0], basis[1]), ((1,), (0,)))
            own_planes = slice(k * some, (k + 1) * some)
            step = velocity[a + 1, own_planes] - 32.0 * smoothed.reshape(some, rows, x_length)
            result[a, own_planes] = 0.5 * step
            there = out.at[a + 1, pl.ds(k * some, some)]
            own_copy = pltpu.make_async_copy(result.at[a, pl.ds(k * some, some)], there, done.at[1 + 2 * a + k])
            own_copy.start()
            leaving.append(own_copy)
    for copy in leaving:
        copy.wait()


def place_kernel(slabs, place, *refs):
    received, warped = refs[:slabs], refs[slabs]
    for step in range(slabs):
        block = pl.ds(pl.multiple_of(around(place[0] - HOPS[step], slabs) * BLOCK, BLOCK), BLOCK)
        warped[:, :, block] = received[step][1:-1]


def local_blocks(velocity, template, moving, stiffness, fetch_plane, tissue):
    planes, rows, x_length = moving.shape
    slabs, subs = lax.axis_size("slab"), lax.axis_size("sub")
    total_z, total_y = planes * slabs, rows * subs
    devices = slabs * subs
    part = x_length // devices
    area = planes * rows
    place = jnp.stack([lax.axis_index("slab"), lax.axis_index("sub")])
    bf16, f16, f32 = jnp.bfloat16, jnp.float16, jnp.float32

    def shape(dims, kind=f32):
        return jax.ShapeDtypeStruct(dims, kind)

    def scatter(sends, axis, hops=(0, 1, 2, 3)):
        count = lax.axis_size(axis)
        return [sends[0]] + [
            lax.ppermute(sends[d], axis, [(i, (i + hops[d]) % count) for i in range(count)]) for d in range(1, count)
        ]

    def exchange(values):
        return lax.all_to_all(values, ("slab", "sub"), split_axis=0, concat_axis=0, tiled=True)

    fetch, marks = fetch_plane.swapaxes(1, 2), tissue.swapaxes(1, 2)
    coefficient = call(coefficient_kernel, shape(moving.shape), stiffness, marks, flops=1 << 30)
    sends = call(
        functools.partial(send_columns_kernel, slabs),
        [shape(((rows + 2) * planes, BLOCK), bf16)] * slabs,
        place,
        moving,
        fetch,
    )
    sends = call(
        functools.partial(pick_kernel, slabs),
        [shape((planes + 2, rows, BLOCK), bf16)] * slabs,
        place,
        *scatter(sends, "slab", HOPS),
        flops=1 << 30,
    )
    received = scatter(sends, "slab", HOPS)
    basis_x = in_two(real_basis(x_length))
    basis_z = np.kron(real_basis(total_z), np.eye(8))
    basis_z = np.concatenate([in_two(basis_z), in_two(basis_z.T)])
    basis_y = real_basis(total_y)
    basis_y = np.concatenate([in_two(b) for b in (basis_y.T, basis_y, np.roll(basis_y.T, -1, 0))])
    cut = part // 2
    with_z, with_y = 2 * part - cut, part + cut
    first, image, weight, chain, kept = call(
        functools.partial(force_zx_kernel, slabs, subs),
        [
            shape((3 * planes, x_length)),
            shape(moving.shape),
            shape(moving.shape),
            shape((slabs, subs, with_z, area)),
            shape((devices, cut, area)),
        ],
        place,
        *received,
        template,
        coefficient,
        basis_x,
        scratch=[pltpu.VMEM((planes + 2, rows, x_length), f32), pltpu.VMEM((2, x_length, area), f32)],
        flops=3 << 30,
    )
    beyond = lax.ppermute(first, "sub", [((i + 1) % subs, i) for i in range(subs)])
    chain = chain.astype(f16)
    chain = scatter([chain[d] for d in range(slabs)], "slab")
    later, *chain = lax.optimization_barrier((place, *chain))
    warped = call(functools.partial(place_kernel, slabs), shape(moving.shape, bf16), later, *received)
    chain = scatter([jnp.stack([r[e] for r in chain]) for e in range(subs)], "sub")
    spectra = call(
        force_y_kernel,
        shape((devices, with_y, area)),
        beyond,
        image,
        weight,
        basis_x,
        kept,
        flops=2 << 30,
    )
    spectra = exchange(spectra.astype(f16))
    chain = call(
        functools.partial(solve_zx_kernel, slabs, subs, x_length),
        [shape((subs, with_z, area))] * slabs,
        place,
        *[r.astype(f32) for r in chain],
        basis_z,
        basis_y,
        scratch=[pltpu.VMEM((devices, with_z, area), f32), pltpu.VMEM((total_z, with_z, total_y), f32)],
        flops=2 << 30,
    )
    chain, spectra, warped = lax.optimization_barrier((chain, spectra, warped))
    chain = scatter([r.astype(f16) for r in chain], "slab")
    chain = scatter([jnp.stack([r[e] for r in chain]) for e in range(subs)], "sub")
    spectra = call(
        functools.partial(solve_yx_kernel, subs, x_length),
        shape((devices, with_y, area)),
        place,
        spectra.astype(f32),
        basis_z,
        basis_y,
        scratch=[pltpu.VMEM((total_z, with_y, total_y), f32)],
        flops=2 << 30,
    )
    spectra = exchange(spectra.astype(f16))
    x_wave = np.arange(x_length)
    x_wave = 2.0 * np.pi / x_length * np.where(x_wave <= x_length // 2, x_wave, x_wave - x_length // 2)
    basis_back = in_two(real_basis(x_length) / (256.0 * x_wave**2 + 1.0)[:, None])
    updated, kept = call(
        functools.partial(update_z_kernel, slabs, subs),
        [shape(moving.shape), shape((devices, part - cut, area))],
        place,
        basis_back,
        velocity,
        *[r.astype(f32) for r in chain],
        scratch=[pltpu.VMEM((x_length, area), f32)],
        flops=1 << 30,
    )
    new_velocity = call(
        update_kernel,
        shape(velocity.shape),
        spectra.astype(f32),
        basis_back,
        velocity,
        updated,
        kept,
        scratch=[pltpu.VMEM((2,) + moving.shape, f32), pltpu.SemaphoreType.DMA((5,))],
        flops=2 << 30,
        stays=1,
    )
    return (new_velocity, warped)


def local(velocity, template, moving, stiffness, fetch_plane, tissue):
    planes, rows, x_length = moving.shape
    slabs, subs = lax.axis_size("slab"), lax.axis_size("sub")
    fits = (
        x_length == slabs * BLOCK
        and planes == 8
        and planes * slabs * 8 == 256
        and rows % 16 == 0
        and rows * subs == BLOCK
        and slabs == subs == len(HOPS)
        and x_length % (32 * slabs * subs) == 0
    )
    run = local_blocks if fits else local_general
    return run(velocity, template, moving, stiffness, fetch_plane, tissue)


def solution(mesh):
    placed = (
        P(None, ("groups", "slab"), "sub", None),
        P(("groups", "slab"), "sub", None),
        P(("groups", "slab"), "sub", None),
        P(("groups", "slab"), "sub", None),
        P(("groups", "slab"), "sub", None),
        P(("groups", "slab"), "sub", None),
    )
    return jax.shard_map(
        local,
        mesh=mesh,
        in_specs=placed,
        out_specs=(P(None, ("groups", "slab"), "sub", None), P(("groups", "slab"), "sub", None)),
        check_vma=False,
    )
```
